32 devices in a mesh: dp: 16 (over z, y, core), seq: 2 (over x).
Axes of the slice: x: 2, y: 2, z: 4, core: 2. Of those that a mesh axis runs over, the one named last changes fastest.
Arguments:
- tokens: bfloat16 [16, 256, 8192], P('dp', None, 'seq'), may hold values from -6 to 6
- queries: bfloat16 [16, 256, 1024], P('dp', 'seq'), may hold values from -96 to 96
- grad_out: bfloat16 [16, 256, 1024], P('dp', 'seq'), may hold values from -6 to 6
- w_kv: bfloat16 [8192, 256], P('seq'), may hold values from -0.0625 to 0.0625
- doc_ids: int32 [16, 256], P('dp'), may hold values from 0 to 5, never falling along the last dimension, each value on 1 to 85 neighbouring positions
- span_order: int32 [2], replicated, may hold values from 0 to 1, each once
Outputs:
- attention: bfloat16 [16, 256, 1024], P('dp', 'seq')
- query_grad: bfloat16 [16, 256, 1024], P('dp', 'seq')
- weight_grad: bfloat16 [8192, 256], P('seq')
The draws below stay inside these ranges and needn't reach their ends.
Inputs may be any that keep to these rules, and one draw needn't show every extreme that they name: `doc_ids`: document ids never fall along positions; every id is used; a document holds at most 85 positions. `span_order`: each block index appears once.
All inputs are finite; a program needn't handle non-finite values.
Results may differ from the reference program's by a relative error of at most 0.007.
The reference program's roundings to bfloat16 on the way (of `key_value`, `probs_low`, `grad_scores` and `grad_kv`) count: a program that leaves them out, or rounds other values in their place, can miss the bound.
Values may be sent and summed in bfloat16 or wider, within the bound.
No kernel may reach another device: no remote copies, remote signals or barrier semaphores. Data moves between devices by JAX's collectives and lax.ppermute only.
A program may use at most 64 MiB of HBM per device.

```python
import math
import jax
import jax.numpy as jnp
import numpy as np
from jax import lax

D = 8192
HEAD = 128
QH = 8
TOK_DEV = 128
DOCS = 6
SEQ = 256
MOST = 85
PACKS = 16
SPANS = 2


def draw_queries(key, part):
    key = jax.random.fold_in(key, 7)
    first_key = jax.random.fold_in(key, 0)
    base = jnp.clip(jax.random.normal(first_key, (PACKS, SEQ, QH * HEAD), jnp.float32), -6.0, 6.0)
    return base.astype(jnp.bfloat16)


def block_scale(stream_key, shape, shards, least, top_value):
    def one(position, shards_of):
        heights = jax.random.uniform(jax.random.fold_in(jax.random.fold_in(stream_key, 6), position), (shards_of,), jnp.float32, least / len(shards), top_value / len(shards))
        return jnp.repeat(jnp.exp(heights), shape[position] // shards_of).reshape((-1,) + (1,) * (len(shape) - position - 1))

    factor_of = one(*shards[0])
    for cut in shards[1:]:
        factor_of = factor_of * one(*cut)
    return factor_of


def length_profile(number_of, total, bound, lean):
    loads = [(1 << 20) // math.isqrt(rank ** lean) + 1 for rank in range(2, number_of + 1)]
    surplus, counts = total - bound - (number_of - 1), [1] * (number_of - 1)
    while surplus > 0:
        candidates = [i for i in range(number_of - 1) if counts[i] < bound]
        mass, remaining = sum([loads[i] for i in candidates]), surplus
        for i in candidates:
            more = min(bound - counts[i], max(1, remaining * loads[i] // mass), surplus)
            counts[i] = counts[i] + more
            surplus = surplus - more
    return np.array([bound] + counts)


def uneven(key, count, total, most, skew):
    if count == 2:
        one = jax.random.randint(key, (), max(1, total - most), min(most, total - 1) + 1)
        return jnp.stack([one, total - one])
    tallies = jnp.asarray(length_profile(count, total, most, skew), jnp.int32)
    couples = (count - 1) // 2
    donor, receiver = tallies[1:1 + 2 * couples:2], tallies[2:2 + 2 * couples:2]
    slack = jnp.minimum(donor - 1, most - receiver)
    passed = jax.random.randint(jax.random.fold_in(key, 1), (couples,), 0, 1 << 20) % (slack + 1)
    tallies = tallies.at[1:1 + 2 * couples:2].set(donor - passed).at[2:2 + 2 * couples:2].set(receiver + passed)
    return tallies[jax.random.permutation(jax.random.fold_in(key, 2), count)]


def bell_draw(stream_key, extent, scale, most, cuts=(), held_as=jnp.bfloat16):
    result = scale * jax.random.normal(stream_key, extent, jnp.float32)
    if cuts:
        result = result * block_scale(stream_key, extent, cuts, -0.22, 0.18)
    return jnp.clip(result, -most, most).astype(held_as)


def setup_inputs(seed: int = 0) -> dict:
    keys = jax.random.split(jax.random.key(seed), 7)
    return {
        "tokens": bell_draw(keys[0], (PACKS, SEQ, D), 1.0, 6.0, ((0, 16), (2, 2))),
        "queries": draw_queries(jax.random.fold_in(keys[6], 71), 0),
        "grad_out": bell_draw(keys[2], (PACKS, SEQ, QH * HEAD), 1.0, 6.0, ((0, 16), (1, 2))),
        "w_kv": bell_draw(keys[3], (D, 2 * HEAD), D ** -0.5, 0.0625, ((0, 2),)),
        "doc_ids": jax.vmap(lambda own: jnp.searchsorted(jnp.cumsum(uneven(own, DOCS, SEQ, MOST, 1)), jnp.arange(SEQ), side="right"))(jax.random.split(keys[4], PACKS)).reshape((PACKS, SEQ)).astype(jnp.int32),
        "span_order": jax.random.permutation(keys[5], SPANS).astype(jnp.int32),
    }


def reference(tokens, queries, grad_out, w_kv, doc_ids, span_order):
    row_ids = jnp.arange(SEQ, dtype=jnp.int32)
    positions = (span_order[row_ids // TOK_DEV] * TOK_DEV + row_ids % TOK_DEV).astype(jnp.int32)
    causal = positions[None, :] <= positions[:, None]
    score_scale = 1.0 / math.sqrt(HEAD)
    highest = lax.Precision.HIGHEST

    def one_pack(running, inputs):
        pack_tokens, pack_queries, pack_grads, pack_docs = inputs
        key_value = jnp.dot(pack_tokens, w_kv, preferred_element_type=jnp.float32).astype(jnp.bfloat16)
        key_part = key_value[:, :HEAD].astype(jnp.float32)
        value_part = key_value[:, HEAD:].astype(jnp.float32)
        doc_rows = pack_docs[positions]
        allowed = causal & (doc_rows[None, :] == doc_rows[:, None])
        query_heads = pack_queries.reshape(SEQ, QH, HEAD).astype(jnp.float32)
        grad_heads = pack_grads.reshape(SEQ, QH, HEAD).astype(jnp.float32)
        scores = jnp.einsum('qhe,ke->hqk', query_heads, key_part, precision=highest) * score_scale
        scores = jnp.where(allowed[None], scores, jnp.float32(-1e+30))
        top_score = lax.optimization_barrier(jnp.max(scores, axis=-1, keepdims=True))
        expo = jnp.exp(scores - top_score)
        attn_probs = expo / lax.optimization_barrier(jnp.sum(expo, axis=-1, keepdims=True))
        probs_low = lax.optimization_barrier(attn_probs.astype(jnp.bfloat16)).astype(jnp.float32)
        attended = jnp.einsum('hqk,ke->qhe', probs_low, value_part, precision=highest)
        attention = attended.astype(jnp.bfloat16).reshape(SEQ, QH * HEAD)
        grad_probs = jnp.einsum('qhe,ke->hqk', grad_heads, value_part, precision=highest)
        row_delta = lax.optimization_barrier(jnp.sum(attn_probs * grad_probs, axis=-1, keepdims=True))
        grad_scores = attn_probs * (grad_probs - row_delta) * score_scale
        grad_scores = lax.optimization_barrier(grad_scores.astype(jnp.bfloat16)).astype(jnp.float32)
        query_grad = jnp.einsum('hqk,ke->qhe', grad_scores, key_part, precision=highest)
        query_grad = query_grad.astype(jnp.bfloat16).reshape(SEQ, QH * HEAD)
        key_grad = jnp.einsum('hqk,qhe->ke', grad_scores, query_heads, precision=highest)
        value_grad = jnp.einsum('hqk,qhe->ke', probs_low, grad_heads, precision=highest)
        grad_kv = jnp.concatenate([key_grad, value_grad], axis=1).astype(jnp.bfloat16)
        weight_part = jnp.dot(pack_tokens.T, grad_kv, preferred_element_type=jnp.float32)
        return (running + weight_part, (attention, query_grad))
    start = jnp.zeros((D, 2 * HEAD), jnp.float32)
    weight_total, outputs = lax.scan(one_pack, start, (tokens, queries, grad_out, doc_ids))
    attention, query_grad = outputs
    weight_grad = (weight_total / PACKS).astype(jnp.bfloat16)
    return (attention, query_grad, weight_grad)
```

```python
import functools
import math

import jax
import jax.numpy as jnp
from jax import lax
from jax.experimental import pallas as pl
from jax.experimental.pallas import tpu as pltpu
from jax.sharding import PartitionSpec as P

HEAD = 128
QH = 8
GROUP = 2
F32 = jnp.float32
BF16 = jnp.bfloat16
NT = (((1,), (1,)), ((), ()))
TN = (((0,), (0,)), ((), ()))
NN = (((1,), (0,)), ((), ()))


def _mm(a, b, dims):
    return lax.dot_general(a, b, dims, preferred_element_type=F32)


def attention_kernel(parts, own, order_ref, docs_ref, q_ref, g_ref, *refs):
    kv_refs = refs[:parts]
    att_ref, qg_ref, kvg_ref = refs[parts:]
    rows = q_ref.shape[0]
    seq_len = kv_refs[0].shape[0]
    spans = seq_len // rows
    if parts == 1:
        kv = kv_refs[0][...]
    else:
        kv = (kv_refs[0][...] + kv_refs[1][...]).astype(BF16)
    keys = kv[:, :HEAD]
    values = kv[:, HEAD:]
    keys_t = keys.T
    values_t = values.T
    scale = 1.0 / math.sqrt(HEAD)
    me = lax.axis_index(own)

    def row_docs(span):
        return docs_ref[pl.ds(order_ref[span], 1), :]

    masks = []
    q_docs = row_docs(me)
    q_span = order_ref[me]
    q_pos = lax.broadcasted_iota(jnp.int32, (rows, rows), 1)
    k_pos = lax.broadcasted_iota(jnp.int32, (rows, rows), 0)
    for span in range(spans):
        k_docs = jnp.broadcast_to(row_docs(span), (rows, rows)).T
        gap = (order_ref[span] - q_span) * rows
        masks.append((k_pos + gap <= q_pos) & (k_docs == q_docs))
    allowed = jnp.concatenate(masks, axis=0)
    allowed = jnp.concatenate([allowed] * GROUP, axis=1)

    key_grad = jnp.zeros((seq_len, HEAD), F32)
    value_grad = jnp.zeros((seq_len, HEAD), F32)
    for first in range(0, QH, GROUP):
        heads = range(first, first + GROUP)
        q = jnp.concatenate([q_ref[:, h * HEAD : (h + 1) * HEAD] for h in heads], axis=0)
        g = jnp.concatenate([g_ref[:, h * HEAD : (h + 1) * HEAD] for h in heads], axis=0)
        scores = jnp.where(allowed, _mm(keys, q, NT) * scale, F32(-1e30))
        expo = jnp.exp(scores - jnp.max(scores, axis=0, keepdims=True))
        probs = expo * (1.0 / jnp.sum(expo, axis=0, keepdims=True))
        low = probs.astype(BF16)
        grad_probs = _mm(values, g, NT)
        delta = jnp.sum(probs * grad_probs, axis=0, keepdims=True)
        grad_scores = (probs * (grad_probs - delta) * scale).astype(BF16)
        att = _mm(values_t, low, NN)
        qg = _mm(keys_t, grad_scores, NN)
        for i, h in enumerate(heads):
            cols = slice(h * HEAD, (h + 1) * HEAD)
            att_ref[:, cols] = att[:, i * rows : (i + 1) * rows].T.astype(BF16)
            qg_ref[:, cols] = qg[:, i * rows : (i + 1) * rows].T.astype(BF16)
        key_grad += _mm(grad_scores, q, NN)
        value_grad += _mm(low, g, NN)
    kvg_ref[:, :HEAD] = key_grad
    kvg_ref[:, HEAD:] = value_grad


def attend(order, docs, q, g, kvs):
    vmem = pl.BlockSpec(memory_space=pltpu.VMEM)
    return pl.pallas_call(
        functools.partial(attention_kernel, len(kvs), "seq"),
        out_shape=(
            jax.ShapeDtypeStruct(q.shape, BF16),
            jax.ShapeDtypeStruct(q.shape, BF16),
            jax.ShapeDtypeStruct((kvs[0].shape[0], 2 * HEAD), F32),
        ),
        in_specs=[pl.BlockSpec(memory_space=pltpu.SMEM)] + [vmem] * (3 + len(kvs)),
        out_specs=(vmem, vmem, vmem),
        compiler_params=pltpu.CompilerParams(vmem_limit_bytes=48 * 1024 * 1024),
        name="attention_fwd_bwd",
    )(order, docs, q, g, *kvs)


def per_device(tokens, queries, grad_out, w_kv, doc_ids, span_order):
    seq_size = lax.axis_size("seq")
    dp_size = lax.axis_size("dp")
    rows_dev = queries.shape[1]
    flat = tokens[0]
    spread = lax.all_to_all(flat, "dp", split_axis=1, concat_axis=0, tiled=True)
    partial = jnp.dot(flat, w_kv, preferred_element_type=F32)
    swap = [(i, i ^ 1) for i in range(2)]
    if seq_size == 2:
        kvs = [partial, lax.ppermute(partial, "seq", swap)]
    else:
        own = lax.psum_scatter(partial, "seq", scatter_dimension=0, tiled=True).astype(BF16)
        kvs = [lax.all_gather(own, "seq", axis=0, tiled=True)]
    docs = doc_ids.reshape(-1, rows_dev)
    attention, query_grad, terms = attend(span_order, docs, queries[0], grad_out[0], kvs)
    if seq_size == 2:
        grad_kv = (terms + lax.ppermute(terms, "seq", swap)).astype(BF16)
    else:
        grad_kv = lax.psum(terms, "seq").astype(BF16)
    all_grads = lax.all_gather(grad_kv, "dp", axis=0, tiled=True)
    piece = _mm(spread, all_grads, TN)
    piece = (piece * (1.0 / dp_size)).astype(BF16)
    weight_grad = lax.all_gather(piece, "dp", axis=0, tiled=True)
    return (attention[None], query_grad[None], weight_grad)


def solution(mesh):
    return jax.shard_map(
        per_device,
        mesh=mesh,
        in_specs=(
            P("dp", None, "seq"),
            P("dp", "seq", None),
            P("dp", "seq", None),
            P("seq", None),
            P("dp", None),
            P(),
        ),
        out_specs=(P("dp", "seq", None), P("dp", "seq", None), P("seq", None)),
        check_vma=False,
    )
```

```python
import functools
import math

import jax
import jax.numpy as jnp
from jax import lax
from jax.experimental import pallas as pl
from jax.experimental.pallas import tpu as pltpu
from jax.sharding import PartitionSpec as P

HEAD = 128
QH = 8
GROUP = 2
F32 = jnp.float32
BF16 = jnp.bfloat16
NT = (((1,), (1,)), ((), ()))
TN = (((0,), (0,)), ((), ()))
NN = (((1,), (0,)), ((), ()))


def _mm(a, b, dims):
    return lax.dot_general(a, b, dims, preferred_element_type=F32)


def attention_kernel(parts, own, order_ref, docs_ref, q_ref, g_ref, *refs):
    kv_refs = refs[:parts]
    att_ref, qg_ref, kvg_ref = refs[parts:]
    rows = q_ref.shape[0]
    seq_len = kv_refs[0].shape[0]
    spans = seq_len // rows
    if parts == 1:
        kv = kv_refs[0][...]
    else:
        kv = (kv_refs[0][...] + kv_refs[1][...]).astype(BF16)
    keys = kv[:, :HEAD]
    values = kv[:, HEAD:]
    keys_t = keys.T
    values_t = values.T
    scale = 1.0 / math.sqrt(HEAD)
    me = lax.axis_index(own)

    def row_docs(span):
        return docs_ref[pl.ds(order_ref[span], 1), :]

    masks = []
    q_docs = row_docs(me)
    q_span = order_ref[me]
    q_pos = lax.broadcasted_iota(jnp.int32, (rows, rows), 1)
    k_pos = lax.broadcasted_iota(jnp.int32, (rows, rows), 0)
    for span in range(spans):
        k_docs = jnp.broadcast_to(row_docs(span), (rows, rows)).T
        gap = (order_ref[span] - q_span) * rows
        masks.append((k_pos + gap <= q_pos) & (k_docs == q_docs))
    allowed = jnp.concatenate(masks, axis=0)
    allowed = jnp.concatenate([allowed] * GROUP, axis=1)

    key_grad = jnp.zeros((seq_len, HEAD), F32)
    value_grad = jnp.zeros((seq_len, HEAD), F32)
    for first in range(0, QH, GROUP):
        heads = range(first, first + GROUP)
        q = jnp.concatenate([q_ref[:, h * HEAD : (h + 1) * HEAD] for h in heads], axis=0)
        g = jnp.concatenate([g_ref[:, h * HEAD : (h + 1) * HEAD] for h in heads], axis=0)
        scores = jnp.where(allowed, _mm(keys, q, NT) * scale, F32(-1e30))
        expo = jnp.exp(scores - jnp.max(scores, axis=0, keepdims=True))
        probs = expo * (1.0 / jnp.sum(expo, axis=0, keepdims=True))
        low = probs.astype(BF16)
        grad_probs = _mm(values, g, NT)
        delta = jnp.sum(probs * grad_probs, axis=0, keepdims=True)
        grad_scores = (probs * (grad_probs - delta) * scale).astype(BF16)
        att = _mm(values_t, low, NN)
        qg = _mm(keys_t, grad_scores, NN)
        for i, h in enumerate(heads):
            cols = slice(h * HEAD, (h + 1) * HEAD)
            att_ref[:, cols] = att[:, i * rows : (i + 1) * rows].T.astype(BF16)
            qg_ref[:, cols] = qg[:, i * rows : (i + 1) * rows].T.astype(BF16)
        key_grad += _mm(grad_scores, q, NN)
        value_grad += _mm(low, g, NN)
    kvg_ref[:HEAD, :] = key_grad.T
    kvg_ref[HEAD:, :] = value_grad.T


def attend(order, docs, q, g, kvs):
    vmem = pl.BlockSpec(memory_space=pltpu.VMEM)
    return pl.pallas_call(
        functools.partial(attention_kernel, len(kvs), "seq"),
        out_shape=(
            jax.ShapeDtypeStruct(q.shape, BF16),
            jax.ShapeDtypeStruct(q.shape, BF16),
            jax.ShapeDtypeStruct((2 * HEAD, kvs[0].shape[0]), F32),
        ),
        in_specs=[pl.BlockSpec(memory_space=pltpu.SMEM)] + [vmem] * (3 + len(kvs)),
        out_specs=(vmem, vmem, vmem),
        compiler_params=pltpu.CompilerParams(vmem_limit_bytes=48 * 1024 * 1024),
        name="attention_fwd_bwd",
    )(order, docs, q, g, *kvs)


ANY = pl.BlockSpec(memory_space=pl.ANY)
VMEM = pl.BlockSpec(memory_space=pltpu.VMEM)
LIMIT = pltpu.CompilerParams(vmem_limit_bytes=48 * 1024 * 1024)
CORE, Y, Z1, Z2 = 1, 2, 4, 8
NEAR = 8


def project_kernel(tok_ref, w_ref, out_ref, *refs):
    slices, (tok_v, w_v, in_sems, w_sems, out_sems) = refs[:NEAR], refs[NEAR:]
    width = slices[0].shape[1]
    mine = lax.rem(lax.axis_index("dp"), NEAR)
    reads = []
    for k in range(NEAR):
        first = pl.multiple_of((mine ^ k) * width, width)
        tok = pltpu.make_async_copy(tok_ref.at[:, pl.ds(first, width)], tok_v.at[k], in_sems.at[k])
        w = pltpu.make_async_copy(w_ref.at[pl.ds(first, width), :], w_v.at[k], w_sems.at[k])
        tok.start()
        w.start()
        reads.append((tok, w))
    writes = []
    total = None
    for k in range(NEAR):
        tok, w = reads[k]
        tok.wait()
        write = pltpu.make_async_copy(tok_v.at[k], slices[k], out_sems.at[k])
        write.start()
        writes.append(write)
        w.wait()
        term = _mm(tok_v[k], w_v[k], NN)
        total = term if total is None else total + term
    out_ref[...] = total
    for write in writes:
        write.wait()


def project(tokens, w_kv):
    rows, features = tokens.shape
    width = features // NEAR
    return pl.pallas_call(
        project_kernel,
        out_shape=[jax.ShapeDtypeStruct((rows, 2 * HEAD), F32)]
        + [jax.ShapeDtypeStruct((rows, width), BF16)] * NEAR,
        in_specs=[ANY, ANY],
        out_specs=[VMEM] + [ANY] * NEAR,
        scratch_shapes=[
            pltpu.VMEM((NEAR, rows, width), BF16),
            pltpu.VMEM((NEAR, width, 2 * HEAD), BF16),
            pltpu.SemaphoreType.DMA((NEAR,)),
            pltpu.SemaphoreType.DMA((NEAR,)),
            pltpu.SemaphoreType.DMA((NEAR,)),
        ],
        compiler_params=LIMIT,
        name="project_and_slice",
    )(tokens, w_kv)


def weight_kernel(packs, *refs):
    toks, grads = refs[:NEAR], refs[NEAR : 2 * NEAR]
    keep_ref, send_ref, total = refs[2 * NEAR :]
    half = keep_ref.shape[1]
    acc = _mm(grads[0][...], toks[0][...], NN)
    for k in range(1, NEAR):
        acc += _mm(grads[k][...], toks[k][...], NN)
    total[...] = acc * (1.0 / packs)
    high = lax.axis_index("dp") // NEAR
    keep_ref[...] = total[:, pl.ds(pl.multiple_of(high * half, half), half)]
    send_ref[...] = total[:, pl.ds(pl.multiple_of((1 - high) * half, half), half)]


def weight_part(toks, grads, packs):
    width = toks[0].shape[1]
    cols = grads[0].shape[0]
    half = jax.ShapeDtypeStruct((cols, width // 2), F32)
    return pl.pallas_call(
        functools.partial(weight_kernel, packs),
        out_shape=[half, half],
        in_specs=[VMEM] * (2 * NEAR),
        out_specs=[VMEM, VMEM],
        scratch_shapes=[pltpu.VMEM((cols, width), F32)],
        compiler_params=LIMIT,
        name="weight_part",
    )(*toks, *grads)


def finish_kernel(a_ref, b_ref, out_ref):
    out_ref[...] = (a_ref[...] + b_ref[...]).T.astype(BF16)


def finish(a, b):
    return pl.pallas_call(
        finish_kernel,
        out_shape=jax.ShapeDtypeStruct((a.shape[1], a.shape[0]), BF16),
        in_specs=[VMEM, VMEM],
        out_specs=VMEM,
        compiler_params=LIMIT,
        name="weight_finish",
    )(a, b)


def assemble_kernel(count, *refs):
    shards, out_ref, sems = refs[:count], refs[count], refs[count + 1]
    rows = shards[0].shape[0]
    me = lax.axis_index("dp")
    copies = []
    for k in range(count):
        source = me ^ k
        place = lax.rem(source, NEAR) * (count // NEAR) + source // NEAR
        first = pl.multiple_of(place * rows, rows)
        copy = pltpu.make_async_copy(shards[k], out_ref.at[pl.ds(first, rows), :], sems.at[k])
        copy.start()
        copies.append(copy)
    for copy in copies:
        copy.wait()


def assemble(shards):
    count = len(shards)
    rows, cols = shards[0].shape
    return pl.pallas_call(
        functools.partial(assemble_kernel, count),
        out_shape=jax.ShapeDtypeStruct((count * rows, cols), BF16),
        in_specs=[ANY] * count,
        out_specs=ANY,
        scratch_shapes=[pltpu.SemaphoreType.DMA((count,))],
        compiler_params=LIMIT,
        name="weight_assemble",
    )(*shards)


def hop(value, bits):
    count = lax.axis_size("dp")
    return lax.ppermute(value, "dp", [(i, i ^ bits) for i in range(count)])


def per_device_16x2(tokens, queries, grad_out, w_kv, doc_ids, span_order):
    dp_size = lax.axis_size("dp")
    rows_dev = queries.shape[1]
    swap = [(0, 1), (1, 0)]
    partial, *own = project(tokens[0], w_kv)
    other = lax.ppermute(partial, "seq", swap)
    toks = [own[0]] + [hop(own[k], k) for k in range(1, NEAR)]
    docs = doc_ids.reshape(-1, rows_dev)
    attention, query_grad, terms = attend(
        span_order, docs, queries[0], grad_out[0], [partial, other]
    )
    grad = (terms + lax.ppermute(terms, "seq", swap)).astype(BF16)
    grads = {0: grad}
    for bits in (Y, Z1, Y | Z1, CORE):
        grads[bits] = hop(grad, bits)
    for bits in (Y, Z1, Y | Z1):
        grads[bits | CORE] = hop(grads[bits], CORE)
    keep, send = weight_part(toks, [grads[k] for k in range(NEAR)], dp_size)
    have = {0: finish(keep, hop(send, Z2))}
    for bits in (Z1, Y, Z2, CORE):
        have[bits] = hop(have[0], bits)
    have[Z1 | Y] = hop(have[Z1], Y)
    have[Z2 | Z1] = hop(have[Z2], Z1)
    have[Z2 | Y] = hop(have[Z2], Y)
    have[Z2 | Z1 | Y] = hop(have[Z2 | Z1], Y)
    for bits in (Y, Z1, Z2, Z1 | Y, Z2 | Y, Z2 | Z1, Z2 | Z1 | Y):
        have[bits | CORE] = hop(have[bits], CORE)
    weight_grad = assemble([have[k] for k in range(dp_size)])
    return (attention[None], query_grad[None], weight_grad)


def per_device(tokens, queries, grad_out, w_kv, doc_ids, span_order):
    dp_size = lax.axis_size("dp")
    rows_dev = queries.shape[1]
    flat = tokens[0]
    spread = lax.all_to_all(flat, "dp", split_axis=1, concat_axis=0, tiled=True)
    partial = jnp.dot(flat, w_kv, preferred_element_type=F32)
    own = lax.psum_scatter(partial, "seq", scatter_dimension=0, tiled=True).astype(BF16)
    kvs = [lax.all_gather(own, "seq", axis=0, tiled=True)]
    docs = doc_ids.reshape(-1, rows_dev)
    attention, query_grad, terms = attend(span_order, docs, queries[0], grad_out[0], kvs)
    grad_kv = lax.psum(terms.T, "seq").astype(BF16)
    all_grads = lax.all_gather(grad_kv, "dp", axis=0, tiled=True)
    piece = (_mm(spread, all_grads, TN) * (1.0 / dp_size)).astype(BF16)
    weight_grad = lax.all_gather(piece, "dp", axis=0, tiled=True)
    return (attention[None], query_grad[None], weight_grad)


def solution(mesh):
    small = mesh.shape["dp"] == 16 and mesh.shape["seq"] == 2
    return jax.shard_map(
        per_device_16x2 if small else per_device,
        mesh=mesh,
        in_specs=(
            P("dp", None, "seq"),
            P("dp", "seq", None),
            P("dp", "seq", None),
            P("seq", None),
            P("dp", None),
            P(),
        ),
        out_specs=(P("dp", "seq", None), P("dp", "seq", None), P("seq", None)),
        check_vma=False,
    )
```

```python
import functools
import math

import jax
import jax.numpy as jnp
from jax import lax
from jax.experimental import pallas as pl
from jax.experimental.pallas import tpu as pltpu
from jax.sharding import PartitionSpec as P

HEAD = 128
QH = 8
GROUP = 2
F32 = jnp.float32
BF16 = jnp.bfloat16
NT = (((1,), (1,)), ((), ()))
TN = (((0,), (0,)), ((), ()))
NN = (((1,), (0,)), ((), ()))


def _mm(a, b, dims):
    return lax.dot_general(a, b, dims, preferred_element_type=F32)


def attention_kernel(parts, own, order_ref, docs_ref, q_ref, g_ref, *refs):
    kv_refs = refs[:parts]
    att_ref, qg_ref, kvg_ref = refs[parts:]
    rows = q_ref.shape[0]
    seq_len = kv_refs[0].shape[0]
    spans = seq_len // rows
    if parts == 1:
        kv = kv_refs[0][...]
    else:
        kv = (kv_refs[0][...] + kv_refs[1][...]).astype(BF16)
    keys = kv[:, :HEAD]
    values = kv[:, HEAD:]
    keys_t = keys.T
    values_t = values.T
    scale = 1.0 / math.sqrt(HEAD)
    me = lax.axis_index(own)

    def row_docs(span):
        return docs_ref[pl.ds(order_ref[span], 1), :]

    masks = []
    q_docs = row_docs(me)
    q_span = order_ref[me]
    q_pos = lax.broadcasted_iota(jnp.int32, (rows, rows), 1)
    k_pos = lax.broadcasted_iota(jnp.int32, (rows, rows), 0)
    for span in range(spans):
        k_docs = jnp.broadcast_to(row_docs(span), (rows, rows)).T
        gap = (order_ref[span] - q_span) * rows
        masks.append((k_pos + gap <= q_pos) & (k_docs == q_docs))
    allowed = jnp.concatenate(masks, axis=0)
    allowed = jnp.concatenate([allowed] * GROUP, axis=1)

    key_grad = jnp.zeros((seq_len, HEAD), F32)
    value_grad = jnp.zeros((seq_len, HEAD), F32)
    for first in range(0, QH, GROUP):
        heads = range(first, first + GROUP)
        q = jnp.concatenate([q_ref[:, h * HEAD : (h + 1) * HEAD] for h in heads], axis=0)
        g = jnp.concatenate([g_ref[:, h * HEAD : (h + 1) * HEAD] for h in heads], axis=0)
        scores = jnp.where(allowed, _mm(keys, q, NT) * scale, F32(-1e30))
        expo = jnp.exp(scores - jnp.max(scores, axis=0, keepdims=True))
        probs = expo * (1.0 / jnp.sum(expo, axis=0, keepdims=True))
        low = probs.astype(BF16)
        grad_probs = _mm(values, g, NT)
        delta = jnp.sum(probs * grad_probs, axis=0, keepdims=True)
        grad_scores = (probs * (grad_probs - delta) * scale).astype(BF16)
        att = _mm(values_t, low, NN)
        qg = _mm(keys_t, grad_scores, NN)
        for i, h in enumerate(heads):
            cols = slice(h * HEAD, (h + 1) * HEAD)
            att_ref[:, cols] = att[:, i * rows : (i + 1) * rows].T.astype(BF16)
            qg_ref[:, cols] = qg[:, i * rows : (i + 1) * rows].T.astype(BF16)
        key_grad += _mm(grad_scores, q, NN)
        value_grad += _mm(low, g, NN)
    kvg_ref[:HEAD, :] = key_grad.T
    kvg_ref[HEAD:, :] = value_grad.T


def attend(order, docs, q, g, kvs):
    vmem = pl.BlockSpec(memory_space=pltpu.VMEM)
    return pl.pallas_call(
        functools.partial(attention_kernel, len(kvs), "seq"),
        out_shape=(
            jax.ShapeDtypeStruct(q.shape, BF16),
            jax.ShapeDtypeStruct(q.shape, BF16),
            jax.ShapeDtypeStruct((2 * HEAD, kvs[0].shape[0]), F32),
        ),
        in_specs=[pl.BlockSpec(memory_space=pltpu.SMEM)] + [vmem] * (3 + len(kvs)),
        out_specs=(vmem, vmem, vmem),
        compiler_params=pltpu.CompilerParams(vmem_limit_bytes=48 * 1024 * 1024),
        name="attention_fwd_bwd",
    )(order, docs, q, g, *kvs)


ANY = pl.BlockSpec(memory_space=pl.ANY)
VMEM = pl.BlockSpec(memory_space=pltpu.VMEM)
LIMIT = pltpu.CompilerParams(vmem_limit_bytes=48 * 1024 * 1024)
CORE, Y, Z1, Z2 = 1, 2, 4, 8
CORES = 2
BLOCK = 4


def block_of(device):
    return lax.rem(device // CORES, BLOCK)


def slice_kernel(tok_ref, *refs):
    slices, sems = refs[:BLOCK], refs[BLOCK]
    width = slices[0].shape[1]
    mine = block_of(lax.axis_index("dp"))
    copies = []
    for k in (1, 2, 3, 0):
        first = pl.multiple_of((mine ^ k) * width, width)
        copy = pltpu.make_async_copy(tok_ref.at[:, pl.ds(first, width)], slices[k], sems.at[k])
        copy.start()
        copies.append(copy)
    for copy in copies:
        copy.wait()


def slice_tokens(tokens):
    rows, features = tokens.shape
    return pl.pallas_call(
        slice_kernel,
        out_shape=[jax.ShapeDtypeStruct((rows, features // BLOCK), BF16)] * BLOCK,
        in_specs=[pl.BlockSpec(memory_space=pltpu.HBM)],
        out_specs=[VMEM] * BLOCK,
        scratch_shapes=[pltpu.SemaphoreType.DMA((BLOCK,))],
        compiler_params=LIMIT,
        name="slice_tokens",
    )(tokens)


def project_kernel(w_ref, *refs):
    slices, out_ref = refs[:BLOCK], refs[BLOCK]
    width = slices[0].shape[1]
    mine = block_of(lax.axis_index("dp"))
    total = None
    for k in range(BLOCK):
        first = pl.multiple_of((mine ^ k) * width, width)
        term = _mm(slices[k][...], w_ref[pl.ds(first, width), :], NN)
        total = term if total is None else total + term
    out_ref[...] = total


def project(slices, w_kv):
    return pl.pallas_call(
        project_kernel,
        out_shape=jax.ShapeDtypeStruct((slices[0].shape[0], 2 * HEAD), F32),
        in_specs=[VMEM] * (1 + BLOCK),
        out_specs=VMEM,
        compiler_params=LIMIT,
        name="project",
    )(w_kv, *slices)


def round_kernel(a_ref, b_ref, *refs):
    refs[-1][...] = (a_ref[...] + b_ref[...]).astype(BF16)


def round_grad(a, b, arrived):
    return pl.pallas_call(
        round_kernel,
        out_shape=jax.ShapeDtypeStruct(a.shape, BF16),
        in_specs=[VMEM, VMEM] + [ANY] * len(arrived),
        out_specs=VMEM,
        compiler_params=LIMIT,
        name="round_grad",
    )(a, b, *arrived)


def weight_kernel(packs, *refs):
    toks, grads = refs[:BLOCK], refs[BLOCK : 2 * BLOCK]
    keep_ref, send_ref = refs[2 * BLOCK :]
    half = keep_ref.shape[1]
    core = lax.rem(lax.axis_index("dp"), CORES)
    for ref, which in ((send_ref, 1 - core), (keep_ref, core)):
        cols = pl.ds(pl.multiple_of(which * half, half), half)
        acc = _mm(grads[0][...], toks[0][:, cols], NN)
        for k in range(1, BLOCK):
            acc += _mm(grads[k][...], toks[k][:, cols], NN)
        ref[...] = acc * (1.0 / packs)


def weight_part(toks, grads, packs):
    half = jax.ShapeDtypeStruct((grads[0].shape[0], toks[0].shape[1] // CORES), F32)
    return pl.pallas_call(
        functools.partial(weight_kernel, packs),
        out_shape=[half, half],
        in_specs=[VMEM] * (2 * BLOCK),
        out_specs=[VMEM, VMEM],
        compiler_params=LIMIT,
        name="weight_part",
    )(*toks, *grads)


def fold_kernel(a_ref, b_ref, keep_ref, send_ref):
    half = keep_ref.shape[1]
    high = lax.axis_index("dp") // (CORES * BLOCK)
    for ref, which in ((send_ref, 1 - high), (keep_ref, high)):
        cols = pl.ds(pl.multiple_of(which * half, half), half)
        ref[...] = a_ref[:, cols] + b_ref[:, cols]


def fold(a, b):
    half = jax.ShapeDtypeStruct((a.shape[0], a.shape[1] // 2), F32)
    return pl.pallas_call(
        fold_kernel,
        out_shape=[half, half],
        in_specs=[VMEM, VMEM],
        out_specs=[VMEM, VMEM],
        compiler_params=LIMIT,
        name="weight_fold",
    )(a, b)


def finish_kernel(a_ref, b_ref, out_ref):
    out_ref[...] = (a_ref[...] + b_ref[...]).T.astype(BF16)


def finish(a, b):
    return pl.pallas_call(
        finish_kernel,
        out_shape=jax.ShapeDtypeStruct((a.shape[1], a.shape[0]), BF16),
        in_specs=[VMEM, VMEM],
        out_specs=VMEM,
        compiler_params=LIMIT,
        name="weight_finish",
    )(a, b)


def stack_kernel(*refs):
    out_ref = refs[-1]
    first = 0
    for ref in refs[:-1]:
        out_ref[first : first + ref.shape[0], :] = ref[...]
        first += ref.shape[0]


def stack(parts):
    rows = sum(part.shape[0] for part in parts)
    return pl.pallas_call(
        stack_kernel,
        out_shape=jax.ShapeDtypeStruct((rows, parts[0].shape[1]), BF16),
        in_specs=[VMEM] * len(parts),
        out_specs=VMEM,
        compiler_params=LIMIT,
        name="stack",
    )(*parts)


def assemble_kernel(held, rows, *refs):
    arrays, out_ref, sems = refs[: len(held)], refs[len(held)], refs[len(held) + 1]
    me = lax.axis_index("dp")
    copies = []
    for array, bits in zip(arrays, held):
        for n, bit in enumerate(bits):
            source = me ^ bit
            high = source // (CORES * BLOCK)
            place = (block_of(source) * CORES + lax.rem(source, CORES)) * 2 + high
            first = pl.multiple_of(place * rows, rows)
            copy = pltpu.make_async_copy(
                array.at[pl.ds(n * rows, rows), :],
                out_ref.at[pl.ds(first, rows), :],
                sems.at[len(copies)],
            )
            copy.start()
            copies.append(copy)
    for copy in copies:
        copy.wait()


def assemble(pieces):
    arrays = [array for array, _ in pieces]
    held = [bits for _, bits in pieces]
    count = sum(len(bits) for bits in held)
    rows = arrays[0].shape[0] // len(held[0])
    return pl.pallas_call(
        functools.partial(assemble_kernel, held, rows),
        out_shape=jax.ShapeDtypeStruct((count * rows, arrays[0].shape[1]), BF16),
        in_specs=[ANY] * len(arrays),
        out_specs=ANY,
        scratch_shapes=[pltpu.SemaphoreType.DMA((count,))],
        compiler_params=LIMIT,
        name="weight_assemble",
    )(*arrays)


def hop(value, bits):
    count = lax.axis_size("dp")
    return lax.ppermute(value, "dp", [(i, i ^ bits) for i in range(count)])


def per_device_16x2(tokens, queries, grad_out, w_kv, doc_ids, span_order):
    dp_size = lax.axis_size("dp")
    rows_dev = queries.shape[1]
    swap = [(0, 1), (1, 0)]
    near = (Y, Z1, Y | Z1)
    slices = slice_tokens(tokens[0])
    arrived = [hop(slices[k], bits) for k, bits in zip((1, 2, 3), near)]
    partial = project(slices, w_kv)
    other = lax.ppermute(partial, "seq", swap)
    docs = doc_ids.reshape(-1, rows_dev)
    attention, query_grad, terms = attend(
        span_order, docs, queries[0], grad_out[0], [partial, other]
    )
    grad = round_grad(terms, lax.ppermute(terms, "seq", swap), arrived)
    grads = [grad] + [hop(grad, bits) for bits in near]
    keep, send = weight_part([slices[0]] + arrived, grads, dp_size)
    keep, send = fold(keep, hop(send, CORE))
    own = finish(keep, hop(send, Z2))
    z1, z2, y = hop(own, Z1), hop(own, Z2), hop(own, Y)
    z12 = hop(z2, Z1)
    zy = hop(stack([z1, z2]), Y)
    z12y = hop(z12, Y)
    most = hop(stack([own, z1, z2, y, z12, zy]), CORE)
    last = hop(z12y, CORE)
    pieces = [
        (own, [0]),
        (z1, [Z1]),
        (z2, [Z2]),
        (y, [Y]),
        (z12, [Z1 | Z2]),
        (zy, [Z1 | Y, Z2 | Y]),
        (z12y, [Z1 | Z2 | Y]),
    ]
    theirs = [bit | CORE for _, bits in pieces[:-1] for bit in bits]
    pieces += [(most, theirs), (last, [CORE | Y | Z1 | Z2])]
    weight_grad = assemble(pieces)
    return (attention[None], query_grad[None], weight_grad)


def per_device(tokens, queries, grad_out, w_kv, doc_ids, span_order):
    dp_size = lax.axis_size("dp")
    rows_dev = queries.shape[1]
    flat = tokens[0]
    spread = lax.all_to_all(flat, "dp", split_axis=1, concat_axis=0, tiled=True)
    partial = jnp.dot(flat, w_kv, preferred_element_type=F32)
    own = lax.psum_scatter(partial, "seq", scatter_dimension=0, tiled=True).astype(BF16)
    kvs = [lax.all_gather(own, "seq", axis=0, tiled=True)]
    docs = doc_ids.reshape(-1, rows_dev)
    attention, query_grad, terms = attend(span_order, docs, queries[0], grad_out[0], kvs)
    grad_kv = lax.psum(terms.T, "seq").astype(BF16)
    all_grads = lax.all_gather(grad_kv, "dp", axis=0, tiled=True)
    piece = (_mm(spread, all_grads, TN) * (1.0 / dp_size)).astype(BF16)
    weight_grad = lax.all_gather(piece, "dp", axis=0, tiled=True)
    return (attention[None], query_grad[None], weight_grad)


def solution(mesh):
    small = mesh.shape["dp"] == 16 and mesh.shape["seq"] == 2
    return jax.shard_map(
        per_device_16x2 if small else per_device,
        mesh=mesh,
        in_specs=(
            P("dp", None, "seq"),
            P("dp", "seq", None),
            P("dp", "seq", None),
            P("seq", None),
            P("dp", None),
            P(),
        ),
        out_specs=(P("dp", "seq", None), P("dp", "seq", None), P("seq", None)),
        check_vma=False,
    )
```

```python
import functools
import math

import jax
import jax.numpy as jnp
from jax import lax
from jax.experimental import pallas as pl
from jax.experimental.pallas import tpu as pltpu
from jax.sharding import PartitionSpec as P

HEAD = 128
QH = 8
GROUP = 2
F32 = jnp.float32
BF16 = jnp.bfloat16
NT = (((1,), (1,)), ((), ()))
TN = (((0,), (0,)), ((), ()))
NN = (((1,), (0,)), ((), ()))


def _mm(a, b, dims):
    return lax.dot_general(a, b, dims, preferred_element_type=F32)


def attention_kernel(parts, own, order_ref, docs_ref, q_ref, g_ref, *refs):
    kv_refs = refs[:parts]
    att_ref, qg_ref, kvg_ref = refs[parts:]
    rows = q_ref.shape[0]
    seq_len = kv_refs[0].shape[0]
    spans = seq_len // rows
    if parts == 1:
        kv = kv_refs[0][...]
    else:
        kv = (kv_refs[0][...] + kv_refs[1][...]).astype(BF16)
    keys = kv[:, :HEAD]
    values = kv[:, HEAD:]
    keys_t = keys.T
    values_t = values.T
    scale = 1.0 / math.sqrt(HEAD)
    me = lax.axis_index(own)

    def row_docs(span):
        return docs_ref[pl.ds(order_ref[span], 1), :]

    masks = []
    q_docs = row_docs(me)
    q_span = order_ref[me]
    q_pos = lax.broadcasted_iota(jnp.int32, (rows, rows), 1)
    k_pos = lax.broadcasted_iota(jnp.int32, (rows, rows), 0)
    for span in range(spans):
        k_docs = jnp.broadcast_to(row_docs(span), (rows, rows)).T
        gap = (order_ref[span] - q_span) * rows
        masks.append((k_pos + gap <= q_pos) & (k_docs == q_docs))
    allowed = jnp.concatenate(masks, axis=0)
    allowed = jnp.concatenate([allowed] * GROUP, axis=1)

    key_grad = jnp.zeros((seq_len, HEAD), F32)
    value_grad = jnp.zeros((seq_len, HEAD), F32)
    for first in range(0, QH, GROUP):
        heads = range(first, first + GROUP)
        q = jnp.concatenate([q_ref[:, h * HEAD : (h + 1) * HEAD] for h in heads], axis=0)
        g = jnp.concatenate([g_ref[:, h * HEAD : (h + 1) * HEAD] for h in heads], axis=0)
        scores = jnp.where(allowed, _mm(keys, q, NT) * scale, F32(-1e30))
        expo = jnp.exp(scores - jnp.max(scores, axis=0, keepdims=True))
        probs = expo * (1.0 / jnp.sum(expo, axis=0, keepdims=True))
        low = probs.astype(BF16)
        grad_probs = _mm(values, g, NT)
        delta = jnp.sum(probs * grad_probs, axis=0, keepdims=True)
        grad_scores = (probs * (grad_probs - delta) * scale).astype(BF16)
        att = _mm(values_t, low, NN)
        qg = _mm(keys_t, grad_scores, NN)
        for i, h in enumerate(heads):
            cols = slice(h * HEAD, (h + 1) * HEAD)
            att_ref[:, cols] = att[:, i * rows : (i + 1) * rows].T.astype(BF16)
            qg_ref[:, cols] = qg[:, i * rows : (i + 1) * rows].T.astype(BF16)
        key_grad += _mm(grad_scores, q, NN)
        value_grad += _mm(low, g, NN)
    kvg_ref[:HEAD, :] = key_grad.T
    kvg_ref[HEAD:, :] = value_grad.T


def attend(order, docs, q, g, kvs):
    vmem = pl.BlockSpec(memory_space=pltpu.VMEM)
    return pl.pallas_call(
        functools.partial(attention_kernel, len(kvs), "seq"),
        out_shape=(
            jax.ShapeDtypeStruct(q.shape, BF16),
            jax.ShapeDtypeStruct(q.shape, BF16),
            jax.ShapeDtypeStruct((2 * HEAD, kvs[0].shape[0]), F32),
        ),
        in_specs=[pl.BlockSpec(memory_space=pltpu.SMEM)] + [vmem] * (3 + len(kvs)),
        out_specs=(vmem, vmem, vmem),
        compiler_params=pltpu.CompilerParams(vmem_limit_bytes=48 * 1024 * 1024),
        name="attention_fwd_bwd",
    )(order, docs, q, g, *kvs)


ANY = pl.BlockSpec(memory_space=pl.ANY)
VMEM = pl.BlockSpec(memory_space=pltpu.VMEM)
LIMIT = pltpu.CompilerParams(vmem_limit_bytes=48 * 1024 * 1024)
CORE, Y, Z1, Z2 = 1, 2, 4, 8
CORES = 2
BLOCK = 4


def block_of(device):
    return lax.rem(device // CORES, BLOCK)


def project_kernel(tok_ref, w_ref, out_ref, *refs):
    slices, (tok_v, w_v, tok_sems, w_sems, out_sems) = refs[:BLOCK], refs[BLOCK:]
    width = slices[0].shape[1]
    mine = block_of(lax.axis_index("dp"))
    order = (1, 2, 3, 0)
    reads = []
    for k in order:
        first = pl.multiple_of((mine ^ k) * width, width)
        tok = pltpu.make_async_copy(tok_ref.at[:, pl.ds(first, width)], tok_v.at[k], tok_sems.at[k])
        w = pltpu.make_async_copy(w_ref.at[pl.ds(first, width), :], w_v.at[k], w_sems.at[k])
        tok.start()
        w.start()
        reads.append((tok, w))
    total = None
    writes = []
    for k, (tok, w) in zip(order, reads):
        tok.wait()
        write = pltpu.make_async_copy(tok_v.at[k], slices[k], out_sems.at[k])
        write.start()
        writes.append(write)
        w.wait()
        term = _mm(tok_v[k], w_v[k], NN)
        total = term if total is None else total + term
    out_ref[...] = total
    for write in writes:
        write.wait()


def project(tokens, w_kv):
    rows, features = tokens.shape
    cols = w_kv.shape[1]
    width = features // BLOCK
    return pl.pallas_call(
        project_kernel,
        out_shape=[jax.ShapeDtypeStruct((rows, cols), F32)]
        + [jax.ShapeDtypeStruct((rows, width), BF16)] * BLOCK,
        in_specs=[ANY, ANY],
        out_specs=[VMEM] + [ANY] * BLOCK,
        scratch_shapes=[
            pltpu.VMEM((BLOCK, rows, width), BF16),
            pltpu.VMEM((BLOCK, width, cols), BF16),
            pltpu.SemaphoreType.DMA((BLOCK,)),
            pltpu.SemaphoreType.DMA((BLOCK,)),
            pltpu.SemaphoreType.DMA((BLOCK,)),
        ],
        compiler_params=pltpu.CompilerParams(vmem_limit_bytes=60 * 1024 * 1024),
        name="project_and_slice",
    )(tokens, w_kv)


def round_kernel(a_ref, b_ref, *refs):
    refs[-1][...] = (a_ref[...] + b_ref[...]).astype(BF16)


def round_grad(a, b, arrived):
    return pl.pallas_call(
        round_kernel,
        out_shape=jax.ShapeDtypeStruct(a.shape, BF16),
        in_specs=[VMEM, VMEM] + [ANY] * len(arrived),
        out_specs=VMEM,
        compiler_params=LIMIT,
        name="round_grad",
    )(a, b, *arrived)


def weight_kernel(packs, near_half, *refs):
    toks, grads = refs[:BLOCK], refs[BLOCK : 2 * BLOCK]
    keep_ref, send_ref = refs[2 * BLOCK :]
    width = keep_ref.shape[1]
    me = lax.axis_index("dp")
    core = lax.rem(me, CORES)
    high = me // (CORES * BLOCK)
    high = high if near_half else 1 - high
    for ref, which in ((send_ref, 1 - core), (keep_ref, core)):
        cols = pl.ds(pl.multiple_of((which * 2 + high) * width, width), width)
        acc = _mm(grads[0][...], toks[0][:, cols], NN)
        for k in range(1, BLOCK):
            acc += _mm(grads[k][...], toks[k][:, cols], NN)
        ref[...] = acc * (1.0 / packs)


def weight_part(toks, grads, packs, near_half):
    part = jax.ShapeDtypeStruct((grads[0].shape[0], toks[0].shape[1] // (2 * CORES)), F32)
    return pl.pallas_call(
        functools.partial(weight_kernel, packs, near_half),
        out_shape=[part, part],
        in_specs=[VMEM] * (2 * BLOCK),
        out_specs=[VMEM, VMEM],
        compiler_params=LIMIT,
        name="weight_near" if near_half else "weight_far",
    )(*toks, *grads)


def fold_kernel(a_ref, b_ref, out_ref):
    out_ref[...] = a_ref[...] + b_ref[...]


def fold(a, b):
    return pl.pallas_call(
        fold_kernel,
        out_shape=jax.ShapeDtypeStruct(a.shape, F32),
        in_specs=[VMEM, VMEM],
        out_specs=VMEM,
        compiler_params=LIMIT,
        name="weight_fold",
    )(a, b)


def finish_kernel(a_ref, b_ref, c_ref, out_ref):
    out_ref[...] = (a_ref[...] + b_ref[...] + c_ref[...]).T.astype(BF16)


def finish(a, b, c):
    return pl.pallas_call(
        finish_kernel,
        out_shape=jax.ShapeDtypeStruct((a.shape[1], a.shape[0]), BF16),
        in_specs=[VMEM] * 3,
        out_specs=VMEM,
        compiler_params=LIMIT,
        name="weight_finish",
    )(a, b, c)


def stack_kernel(count, *refs):
    out_ref = refs[-1]
    first = 0
    for ref in refs[:count]:
        out_ref[first : first + ref.shape[0], :] = ref[...]
        first += ref.shape[0]


def stack(parts, after=()):
    rows = sum(part.shape[0] for part in parts)
    return pl.pallas_call(
        functools.partial(stack_kernel, len(parts)),
        out_shape=jax.ShapeDtypeStruct((rows, parts[0].shape[1]), BF16),
        in_specs=[VMEM] * len(parts) + [ANY] * len(after),
        out_specs=VMEM,
        compiler_params=LIMIT,
        name="stack",
    )(*parts, *after)


def assemble_kernel(held, rows, *refs):
    arrays, out_ref, sems = refs[: len(held)], refs[len(held)], refs[len(held) + 1]
    me = lax.axis_index("dp")
    copies = []
    for array, bits in zip(arrays, held):
        for n, bit in enumerate(bits):
            source = me ^ bit
            high = source // (CORES * BLOCK)
            place = (block_of(source) * CORES + lax.rem(source, CORES)) * 2 + high
            first = pl.multiple_of(place * rows, rows)
            copy = pltpu.make_async_copy(
                array.at[pl.ds(n * rows, rows), :],
                out_ref.at[pl.ds(first, rows), :],
                sems.at[len(copies)],
            )
            copy.start()
            copies.append(copy)
    for copy in copies:
        copy.wait()


def assemble(pieces):
    arrays = [array for array, _ in pieces]
    held = [bits for _, bits in pieces]
    count = sum(len(bits) for bits in held)
    rows = arrays[0].shape[0] // len(held[0])
    return pl.pallas_call(
        functools.partial(assemble_kernel, held, rows),
        out_shape=jax.ShapeDtypeStruct((count * rows, arrays[0].shape[1]), BF16),
        in_specs=[ANY] * len(arrays),
        out_specs=ANY,
        scratch_shapes=[pltpu.SemaphoreType.DMA((count,))],
        compiler_params=LIMIT,
        name="weight_assemble",
    )(*arrays)


def hop(value, bits):
    count = lax.axis_size("dp")
    return lax.ppermute(value, "dp", [(i, i ^ bits) for i in range(count)])


def per_device_16x2(tokens, queries, grad_out, w_kv, doc_ids, span_order):
    dp_size = lax.axis_size("dp")
    rows_dev = queries.shape[1]
    swap = [(0, 1), (1, 0)]
    near = (Y, Z1, Y | Z1)
    partial, *slices = project(tokens[0], w_kv)
    arrived = [hop(slices[k], near[k - 1]) for k in (3, 1, 2)]
    arrived = [arrived[1], arrived[2], arrived[0]]
    other = lax.ppermute(partial, "seq", swap)
    docs = doc_ids.reshape(-1, rows_dev)
    attention, query_grad, terms = attend(
        span_order, docs, queries[0], grad_out[0], [partial, other]
    )
    grad = round_grad(terms, lax.ppermute(terms, "seq", swap), [])
    grads = [grad] + [hop(grad, bits) for bits in near]
    toks = [slices[0]] + arrived
    keep, send = weight_part(toks, grads, dp_size, False)
    far = hop(fold(keep, hop(send, CORE)), Z2)
    keep, send = weight_part(toks, grads, dp_size, True)
    own = finish(keep, hop(send, CORE), far)
    z1, z2, y = hop(own, Z1), hop(own, Z2), hop(own, Y)
    z12 = hop(z2, Z1)
    zy = hop(stack([z1, z2], [y]), Y)
    z12y = hop(z12, Y)
    first = hop(stack([own, z1, z2, y]), CORE)
    last = hop(stack([zy, z12, z12y]), CORE)
    pieces = [
        (own, [0]),
        (z1, [Z1]),
        (z2, [Z2]),
        (y, [Y]),
        (zy, [Z1 | Y, Z2 | Y]),
        (z12, [Z1 | Z2]),
        (z12y, [Z1 | Z2 | Y]),
    ]
    held = [[bit | CORE for _, bits in part for bit in bits] for part in (pieces[:4], pieces[4:])]
    pieces += [(first, held[0]), (last, held[1])]
    weight_grad = assemble(pieces)
    return (attention[None], query_grad[None], weight_grad)


def per_device(tokens, queries, grad_out, w_kv, doc_ids, span_order):
    dp_size = lax.axis_size("dp")
    rows_dev = queries.shape[1]
    flat = tokens[0]
    spread = lax.all_to_all(flat, "dp", split_axis=1, concat_axis=0, tiled=True)
    partial = jnp.dot(flat, w_kv, preferred_element_type=F32)
    own = lax.psum_scatter(partial, "seq", scatter_dimension=0, tiled=True).astype(BF16)
    kvs = [lax.all_gather(own, "seq", axis=0, tiled=True)]
    docs = doc_ids.reshape(-1, rows_dev)
    attention, query_grad, terms = attend(span_order, docs, queries[0], grad_out[0], kvs)
    grad_kv = lax.psum(terms.T, "seq").astype(BF16)
    all_grads = lax.all_gather(grad_kv, "dp", axis=0, tiled=True)
    piece = (_mm(spread, all_grads, TN) * (1.0 / dp_size)).astype(BF16)
    weight_grad = lax.all_gather(piece, "dp", axis=0, tiled=True)
    return (attention[None], query_grad[None], weight_grad)


def solution(mesh):
    small = mesh.shape["dp"] == 16 and mesh.shape["seq"] == 2
    return jax.shard_map(
        per_device_16x2 if small else per_device,
        mesh=mesh,
        in_specs=(
            P("dp", None, "seq"),
            P("dp", "seq", None),
            P("dp", "seq", None),
            P("seq", None),
            P("dp", None),
            P(),
        ),
        out_specs=(P("dp", "seq", None), P("dp", "seq", None), P("seq", None)),
        check_vma=False,
    )
```

```python
import functools
import math

import jax
import jax.numpy as jnp
from jax import lax
from jax.experimental import pallas as pl
from jax.experimental.pallas import tpu as pltpu
from jax.sharding import PartitionSpec as P

HEAD = 128
QH = 8
GROUP = 2
F32 = jnp.float32
BF16 = jnp.bfloat16
NT = (((1,), (1,)), ((), ()))
TN = (((0,), (0,)), ((), ()))
NN = (((1,), (0,)), ((), ()))


def _mm(a, b, dims):
    return lax.dot_general(a, b, dims, preferred_element_type=F32)


def attention_kernel(parts, own, order_ref, docs_ref, q_ref, g_ref, *refs):
    kv_refs = refs[:parts]
    att_ref, qg_ref, kvg_ref = refs[-3:]
    rows = q_ref.shape[0]
    seq_len = kv_refs[0].shape[0]
    spans = seq_len // rows
    if parts == 1:
        kv = kv_refs[0][...]
    else:
        kv = (kv_refs[0][...] + kv_refs[1][...]).astype(BF16)
    keys = kv[:, :HEAD]
    values = kv[:, HEAD:]
    keys_t = keys.T
    values_t = values.T
    scale = 1.0 / math.sqrt(HEAD)
    me = lax.axis_index(own)

    def row_docs(span):
        return docs_ref[pl.ds(order_ref[span], 1), :]

    masks = []
    q_docs = row_docs(me)
    q_span = order_ref[me]
    q_pos = lax.broadcasted_iota(jnp.int32, (rows, rows), 1)
    k_pos = lax.broadcasted_iota(jnp.int32, (rows, rows), 0)
    for span in range(spans):
        k_docs = jnp.broadcast_to(row_docs(span), (rows, rows)).T
        gap = (order_ref[span] - q_span) * rows
        masks.append((k_pos + gap <= q_pos) & (k_docs == q_docs))
    allowed = jnp.concatenate(masks, axis=0)
    allowed = jnp.concatenate([allowed] * GROUP, axis=1)

    key_grad = jnp.zeros((seq_len, HEAD), F32)
    value_grad = jnp.zeros((seq_len, HEAD), F32)
    for first in range(0, QH, GROUP):
        heads = range(first, first + GROUP)
        q = jnp.concatenate([q_ref[:, h * HEAD : (h + 1) * HEAD] for h in heads], axis=0)
        g = jnp.concatenate([g_ref[:, h * HEAD : (h + 1) * HEAD] for h in heads], axis=0)
        scores = jnp.where(allowed, _mm(keys, q, NT) * scale, F32(-1e30))
        expo = jnp.exp(scores - jnp.max(scores, axis=0, keepdims=True))
        probs = expo * (1.0 / jnp.sum(expo, axis=0, keepdims=True))
        low = probs.astype(BF16)
        grad_probs = _mm(values, g, NT)
        delta = jnp.sum(probs * grad_probs, axis=0, keepdims=True)
        grad_scores = (probs * (grad_probs - delta) * scale).astype(BF16)
        att = _mm(values_t, low, NN)
        qg = _mm(keys_t, grad_scores, NN)
        for i, h in enumerate(heads):
            cols = slice(h * HEAD, (h + 1) * HEAD)
            att_ref[:, cols] = att[:, i * rows : (i + 1) * rows].T.astype(BF16)
            qg_ref[:, cols] = qg[:, i * rows : (i + 1) * rows].T.astype(BF16)
        key_grad += _mm(grad_scores, q, NN)
        value_grad += _mm(low, g, NN)
    kvg_ref[:HEAD, :] = key_grad.T
    kvg_ref[HEAD:, :] = value_grad.T


def attend(order, docs, q, g, kvs, after=()):
    vmem = pl.BlockSpec(memory_space=pltpu.VMEM)
    return pl.pallas_call(
        functools.partial(attention_kernel, len(kvs), "seq"),
        out_shape=(
            jax.ShapeDtypeStruct(q.shape, BF16),
            jax.ShapeDtypeStruct(q.shape, BF16),
            jax.ShapeDtypeStruct((2 * HEAD, kvs[0].shape[0]), F32),
        ),
        in_specs=[pl.BlockSpec(memory_space=pltpu.SMEM)]
        + [vmem] * (3 + len(kvs))
        + [pl.BlockSpec(memory_space=pl.ANY)] * len(after),
        out_specs=(vmem, vmem, vmem),
        compiler_params=pltpu.CompilerParams(vmem_limit_bytes=48 * 1024 * 1024),
        name="attention_fwd_bwd",
    )(order, docs, q, g, *kvs, *after)


ANY = pl.BlockSpec(memory_space=pl.ANY)
VMEM = pl.BlockSpec(memory_space=pltpu.VMEM)
LIMIT = pltpu.CompilerParams(vmem_limit_bytes=48 * 1024 * 1024)
CORE, Y, Z1, Z2 = 1, 2, 4, 8
CORES = 2
BLOCK = 4


def block_of(device):
    return lax.rem(device // CORES, BLOCK)


def half_cols(device, k, core, far_half, width):
    high = device // (CORES * BLOCK)
    high = 1 - high if far_half else high
    return pl.multiple_of((((block_of(device) ^ k) * CORES + core) * 2 + high) * width, width)


def slice_kernel(wanted, tok_ref, *refs):
    slices, sems = refs[-1 - len(wanted) : -1], refs[-1]
    me = lax.axis_index("dp")
    copies = []
    for (k, halves), ref in zip(wanted, slices):
        width = ref.shape[1] // (CORES * len(halves))
        for n, far_half in enumerate(halves):
            for core in range(CORES):
                copy = pltpu.make_async_copy(
                    tok_ref.at[:, pl.ds(half_cols(me, k, core, far_half, width), width)],
                    ref.at[:, pl.ds((n * CORES + core) * width, width)],
                    sems.at[len(copies)],
                )
                copy.start()
                copies.append(copy)
    for copy in copies:
        copy.wait()


def slice_tokens(tokens, wanted, name, after=()):
    rows, features = tokens.shape
    half = features // (2 * BLOCK)
    return pl.pallas_call(
        functools.partial(slice_kernel, wanted),
        out_shape=[jax.ShapeDtypeStruct((rows, half * len(halves)), BF16) for _, halves in wanted],
        in_specs=[ANY] * (1 + len(after)),
        out_specs=[VMEM] * len(wanted),
        scratch_shapes=[pltpu.SemaphoreType.DMA((sum(2 * len(halves) for _, halves in wanted),))],
        compiler_params=LIMIT,
        name=name,
    )(tokens, *after)


def project_kernel(tok_ref, w_ref, out_ref):
    out_ref[...] = _mm(tok_ref[...], w_ref[...], NN)


def project(tokens, w_kv):
    return pl.pallas_call(
        project_kernel,
        out_shape=jax.ShapeDtypeStruct((tokens.shape[0], w_kv.shape[1]), F32),
        in_specs=[VMEM, VMEM],
        out_specs=VMEM,
        compiler_params=LIMIT,
        name="project",
    )(tokens, w_kv)


def after_kernel(in_ref, *refs):
    refs[-1][...] = in_ref[...]


def after(value, arrived):
    return pl.pallas_call(
        after_kernel,
        out_shape=jax.ShapeDtypeStruct(value.shape, value.dtype),
        in_specs=[VMEM] + [ANY] * len(arrived),
        out_specs=VMEM,
        compiler_params=LIMIT,
        name="after",
    )(value, *arrived)


def round_kernel(a_ref, b_ref, *refs):
    refs[-1][...] = (a_ref[...] + b_ref[...]).astype(BF16)


def round_grad(a, b, arrived):
    return pl.pallas_call(
        round_kernel,
        out_shape=jax.ShapeDtypeStruct(a.shape, BF16),
        in_specs=[VMEM, VMEM] + [ANY] * len(arrived),
        out_specs=VMEM,
        compiler_params=LIMIT,
        name="round_grad",
    )(a, b, *arrived)


def weight_kernel(packs, starts, *refs):
    toks, grads = refs[:BLOCK], refs[BLOCK : 2 * BLOCK]
    keep_ref, send_ref = refs[2 * BLOCK :]
    width = keep_ref.shape[1]
    starts = [start * width for start in starts]
    core = lax.rem(lax.axis_index("dp"), CORES)
    for ref, which in ((send_ref, 1 - core), (keep_ref, core)):
        acc = None
        for k in range(BLOCK):
            first = pl.multiple_of(starts[k] + which * width, width)
            term = _mm(grads[k][...], toks[k][:, pl.ds(first, width)], NN)
            acc = term if acc is None else acc + term
        ref[...] = acc * (1.0 / packs)


def weight_part(toks, grads, packs, starts):
    part = jax.ShapeDtypeStruct((grads[0].shape[0], toks[0].shape[1] // CORES), F32)
    return pl.pallas_call(
        functools.partial(weight_kernel, packs, starts),
        out_shape=[part, part],
        in_specs=[VMEM] * (2 * BLOCK),
        out_specs=[VMEM, VMEM],
        compiler_params=LIMIT,
        name="weight_part",
    )(*toks, *grads)


def fold_kernel(a_ref, b_ref, out_ref):
    out_ref[...] = a_ref[...] + b_ref[...]


def fold(a, b):
    return pl.pallas_call(
        fold_kernel,
        out_shape=jax.ShapeDtypeStruct(a.shape, F32),
        in_specs=[VMEM, VMEM],
        out_specs=VMEM,
        compiler_params=LIMIT,
        name="weight_fold",
    )(a, b)


def finish_kernel(a_ref, b_ref, out_ref):
    out_ref[...] = (a_ref[...] + b_ref[...]).T.astype(BF16)


def finish(a, b):
    return pl.pallas_call(
        finish_kernel,
        out_shape=jax.ShapeDtypeStruct((a.shape[1], a.shape[0]), BF16),
        in_specs=[VMEM] * 2,
        out_specs=VMEM,
        compiler_params=LIMIT,
        name="weight_finish",
    )(a, b)


def stack_kernel(count, *refs):
    out_ref = refs[-1]
    first = 0
    for ref in refs[:count]:
        out_ref[first : first + ref.shape[0], :] = ref[...]
        first += ref.shape[0]


def stack(parts, after=()):
    rows = sum(part.shape[0] for part in parts)
    return pl.pallas_call(
        functools.partial(stack_kernel, len(parts)),
        out_shape=jax.ShapeDtypeStruct((rows, parts[0].shape[1]), BF16),
        in_specs=[VMEM] * len(parts) + [ANY] * len(after),
        out_specs=VMEM,
        compiler_params=LIMIT,
        name="stack",
    )(*parts, *after)


def assemble_kernel(held, rows, *refs):
    arrays, out_ref, sems = refs[: len(held)], refs[len(held)], refs[len(held) + 1]
    me = lax.axis_index("dp")
    copies = []
    for array, bits in zip(arrays, held):
        for n, bit in enumerate(bits):
            source = me ^ bit
            high = source // (CORES * BLOCK)
            place = (block_of(source) * CORES + lax.rem(source, CORES)) * 2 + high
            first = pl.multiple_of(place * rows, rows)
            copy = pltpu.make_async_copy(
                array.at[pl.ds(n * rows, rows), :],
                out_ref.at[pl.ds(first, rows), :],
                sems.at[len(copies)],
            )
            copy.start()
            copies.append(copy)
    for copy in copies:
        copy.wait()


def assemble(pieces):
    arrays = [array for array, _ in pieces]
    held = [bits for _, bits in pieces]
    count = sum(len(bits) for bits in held)
    rows = arrays[0].shape[0] // len(held[0])
    return pl.pallas_call(
        functools.partial(assemble_kernel, held, rows),
        out_shape=jax.ShapeDtypeStruct((count * rows, arrays[0].shape[1]), BF16),
        in_specs=[ANY] * len(arrays),
        out_specs=ANY,
        scratch_shapes=[pltpu.SemaphoreType.DMA((count,))],
        compiler_params=LIMIT,
        name="weight_assemble",
    )(*arrays)


def hop(value, bits):
    count = lax.axis_size("dp")
    return lax.ppermute(value, "dp", [(i, i ^ bits) for i in range(count)])


def per_device_16x2(tokens, queries, grad_out, w_kv, doc_ids, span_order):
    dp_size = lax.axis_size("dp")
    rows_dev = queries.shape[1]
    swap = [(0, 1), (1, 0)]
    near = (Y, Z1, Y | Z1)
    flat = tokens[0]
    far_own, far_y, far_z, diagonal = slice_tokens(
        flat, [(0, (True,)), (1, (True,)), (2, (True,)), (3, (True, False))], "slice_far"
    )
    far_y, far_z, diagonal = hop(far_y, Y), hop(far_z, Z1), hop(diagonal, Y | Z1)
    partial = project(flat, w_kv)
    other = lax.ppermute(partial, "seq", swap)
    docs = doc_ids.reshape(-1, rows_dev)
    attention, query_grad, terms = attend(
        span_order, docs, queries[0], grad_out[0], [partial, other]
    )
    terms = after(terms, [far_y, far_z])
    grad = round_grad(terms, lax.ppermute(terms, "seq", swap), [diagonal])
    grads = [grad] + [hop(grad, bits) for bits in near]
    keep, send = weight_part([far_own, far_y, far_z, diagonal], grads, dp_size, [0, 0, 0, 0])
    part = fold(keep, hop(send, CORE))
    far = hop(part, Z2)
    near_own, near_y, near_z = slice_tokens(
        flat, [(0, (False,)), (1, (False,)), (2, (False,))], "slice_near", []
    )
    near_y, near_z = hop(near_y, Y), hop(near_z, Z1)
    keep, send = weight_part([near_own, near_y, near_z, diagonal], grads, dp_size, [0, 0, 0, 2])
    own = finish(fold(keep, far), hop(send, CORE))
    z1, z2, y = hop(own, Z1), hop(own, Z2), hop(own, Y)
    z12 = hop(z2, Z1)
    zy = hop(stack([z1, z2], [y]), Y)
    z12y = hop(z12, Y)
    first = hop(stack([own, z1, z2, y]), CORE)
    last = hop(stack([zy, z12, z12y]), CORE)
    pieces = [
        (own, [0]),
        (z1, [Z1]),
        (z2, [Z2]),
        (y, [Y]),
        (zy, [Z1 | Y, Z2 | Y]),
        (z12, [Z1 | Z2]),
        (z12y, [Z1 | Z2 | Y]),
    ]
    held = [[bit | CORE for _, bits in part for bit in bits] for part in (pieces[:4], pieces[4:])]
    pieces += [(first, held[0]), (last, held[1])]
    weight_grad = assemble(pieces)
    return (attention[None], query_grad[None], weight_grad)


def per_device(tokens, queries, grad_out, w_kv, doc_ids, span_order):
    dp_size = lax.axis_size("dp")
    rows_dev = queries.shape[1]
    flat = tokens[0]
    spread = lax.all_to_all(flat, "dp", split_axis=1, concat_axis=0, tiled=True)
    partial = jnp.dot(flat, w_kv, preferred_element_type=F32)
    own = lax.psum_scatter(partial, "seq", scatter_dimension=0, tiled=True).astype(BF16)
    kvs = [lax.all_gather(own, "seq", axis=0, tiled=True)]
    docs = doc_ids.reshape(-1, rows_dev)
    attention, query_grad, terms = attend(span_order, docs, queries[0], grad_out[0], kvs)
    grad_kv = lax.psum(terms.T, "seq").astype(BF16)
    all_grads = lax.all_gather(grad_kv, "dp", axis=0, tiled=True)
    piece = (_mm(spread, all_grads, TN) * (1.0 / dp_size)).astype(BF16)
    weight_grad = lax.all_gather(piece, "dp", axis=0, tiled=True)
    return (attention[None], query_grad[None], weight_grad)


def solution(mesh):
    small = mesh.shape["dp"] == 16 and mesh.shape["seq"] == 2
    return jax.shard_map(
        per_device_16x2 if small else per_device,
        mesh=mesh,
        in_specs=(
            P("dp", None, "seq"),
            P("dp", "seq", None),
            P("dp", "seq", None),
            P("seq", None),
            P("dp", None),
            P(),
        ),
        out_specs=(P("dp", "seq", None), P("dp", "seq", None), P("seq", None)),
        check_vma=False,
    )
```

```python
import functools
import math

import jax
import jax.numpy as jnp
from jax import lax
from jax.experimental import pallas as pl
from jax.experimental.pallas import tpu as pltpu
from jax.sharding import PartitionSpec as P

HEAD = 128
QH = 8
GROUP = 2
F32 = jnp.float32
BF16 = jnp.bfloat16
NT = (((1,), (1,)), ((), ()))
TN = (((0,), (0,)), ((), ()))
NN = (((1,), (0,)), ((), ()))


def _mm(a, b, dims):
    return lax.dot_general(a, b, dims, preferred_element_type=F32)


ANY = pl.BlockSpec(memory_space=pl.ANY)
VMEM = pl.BlockSpec(memory_space=pltpu.VMEM)
LIMIT = pltpu.CompilerParams(vmem_limit_bytes=48 * 1024 * 1024)


def terms_kernel(parts, own, order_ref, docs_ref, q_ref, g_ref, *refs):
    kv_refs = refs[:parts]
    kv_ref, low_ref, ds_ref, terms_ref = refs[-4:]
    rows = q_ref.shape[0]
    seq_len = kv_refs[0].shape[0]
    spans = seq_len // rows
    if parts == 1:
        kv = kv_refs[0][...]
    else:
        kv = (kv_refs[0][...] + kv_refs[1][...]).astype(BF16)
    kv_ref[...] = kv
    keys = kv[:, :HEAD]
    values = kv[:, HEAD:]
    scale = 1.0 / math.sqrt(HEAD)
    me = lax.axis_index(own)

    def row_docs(span):
        return docs_ref[pl.ds(order_ref[span], 1), :]

    masks = []
    q_docs = row_docs(me)
    q_span = order_ref[me]
    q_pos = lax.broadcasted_iota(jnp.int32, (rows, rows), 1)
    k_pos = lax.broadcasted_iota(jnp.int32, (rows, rows), 0)
    for span in range(spans):
        k_docs = jnp.broadcast_to(row_docs(span), (rows, rows)).T
        gap = (order_ref[span] - q_span) * rows
        masks.append((k_pos + gap <= q_pos) & (k_docs == q_docs))
    allowed = jnp.concatenate(masks, axis=0)
    allowed = jnp.concatenate([allowed] * GROUP, axis=1)

    key_grad = jnp.zeros((seq_len, HEAD), F32)
    value_grad = jnp.zeros((seq_len, HEAD), F32)
    for first in range(0, QH, GROUP):
        heads = range(first, first + GROUP)
        q = jnp.concatenate([q_ref[:, h * HEAD : (h + 1) * HEAD] for h in heads], axis=0)
        g = jnp.concatenate([g_ref[:, h * HEAD : (h + 1) * HEAD] for h in heads], axis=0)
        scores = jnp.where(allowed, _mm(keys, q, NT) * scale, F32(-1e30))
        expo = jnp.exp(scores - jnp.max(scores, axis=0, keepdims=True))
        probs = expo * (1.0 / jnp.sum(expo, axis=0, keepdims=True))
        low = probs.astype(BF16)
        grad_probs = _mm(values, g, NT)
        delta = jnp.sum(probs * grad_probs, axis=0, keepdims=True)
        grad_scores = (probs * (grad_probs - delta) * scale).astype(BF16)
        low_ref[:, first * rows : (first + GROUP) * rows] = low
        ds_ref[:, first * rows : (first + GROUP) * rows] = grad_scores
        key_grad += _mm(grad_scores, q, NN)
        value_grad += _mm(low, g, NN)
    terms_ref[:HEAD, :] = key_grad.T
    terms_ref[HEAD:, :] = value_grad.T


def outputs_kernel(kv_ref, low_ref, ds_ref, att_ref, qg_ref, done_ref):
    rows = att_ref.shape[0]
    done_ref[...] = jnp.zeros_like(done_ref)
    keys_t = kv_ref[:, :HEAD].T
    values_t = kv_ref[:, HEAD:].T
    for first in range(0, QH, GROUP):
        cols = slice(first * rows, (first + GROUP) * rows)
        att = _mm(values_t, low_ref[:, cols], NN)
        qg = _mm(keys_t, ds_ref[:, cols], NN)
        for i in range(GROUP):
            head = slice((first + i) * HEAD, (first + i + 1) * HEAD)
            att_ref[:, head] = att[:, i * rows : (i + 1) * rows].T.astype(BF16)
            qg_ref[:, head] = qg[:, i * rows : (i + 1) * rows].T.astype(BF16)


def attend(order, docs, q, g, kvs):
    seq_len, rows = kvs[0].shape[0], q.shape[0]
    kv, low, grad_scores, terms = pl.pallas_call(
        functools.partial(terms_kernel, len(kvs), "seq"),
        out_shape=(
            jax.ShapeDtypeStruct((seq_len, 2 * HEAD), BF16),
            jax.ShapeDtypeStruct((seq_len, QH * rows), BF16),
            jax.ShapeDtypeStruct((seq_len, QH * rows), BF16),
            jax.ShapeDtypeStruct((2 * HEAD, seq_len), F32),
        ),
        in_specs=[pl.BlockSpec(memory_space=pltpu.SMEM)] + [VMEM] * (3 + len(kvs)),
        out_specs=[VMEM] * 4,
        compiler_params=LIMIT,
        name="attention_terms",
    )(order, docs, q, g, *kvs)
    attention, query_grad, done = pl.pallas_call(
        outputs_kernel,
        out_shape=[jax.ShapeDtypeStruct(q.shape, BF16)] * 2 + [jax.ShapeDtypeStruct((8, HEAD), F32)],
        in_specs=[VMEM] * 3,
        out_specs=[VMEM] * 3,
        compiler_params=LIMIT,
        name="attention_outputs",
    )(kv, low, grad_scores)
    return attention, query_grad, terms, done


CORE, Y, Z1, Z2 = 1, 2, 4, 8
CORES = 2
BLOCK = 4


def block_of(device):
    return lax.rem(device // CORES, BLOCK)


def half_cols(device, k, core, far_half, width):
    high = device // (CORES * BLOCK)
    high = 1 - high if far_half else high
    return pl.multiple_of((((block_of(device) ^ k) * CORES + core) * 2 + high) * width, width)


def slice_kernel(wanted, tok_ref, *refs):
    slices, sems = refs[-1 - len(wanted) : -1], refs[-1]
    me = lax.axis_index("dp")
    copies = []
    for (k, halves), ref in zip(wanted, slices):
        width = ref.shape[1] // (CORES * len(halves))
        for n, far_half in enumerate(halves):
            for core in range(CORES):
                copy = pltpu.make_async_copy(
                    tok_ref.at[:, pl.ds(half_cols(me, k, core, far_half, width), width)],
                    ref.at[:, pl.ds((n * CORES + core) * width, width)],
                    sems.at[len(copies)],
                )
                copy.start()
                copies.append(copy)
    for copy in copies:
        copy.wait()


def slice_tokens(tokens, wanted, name, after=()):
    rows, features = tokens.shape
    half = features // (2 * BLOCK)
    return pl.pallas_call(
        functools.partial(slice_kernel, wanted),
        out_shape=[jax.ShapeDtypeStruct((rows, half * len(halves)), BF16) for _, halves in wanted],
        in_specs=[ANY] * (1 + len(after)),
        out_specs=[VMEM] * len(wanted),
        scratch_shapes=[pltpu.SemaphoreType.DMA((sum(2 * len(halves) for _, halves in wanted),))],
        compiler_params=LIMIT,
        name=name,
    )(tokens, *after)


def project_kernel(tok_ref, w_ref, out_ref):
    out_ref[...] = _mm(tok_ref[...], w_ref[...], NN)


def project(tokens, w_kv):
    return pl.pallas_call(
        project_kernel,
        out_shape=jax.ShapeDtypeStruct((tokens.shape[0], w_kv.shape[1]), F32),
        in_specs=[VMEM, VMEM],
        out_specs=VMEM,
        compiler_params=LIMIT,
        name="project",
    )(tokens, w_kv)


def after_kernel(in_ref, *refs):
    refs[-1][...] = in_ref[...]


def after(value, arrived):
    return pl.pallas_call(
        after_kernel,
        out_shape=jax.ShapeDtypeStruct(value.shape, value.dtype),
        in_specs=[VMEM] + [ANY] * len(arrived),
        out_specs=VMEM,
        compiler_params=LIMIT,
        name="after",
    )(value, *arrived)


def round_kernel(a_ref, b_ref, *refs):
    refs[-1][...] = (a_ref[...] + b_ref[...]).astype(BF16)


def round_grad(a, b, arrived):
    return pl.pallas_call(
        round_kernel,
        out_shape=jax.ShapeDtypeStruct(a.shape, BF16),
        in_specs=[VMEM, VMEM] + [ANY] * len(arrived),
        out_specs=VMEM,
        compiler_params=LIMIT,
        name="round_grad",
    )(a, b, *arrived)


def weight_kernel(packs, starts, *refs):
    toks, grads = refs[:BLOCK], refs[BLOCK : 2 * BLOCK]
    keep_ref, send_ref = refs[2 * BLOCK :]
    width = keep_ref.shape[1]
    starts = [start * width for start in starts]
    core = lax.rem(lax.axis_index("dp"), CORES)
    for ref, which in ((send_ref, 1 - core), (keep_ref, core)):
        acc = None
        for k in range(BLOCK):
            first = pl.multiple_of(starts[k] + which * width, width)
            term = _mm(grads[k][...], toks[k][:, pl.ds(first, width)], NN)
            acc = term if acc is None else acc + term
        ref[...] = acc * (1.0 / packs)


def weight_part(toks, grads, packs, starts):
    part = jax.ShapeDtypeStruct((grads[0].shape[0], toks[0].shape[1] // CORES), F32)
    return pl.pallas_call(
        functools.partial(weight_kernel, packs, starts),
        out_shape=[part, part],
        in_specs=[VMEM] * (2 * BLOCK),
        out_specs=[VMEM, VMEM],
        compiler_params=LIMIT,
        name="weight_part",
    )(*toks, *grads)


def fold_kernel(a_ref, b_ref, out_ref):
    out_ref[...] = a_ref[...] + b_ref[...]


def fold(a, b):
    return pl.pallas_call(
        fold_kernel,
        out_shape=jax.ShapeDtypeStruct(a.shape, F32),
        in_specs=[VMEM, VMEM],
        out_specs=VMEM,
        compiler_params=LIMIT,
        name="weight_fold",
    )(a, b)


def finish_kernel(a_ref, b_ref, out_ref):
    out_ref[...] = (a_ref[...] + b_ref[...]).T.astype(BF16)


def finish(a, b):
    return pl.pallas_call(
        finish_kernel,
        out_shape=jax.ShapeDtypeStruct((a.shape[1], a.shape[0]), BF16),
        in_specs=[VMEM] * 2,
        out_specs=VMEM,
        compiler_params=LIMIT,
        name="weight_finish",
    )(a, b)


def stack_kernel(count, *refs):
    out_ref = refs[-1]
    first = 0
    for ref in refs[:count]:
        out_ref[first : first + ref.shape[0], :] = ref[...]
        first += ref.shape[0]


def stack(parts, after=()):
    rows = sum(part.shape[0] for part in parts)
    return pl.pallas_call(
        functools.partial(stack_kernel, len(parts)),
        out_shape=jax.ShapeDtypeStruct((rows, parts[0].shape[1]), BF16),
        in_specs=[VMEM] * len(parts) + [ANY] * len(after),
        out_specs=VMEM,
        compiler_params=LIMIT,
        name="stack",
    )(*parts, *after)


def assemble_kernel(held, rows, *refs):
    arrays, out_ref, sems = refs[: len(held)], refs[-2], refs[-1]
    me = lax.axis_index("dp")
    copies = []
    for array, bits in zip(arrays, held):
        for n, bit in enumerate(bits):
            source = me ^ bit
            high = source // (CORES * BLOCK)
            place = (block_of(source) * CORES + lax.rem(source, CORES)) * 2 + high
            first = pl.multiple_of(place * rows, rows)
            copy = pltpu.make_async_copy(
                array.at[pl.ds(n * rows, rows), :],
                out_ref.at[pl.ds(first, rows), :],
                sems.at[len(copies)],
            )
            copy.start()
            copies.append(copy)
    for copy in copies:
        copy.wait()


def assemble(pieces, total, begun=None):
    arrays = [array for array, _ in pieces]
    held = [bits for _, bits in pieces]
    rows = arrays[0].shape[0] // len(held[0])
    count = len(arrays)
    if begun is not None:
        arrays.append(begun)
    return pl.pallas_call(
        functools.partial(assemble_kernel, held, rows),
        out_shape=jax.ShapeDtypeStruct((total * rows, arrays[0].shape[1]), BF16),
        in_specs=[ANY] * len(arrays),
        out_specs=ANY,
        scratch_shapes=[pltpu.SemaphoreType.DMA((sum(len(bits) for bits in held),))],
        input_output_aliases={} if begun is None else {count: 0},
        compiler_params=LIMIT,
        name="weight_assemble" if begun is None else "weight_complete",
    )(*arrays)


def hop(value, bits):
    count = lax.axis_size("dp")
    return lax.ppermute(value, "dp", [(i, i ^ bits) for i in range(count)])


def per_device_16x2(tokens, queries, grad_out, w_kv, doc_ids, span_order):
    dp_size = lax.axis_size("dp")
    rows_dev = queries.shape[1]
    swap = [(0, 1), (1, 0)]
    near = (Y, Z1, Y | Z1)
    flat = tokens[0]
    far_own, far_y, far_z, diagonal = slice_tokens(
        flat, [(0, (True,)), (1, (True,)), (2, (True,)), (3, (True, False))], "slice_far"
    )
    far_y, far_z, diagonal = hop(far_y, Y), hop(far_z, Z1), hop(diagonal, Y | Z1)
    partial = project(flat, w_kv)
    other = lax.ppermute(partial, "seq", swap)
    docs = doc_ids.reshape(-1, rows_dev)
    attention, query_grad, terms, done = attend(
        span_order, docs, queries[0], grad_out[0], [partial, other]
    )
    terms = after(terms, [far_y, far_z])
    grad = round_grad(terms, lax.ppermute(terms, "seq", swap), [done])
    grads = [grad] + [hop(grad, bits) for bits in near]
    keep, send = weight_part([far_own, far_y, far_z, diagonal], grads, dp_size, [0, 0, 0, 0])
    part = fold(keep, hop(send, CORE))
    far = hop(part, Z2)
    near_own, near_y, near_z = slice_tokens(
        flat, [(0, (False,)), (1, (False,)), (2, (False,))], "slice_near", []
    )
    near_y, near_z = hop(near_y, Y), hop(near_z, Z1)
    keep, send = weight_part([near_own, near_y, near_z, diagonal], grads, dp_size, [0, 0, 0, 2])
    own = finish(fold(keep, far), hop(send, CORE))
    z1, z2, y = hop(own, Z1), hop(own, Z2), hop(own, Y)
    z12 = hop(z2, Z1)
    zy = hop(stack([z1, z2], [y]), Y)
    z12y = hop(z12, Y)
    first = hop(stack([own, z1, z2, y]), CORE)
    last = hop(stack([zy, z12, z12y]), CORE)
    pieces = [
        (own, [0]),
        (z1, [Z1]),
        (z2, [Z2]),
        (y, [Y]),
        (zy, [Z1 | Y, Z2 | Y]),
        (z12, [Z1 | Z2]),
        (z12y, [Z1 | Z2 | Y]),
    ]
    held = [[bit | CORE for _, bits in part for bit in bits] for part in (pieces[:4], pieces[4:])]
    weight_grad = assemble(pieces + [(first, held[0])], dp_size)
    weight_grad = assemble([(last, held[1])], dp_size, weight_grad)
    return (attention[None], query_grad[None], weight_grad)


def per_device(tokens, queries, grad_out, w_kv, doc_ids, span_order):
    dp_size = lax.axis_size("dp")
    rows_dev = queries.shape[1]
    flat = tokens[0]
    spread = lax.all_to_all(flat, "dp", split_axis=1, concat_axis=0, tiled=True)
    partial = jnp.dot(flat, w_kv, preferred_element_type=F32)
    own = lax.psum_scatter(partial, "seq", scatter_dimension=0, tiled=True).astype(BF16)
    kvs = [lax.all_gather(own, "seq", axis=0, tiled=True)]
    docs = doc_ids.reshape(-1, rows_dev)
    attention, query_grad, terms, done = attend(span_order, docs, queries[0], grad_out[0], kvs)
    grad_kv = lax.psum(terms.T, "seq").astype(BF16)
    all_grads = lax.all_gather(grad_kv, "dp", axis=0, tiled=True)
    piece = (_mm(spread, all_grads, TN) * (1.0 / dp_size)).astype(BF16)
    weight_grad = lax.all_gather(piece, "dp", axis=0, tiled=True)
    return (attention[None], query_grad[None], weight_grad)


def solution(mesh):
    small = mesh.shape["dp"] == 16 and mesh.shape["seq"] == 2
    return jax.shard_map(
        per_device_16x2 if small else per_device,
        mesh=mesh,
        in_specs=(
            P("dp", None, "seq"),
            P("dp", "seq", None),
            P("dp", "seq", None),
            P("seq", None),
            P("dp", None),
            P(),
        ),
        out_specs=(P("dp", "seq", None), P("dp", "seq", None), P("seq", None)),
        check_vma=False,
    )
```

```python
import functools
import math

import jax
import jax.numpy as jnp
from jax import lax
from jax.experimental import pallas as pl
from jax.experimental.pallas import tpu as pltpu
from jax.sharding import PartitionSpec as P

HEAD = 128
QH = 8
GROUP = 2
F32 = jnp.float32
BF16 = jnp.bfloat16
NT = (((1,), (1,)), ((), ()))
TN = (((0,), (0,)), ((), ()))
NN = (((1,), (0,)), ((), ()))


def _mm(a, b, dims):
    return lax.dot_general(a, b, dims, preferred_element_type=F32)


ANY = pl.BlockSpec(memory_space=pl.ANY)
VMEM = pl.BlockSpec(memory_space=pltpu.VMEM)
LIMIT = pltpu.CompilerParams(vmem_limit_bytes=48 * 1024 * 1024)


def terms_kernel(parts, own, order_ref, docs_ref, q_ref, g_ref, *refs):
    kv_refs = refs[:parts]
    kv_ref, low_ref, ds_ref, terms_ref = refs[-4:]
    rows = q_ref.shape[0]
    seq_len = kv_refs[0].shape[0]
    spans = seq_len // rows
    if parts == 1:
        kv = kv_refs[0][...]
    else:
        kv = (kv_refs[0][...] + kv_refs[1][...]).astype(BF16)
    kv_ref[...] = kv
    keys = kv[:, :HEAD]
    values = kv[:, HEAD:]
    scale = 1.0 / math.sqrt(HEAD)
    me = lax.axis_index(own)

    def row_docs(span):
        return docs_ref[pl.ds(order_ref[span], 1), :]

    masks = []
    q_docs = row_docs(me)
    q_span = order_ref[me]
    q_pos = lax.broadcasted_iota(jnp.int32, (rows, rows), 1)
    k_pos = lax.broadcasted_iota(jnp.int32, (rows, rows), 0)
    for span in range(spans):
        k_docs = jnp.broadcast_to(row_docs(span), (rows, rows)).T
        gap = (order_ref[span] - q_span) * rows
        masks.append((k_pos + gap <= q_pos) & (k_docs == q_docs))
    allowed = jnp.concatenate(masks, axis=0)
    allowed = jnp.concatenate([allowed] * GROUP, axis=1)

    key_grad = jnp.zeros((seq_len, HEAD), F32)
    value_grad = jnp.zeros((seq_len, HEAD), F32)
    for first in range(0, QH, GROUP):
        heads = range(first, first + GROUP)
        q = jnp.concatenate([q_ref[:, h * HEAD : (h + 1) * HEAD] for h in heads], axis=0)
        g = jnp.concatenate([g_ref[:, h * HEAD : (h + 1) * HEAD] for h in heads], axis=0)
        scores = jnp.where(allowed, _mm(keys, q, NT) * scale, F32(-1e30))
        expo = jnp.exp(scores - jnp.max(scores, axis=0, keepdims=True))
        probs = expo * (1.0 / jnp.sum(expo, axis=0, keepdims=True))
        low = probs.astype(BF16)
        grad_probs = _mm(values, g, NT)
        delta = jnp.sum(probs * grad_probs, axis=0, keepdims=True)
        grad_scores = (probs * (grad_probs - delta) * scale).astype(BF16)
        low_ref[:, first * rows : (first + GROUP) * rows] = low
        ds_ref[:, first * rows : (first + GROUP) * rows] = grad_scores
        key_grad += _mm(grad_scores, q, NN)
        value_grad += _mm(low, g, NN)
    terms_ref[:HEAD, :] = key_grad.T
    terms_ref[HEAD:, :] = value_grad.T


def outputs_kernel(kv_ref, low_ref, ds_ref, att_ref, qg_ref, done_ref):
    rows = att_ref.shape[0]
    done_ref[...] = jnp.zeros_like(done_ref)
    keys_t = kv_ref[:, :HEAD].T
    values_t = kv_ref[:, HEAD:].T
    for first in range(0, QH, GROUP):
        cols = slice(first * rows, (first + GROUP) * rows)
        att = _mm(values_t, low_ref[:, cols], NN)
        qg = _mm(keys_t, ds_ref[:, cols], NN)
        for i in range(GROUP):
            head = slice((first + i) * HEAD, (first + i + 1) * HEAD)
            att_ref[:, head] = att[:, i * rows : (i + 1) * rows].T.astype(BF16)
            qg_ref[:, head] = qg[:, i * rows : (i + 1) * rows].T.astype(BF16)


def attend(order, docs, q, g, kvs):
    seq_len, rows = kvs[0].shape[0], q.shape[0]
    kv, low, grad_scores, terms = pl.pallas_call(
        functools.partial(terms_kernel, len(kvs), "seq"),
        out_shape=(
            jax.ShapeDtypeStruct((seq_len, 2 * HEAD), BF16),
            jax.ShapeDtypeStruct((seq_len, QH * rows), BF16),
            jax.ShapeDtypeStruct((seq_len, QH * rows), BF16),
            jax.ShapeDtypeStruct((2 * HEAD, seq_len), F32),
        ),
        in_specs=[pl.BlockSpec(memory_space=pltpu.SMEM)] + [VMEM] * (3 + len(kvs)),
        out_specs=[VMEM] * 4,
        compiler_params=LIMIT,
        name="attention_terms",
    )(order, docs, q, g, *kvs)
    attention, query_grad, done = pl.pallas_call(
        outputs_kernel,
        out_shape=[jax.ShapeDtypeStruct(q.shape, BF16)] * 2 + [jax.ShapeDtypeStruct((8, HEAD), F32)],
        in_specs=[VMEM] * 3,
        out_specs=[VMEM] * 3,
        compiler_params=LIMIT,
        name="attention_outputs",
    )(kv, low, grad_scores)
    return attention, query_grad, terms, done


CORE, Y, Z1, Z2 = 1, 2, 4, 8
CORES = 2
BLOCK = 4


def block_of(device):
    return lax.rem(device // CORES, BLOCK)


def half_cols(device, k, core, far_half, width):
    high = device // (CORES * BLOCK)
    high = 1 - high if far_half else high
    return pl.multiple_of((((block_of(device) ^ k) * CORES + core) * 2 + high) * width, width)


def slice_kernel(wanted, tok_ref, *refs):
    slices, sems = refs[-1 - len(wanted) : -1], refs[-1]
    me = lax.axis_index("dp")
    copies = []
    for (k, halves), ref in zip(wanted, slices):
        width = ref.shape[1] // (CORES * len(halves))
        for n, far_half in enumerate(halves):
            for core in range(CORES):
                copy = pltpu.make_async_copy(
                    tok_ref.at[:, pl.ds(half_cols(me, k, core, far_half, width), width)],
                    ref.at[:, pl.ds((n * CORES + core) * width, width)],
                    sems.at[len(copies)],
                )
                copy.start()
                copies.append(copy)
    for copy in copies:
        copy.wait()


def slice_tokens(tokens, wanted, name, after=()):
    rows, features = tokens.shape
    half = features // (2 * BLOCK)
    return pl.pallas_call(
        functools.partial(slice_kernel, wanted),
        out_shape=[jax.ShapeDtypeStruct((rows, half * len(halves)), BF16) for _, halves in wanted],
        in_specs=[ANY] * (1 + len(after)),
        out_specs=[VMEM] * len(wanted),
        scratch_shapes=[pltpu.SemaphoreType.DMA((sum(2 * len(halves) for _, halves in wanted),))],
        compiler_params=LIMIT,
        name=name,
    )(tokens, *after)


def project_kernel(tok_ref, w_ref, out_ref):
    out_ref[...] = _mm(tok_ref[...], w_ref[...], NN)


def project(tokens, w_kv):
    return pl.pallas_call(
        project_kernel,
        out_shape=jax.ShapeDtypeStruct((tokens.shape[0], w_kv.shape[1]), F32),
        in_specs=[VMEM, VMEM],
        out_specs=VMEM,
        compiler_params=LIMIT,
        name="project",
    )(tokens, w_kv)


def after_kernel(in_ref, *refs):
    refs[-1][...] = in_ref[...]


def after(value, arrived):
    return pl.pallas_call(
        after_kernel,
        out_shape=jax.ShapeDtypeStruct(value.shape, value.dtype),
        in_specs=[VMEM] + [ANY] * len(arrived),
        out_specs=VMEM,
        compiler_params=LIMIT,
        name="after",
    )(value, *arrived)


def round_kernel(a_ref, b_ref, *refs):
    refs[-1][...] = (a_ref[...] + b_ref[...]).astype(BF16)


def round_grad(a, b, arrived):
    return pl.pallas_call(
        round_kernel,
        out_shape=jax.ShapeDtypeStruct(a.shape, BF16),
        in_specs=[VMEM, VMEM] + [ANY] * len(arrived),
        out_specs=VMEM,
        compiler_params=LIMIT,
        name="round_grad",
    )(a, b, *arrived)


def weight_kernel(packs, starts, *refs):
    toks, grads = refs[:BLOCK], refs[BLOCK : 2 * BLOCK]
    keep_ref, send_ref = refs[2 * BLOCK :]
    width = keep_ref.shape[1]
    starts = [start * width for start in starts]
    core = lax.rem(lax.axis_index("dp"), CORES)
    for ref, which in ((send_ref, 1 - core), (keep_ref, core)):
        acc = None
        for k in range(BLOCK):
            first = pl.multiple_of(starts[k] + which * width, width)
            term = _mm(grads[k][...], toks[k][:, pl.ds(first, width)], NN)
            acc = term if acc is None else acc + term
        ref[...] = acc * (1.0 / packs)


def weight_part(toks, grads, packs, starts):
    part = jax.ShapeDtypeStruct((grads[0].shape[0], toks[0].shape[1] // CORES), F32)
    return pl.pallas_call(
        functools.partial(weight_kernel, packs, starts),
        out_shape=[part, part],
        in_specs=[VMEM] * (2 * BLOCK),
        out_specs=[VMEM, VMEM],
        compiler_params=LIMIT,
        name="weight_part",
    )(*toks, *grads)


def fold_kernel(a_ref, b_ref, *refs):
    low_ref, high_ref = refs[-2:]
    half = low_ref.shape[1]
    low_ref[...] = a_ref[:, :half] + b_ref[:, :half]
    high_ref[...] = a_ref[:, half:] + b_ref[:, half:]


def fold(a, b, arrived=()):
    half = jax.ShapeDtypeStruct((a.shape[0], a.shape[1] // 2), F32)
    return pl.pallas_call(
        fold_kernel,
        out_shape=[half, half],
        in_specs=[VMEM, VMEM] + [ANY] * len(arrived),
        out_specs=[VMEM, VMEM],
        compiler_params=LIMIT,
        name="weight_fold",
    )(a, b, *arrived)


def finish_kernel(a_ref, b_ref, out_ref):
    out_ref[...] = (a_ref[...] + b_ref[...]).T.astype(BF16)


def finish(a, b):
    return pl.pallas_call(
        finish_kernel,
        out_shape=jax.ShapeDtypeStruct((a.shape[1], a.shape[0]), BF16),
        in_specs=[VMEM] * 2,
        out_specs=VMEM,
        compiler_params=LIMIT,
        name="weight_finish",
    )(a, b)


def stack_kernel(count, *refs):
    out_ref = refs[-1]
    first = 0
    for ref in refs[:count]:
        out_ref[first : first + ref.shape[0], :] = ref[...]
        first += ref.shape[0]


def stack(parts, after=()):
    rows = sum(part.shape[0] for part in parts)
    return pl.pallas_call(
        functools.partial(stack_kernel, len(parts)),
        out_shape=jax.ShapeDtypeStruct((rows, parts[0].shape[1]), BF16),
        in_specs=[VMEM] * len(parts) + [ANY] * len(after),
        out_specs=VMEM,
        compiler_params=LIMIT,
        name="stack",
    )(*parts, *after)


def assemble_kernel(held, rows, *refs):
    arrays, out_ref, sems = refs[: len(held)], refs[-2], refs[-1]
    me = lax.axis_index("dp")
    copies = []
    for array, bits in zip(arrays, held):
        for n, (bit, half) in enumerate(bits):
            source = me ^ bit
            high = source // (CORES * BLOCK)
            place = ((block_of(source) * CORES + lax.rem(source, CORES)) * 2 + high) * 2 + half
            first = pl.multiple_of(place * rows, rows)
            copy = pltpu.make_async_copy(
                array.at[pl.ds(n * rows, rows), :],
                out_ref.at[pl.ds(first, rows), :],
                sems.at[len(copies)],
            )
            copy.start()
            copies.append(copy)
    for copy in copies:
        copy.wait()


def assemble(pieces, total, begun=None):
    arrays = [array for array, _ in pieces]
    held = [bits for _, bits in pieces]
    rows = arrays[0].shape[0] // len(held[0])
    count = len(arrays)
    if begun is not None:
        arrays.append(begun)
    return pl.pallas_call(
        functools.partial(assemble_kernel, held, rows),
        out_shape=jax.ShapeDtypeStruct((total * rows, arrays[0].shape[1]), BF16),
        in_specs=[ANY] * len(arrays),
        out_specs=ANY,
        scratch_shapes=[pltpu.SemaphoreType.DMA((sum(len(bits) for bits in held),))],
        input_output_aliases={} if begun is None else {count: 0},
        compiler_params=LIMIT,
        name="weight_assemble" if begun is None else "weight_complete",
    )(*arrays)


def hop(value, bits):
    count = lax.axis_size("dp")
    return lax.ppermute(value, "dp", [(i, i ^ bits) for i in range(count)])


def per_device_16x2(tokens, queries, grad_out, w_kv, doc_ids, span_order):
    dp_size = lax.axis_size("dp")
    rows_dev = queries.shape[1]
    swap = [(0, 1), (1, 0)]
    near = (Y, Z1, Y | Z1)
    flat = tokens[0]
    far_own, far_y, far_z, diagonal = slice_tokens(
        flat, [(0, (True,)), (1, (True,)), (2, (True,)), (3, (True, False))], "slice_far"
    )
    far_y, far_z, diagonal = hop(far_y, Y), hop(far_z, Z1), hop(diagonal, Y | Z1)
    partial = project(flat, w_kv)
    other = lax.ppermute(partial, "seq", swap)
    docs = doc_ids.reshape(-1, rows_dev)
    attention, query_grad, terms, done = attend(
        span_order, docs, queries[0], grad_out[0], [partial, other]
    )
    terms = after(terms, [far_y, far_z])
    grad = round_grad(terms, lax.ppermute(terms, "seq", swap), [done])
    grads = [grad] + [hop(grad, bits) for bits in near]
    near_own, near_y, near_z = slice_tokens(
        flat, [(0, (False,)), (1, (False,)), (2, (False,))], "slice_near"
    )
    near_y, near_z = hop(near_y, Y), hop(near_z, Z1)
    keep, send = weight_part([far_own, far_y, far_z, diagonal], grads, dp_size, [0, 0, 0, 0])
    part_a, part_b = fold(keep, hop(send, CORE), [near_y, near_z])
    far_a, far_b = hop(part_a, Z2), hop(part_b, Z2)
    keep, send = weight_part([near_own, near_y, near_z, diagonal], grads, dp_size, [0, 0, 0, 2])
    near_a, near_b = fold(keep, hop(send, CORE))
    own_a, own_b = finish(near_a, far_a), finish(near_b, far_b)
    z2a, z1a, ya = hop(own_a, Z2), hop(own_a, Z1), hop(own_a, Y)
    z2b = hop(own_b, Z2)
    later = after(own_b, [z2a, z1a, ya])
    z1b, yb = hop(later, Z1), hop(later, Y)
    z12a, z12b = hop(z2a, Z1), hop(z2b, Z1)
    zy = hop(stack([z1a, z1b, z2a, z2b], [yb, z12a]), Y)
    z12y = hop(stack([z12a, z12b]), Y)
    first = hop(stack([own_a, own_b, z1a, z1b, z2a, z2b, ya, yb]), CORE)
    last = hop(stack([zy, z12a, z12b, z12y]), CORE)
    whole = lambda *bits: [(bit, half) for bit in bits for half in (0, 1)]
    near_half = [
        (own_a, [(0, 0)]),
        (own_b, [(0, 1)]),
        (z1a, [(Z1, 0)]),
        (z1b, [(Z1, 1)]),
        (z2a, [(Z2, 0)]),
        (z2b, [(Z2, 1)]),
        (ya, [(Y, 0)]),
        (yb, [(Y, 1)]),
    ]
    far_half = [
        (zy, whole(Z1 | Y, Z2 | Y)),
        (z12a, [(Z1 | Z2, 0)]),
        (z12b, [(Z1 | Z2, 1)]),
        (z12y, whole(Z1 | Z2 | Y)),
    ]
    held = [
        [(bits | CORE, half) for _, part in group for bits, half in part]
        for group in (near_half, far_half)
    ]
    pieces = near_half + far_half
    total = 2 * dp_size
    weight_grad = assemble(pieces + [(first, held[0])], total)
    weight_grad = assemble([(last, held[1])], total, weight_grad)
    return (attention[None], query_grad[None], weight_grad)


def per_device(tokens, queries, grad_out, w_kv, doc_ids, span_order):
    dp_size = lax.axis_size("dp")
    rows_dev = queries.shape[1]
    flat = tokens[0]
    spread = lax.all_to_all(flat, "dp", split_axis=1, concat_axis=0, tiled=True)
    partial = jnp.dot(flat, w_kv, preferred_element_type=F32)
    own = lax.psum_scatter(partial, "seq", scatter_dimension=0, tiled=True).astype(BF16)
    kvs = [lax.all_gather(own, "seq", axis=0, tiled=True)]
    docs = doc_ids.reshape(-1, rows_dev)
    attention, query_grad, terms, done = attend(span_order, docs, queries[0], grad_out[0], kvs)
    grad_kv = lax.psum(terms.T, "seq").astype(BF16)
    all_grads = lax.all_gather(grad_kv, "dp", axis=0, tiled=True)
    piece = (_mm(spread, all_grads, TN) * (1.0 / dp_size)).astype(BF16)
    weight_grad = lax.all_gather(piece, "dp", axis=0, tiled=True)
    return (attention[None], query_grad[None], weight_grad)


def solution(mesh):
    small = mesh.shape["dp"] == 16 and mesh.shape["seq"] == 2
    return jax.shard_map(
        per_device_16x2 if small else per_device,
        mesh=mesh,
        in_specs=(
            P("dp", None, "seq"),
            P("dp", "seq", None),
            P("dp", "seq", None),
            P("seq", None),
            P("dp", None),
            P(),
        ),
        out_specs=(P("dp", "seq", None), P("dp", "seq", None), P("seq", None)),
        check_vma=False,
    )
```

```python
import functools
import math

import jax
import jax.numpy as jnp
from jax import lax
from jax.experimental import pallas as pl
from jax.experimental.pallas import tpu as pltpu
from jax.sharding import PartitionSpec as P

HEAD = 128
QH = 8
GROUP = 2
F32 = jnp.float32
BF16 = jnp.bfloat16
NT = (((1,), (1,)), ((), ()))
TN = (((0,), (0,)), ((), ()))
NN = (((1,), (0,)), ((), ()))


def _mm(a, b, dims):
    return lax.dot_general(a, b, dims, preferred_element_type=F32)


ANY = pl.BlockSpec(memory_space=pl.ANY)
VMEM = pl.BlockSpec(memory_space=pltpu.VMEM)
LIMIT = pltpu.CompilerParams(vmem_limit_bytes=48 * 1024 * 1024)


def terms_kernel(parts, own, order_ref, docs_ref, q_ref, g_ref, *refs):
    kv_refs = refs[:parts]
    kv_ref, low_ref, ds_ref, terms_ref = refs[-4:]
    rows = q_ref.shape[0]
    seq_len = kv_refs[0].shape[0]
    spans = seq_len // rows
    if parts == 1:
        kv = kv_refs[0][...]
    else:
        kv = (kv_refs[0][...] + kv_refs[1][...]).astype(BF16)
    kv_ref[...] = kv
    keys = kv[:, :HEAD]
    values = kv[:, HEAD:]
    scale = 1.0 / math.sqrt(HEAD)
    me = lax.axis_index(own)

    def row_docs(span):
        return docs_ref[pl.ds(order_ref[span], 1), :]

    masks = []
    q_docs = row_docs(me)
    q_span = order_ref[me]
    q_pos = lax.broadcasted_iota(jnp.int32, (rows, rows), 1)
    k_pos = lax.broadcasted_iota(jnp.int32, (rows, rows), 0)
    for span in range(spans):
        k_docs = jnp.broadcast_to(row_docs(span), (rows, rows)).T
        gap = (order_ref[span] - q_span) * rows
        masks.append((k_pos + gap <= q_pos) & (k_docs == q_docs))
    allowed = jnp.concatenate(masks, axis=0)
    allowed = jnp.concatenate([allowed] * GROUP, axis=1)

    key_grad = jnp.zeros((seq_len, HEAD), F32)
    value_grad = jnp.zeros((seq_len, HEAD), F32)
    for first in range(0, QH, GROUP):
        heads = range(first, first + GROUP)
        q = jnp.concatenate([q_ref[:, h * HEAD : (h + 1) * HEAD] for h in heads], axis=0)
        g = jnp.concatenate([g_ref[:, h * HEAD : (h + 1) * HEAD] for h in heads], axis=0)
        scores = jnp.where(allowed, _mm(keys, q, NT) * scale, F32(-1e30))
        expo = jnp.exp(scores - jnp.max(scores, axis=0, keepdims=True))
        probs = expo * (1.0 / jnp.sum(expo, axis=0, keepdims=True))
        low = probs.astype(BF16)
        grad_probs = _mm(values, g, NT)
        delta = jnp.sum(probs * grad_probs, axis=0, keepdims=True)
        grad_scores = (probs * (grad_probs - delta) * scale).astype(BF16)
        low_ref[:, first * rows : (first + GROUP) * rows] = low
        ds_ref[:, first * rows : (first + GROUP) * rows] = grad_scores
        key_grad += _mm(grad_scores, q, NN)
        value_grad += _mm(low, g, NN)
    terms_ref[:HEAD, :] = key_grad.T
    terms_ref[HEAD:, :] = value_grad.T


def outputs_kernel(kv_ref, low_ref, ds_ref, att_ref, qg_ref, done_ref):
    rows = att_ref.shape[0]
    done_ref[...] = jnp.zeros_like(done_ref)
    keys_t = kv_ref[:, :HEAD].T
    values_t = kv_ref[:, HEAD:].T
    for first in range(0, QH, GROUP):
        cols = slice(first * rows, (first + GROUP) * rows)
        att = _mm(values_t, low_ref[:, cols], NN)
        qg = _mm(keys_t, ds_ref[:, cols], NN)
        for i in range(GROUP):
            head = slice((first + i) * HEAD, (first + i + 1) * HEAD)
            att_ref[:, head] = att[:, i * rows : (i + 1) * rows].T.astype(BF16)
            qg_ref[:, head] = qg[:, i * rows : (i + 1) * rows].T.astype(BF16)


def attend(order, docs, q, g, kvs):
    seq_len, rows = kvs[0].shape[0], q.shape[0]
    kv, low, grad_scores, terms = pl.pallas_call(
        functools.partial(terms_kernel, len(kvs), "seq"),
        out_shape=(
            jax.ShapeDtypeStruct((seq_len, 2 * HEAD), BF16),
            jax.ShapeDtypeStruct((seq_len, QH * rows), BF16),
            jax.ShapeDtypeStruct((seq_len, QH * rows), BF16),
            jax.ShapeDtypeStruct((2 * HEAD, seq_len), F32),
        ),
        in_specs=[pl.BlockSpec(memory_space=pltpu.SMEM)] + [VMEM] * (3 + len(kvs)),
        out_specs=[VMEM] * 4,
        compiler_params=LIMIT,
        name="attention_terms",
    )(order, docs, q, g, *kvs)
    attention, query_grad, done = pl.pallas_call(
        outputs_kernel,
        out_shape=[jax.ShapeDtypeStruct(q.shape, BF16)] * 2 + [jax.ShapeDtypeStruct((8, HEAD), F32)],
        in_specs=[VMEM] * 3,
        out_specs=[VMEM] * 3,
        compiler_params=LIMIT,
        name="attention_outputs",
    )(kv, low, grad_scores)
    return attention, query_grad, terms, done


CORE, Y, Z1, Z2 = 1, 2, 4, 8
CHUNKS = 4
CORES = 2
BLOCK = 4


def block_of(device):
    return lax.rem(device // CORES, BLOCK)


def half_cols(device, k, core, far_half, width):
    high = device // (CORES * BLOCK)
    high = 1 - high if far_half else high
    return pl.multiple_of((((block_of(device) ^ k) * CORES + core) * 2 + high) * width, width)


def slice_kernel(wanted, tok_ref, *refs):
    slices, sems = refs[-1 - len(wanted) : -1], refs[-1]
    me = lax.axis_index("dp")
    copies = []
    for (k, halves), ref in zip(wanted, slices):
        width = ref.shape[1] // (CORES * len(halves))
        for n, far_half in enumerate(halves):
            for core in range(CORES):
                copy = pltpu.make_async_copy(
                    tok_ref.at[:, pl.ds(half_cols(me, k, core, far_half, width), width)],
                    ref.at[:, pl.ds((n * CORES + core) * width, width)],
                    sems.at[len(copies)],
                )
                copy.start()
                copies.append(copy)
    for copy in copies:
        copy.wait()


def slice_tokens(tokens, wanted, name, after=()):
    rows, features = tokens.shape
    half = features // (2 * BLOCK)
    return pl.pallas_call(
        functools.partial(slice_kernel, wanted),
        out_shape=[jax.ShapeDtypeStruct((rows, half * len(halves)), BF16) for _, halves in wanted],
        in_specs=[ANY] * (1 + len(after)),
        out_specs=[VMEM] * len(wanted),
        scratch_shapes=[pltpu.SemaphoreType.DMA((sum(2 * len(halves) for _, halves in wanted),))],
        compiler_params=pltpu.CompilerParams(vmem_limit_bytes=48 * 1024 * 1024),
        name=name,
    )(tokens, *after)


def project_kernel(tok_ref, w_ref, out_ref, tok_v, w_v, tok_sems, w_sems):
    chunks, width = w_v.shape[0], w_v.shape[1]
    reads = []
    for k in range(chunks):
        cut = pl.ds(k * width, width)
        tok = pltpu.make_async_copy(tok_ref.at[:, cut], tok_v.at[k], tok_sems.at[k])
        w = pltpu.make_async_copy(w_ref.at[cut, :], w_v.at[k], w_sems.at[k])
        tok.start()
        w.start()
        reads.append((tok, w))
    total = None
    for k, (tok, w) in enumerate(reads):
        tok.wait()
        w.wait()
        term = _mm(tok_v[k], w_v[k], NN)
        total = term if total is None else total + term
    out_ref[...] = total


def project(tokens, w_kv):
    rows, features = tokens.shape
    cols = w_kv.shape[1]
    width = features // CHUNKS
    return pl.pallas_call(
        project_kernel,
        out_shape=jax.ShapeDtypeStruct((rows, cols), F32),
        in_specs=[ANY, ANY],
        out_specs=VMEM,
        scratch_shapes=[
            pltpu.VMEM((CHUNKS, rows, width), BF16),
            pltpu.VMEM((CHUNKS, width, cols), BF16),
            pltpu.SemaphoreType.DMA((CHUNKS,)),
            pltpu.SemaphoreType.DMA((CHUNKS,)),
        ],
        compiler_params=pltpu.CompilerParams(vmem_limit_bytes=62 * 1024 * 1024),
        name="project",
    )(tokens, w_kv)


def round_kernel(a_ref, b_ref, *refs):
    refs[-1][...] = (a_ref[...] + b_ref[...]).astype(BF16)


def round_grad(a, b, arrived):
    return pl.pallas_call(
        round_kernel,
        out_shape=jax.ShapeDtypeStruct(a.shape, BF16),
        in_specs=[VMEM, VMEM] + [ANY] * len(arrived),
        out_specs=VMEM,
        compiler_params=LIMIT,
        name="round_grad",
    )(a, b, *arrived)


def weight_kernel(packs, starts, *refs):
    toks, grads = refs[:BLOCK], refs[BLOCK : 2 * BLOCK]
    keep_ref, send_ref = refs[2 * BLOCK :]
    width = keep_ref.shape[1]
    starts = [start * width for start in starts]
    core = lax.rem(lax.axis_index("dp"), CORES)
    for ref, which in ((send_ref, 1 - core), (keep_ref, core)):
        acc = None
        for k in range(BLOCK):
            first = pl.multiple_of(starts[k] + which * width, width)
            term = _mm(grads[k][...], toks[k][:, pl.ds(first, width)], NN)
            acc = term if acc is None else acc + term
        ref[...] = acc * (1.0 / packs)


def weight_part(toks, grads, packs, starts):
    part = jax.ShapeDtypeStruct((grads[0].shape[0], toks[-1].shape[1] // CORES), F32)
    return pl.pallas_call(
        functools.partial(weight_kernel, packs, starts),
        out_shape=[part, part],
        in_specs=[VMEM] * (2 * BLOCK),
        out_specs=[VMEM, VMEM],
        compiler_params=LIMIT,
        name="weight_part",
    )(*toks, *grads)


def fold_kernel(a_ref, b_ref, out_ref):
    out_ref[...] = a_ref[...] + b_ref[...]


def fold(a, b):
    return pl.pallas_call(
        fold_kernel,
        out_shape=jax.ShapeDtypeStruct(a.shape, F32),
        in_specs=[VMEM, VMEM],
        out_specs=VMEM,
        compiler_params=LIMIT,
        name="weight_fold",
    )(a, b)


def finish_kernel(a_ref, b_ref, out_ref):
    out_ref[...] = (a_ref[...] + b_ref[...]).T.astype(BF16)


def finish(a, b):
    return pl.pallas_call(
        finish_kernel,
        out_shape=jax.ShapeDtypeStruct((a.shape[1], a.shape[0]), BF16),
        in_specs=[VMEM] * 2,
        out_specs=VMEM,
        compiler_params=LIMIT,
        name="weight_finish",
    )(a, b)


def stack_kernel(count, *refs):
    out_ref = refs[-1]
    first = 0
    for ref in refs[:count]:
        out_ref[first : first + ref.shape[0], :] = ref[...]
        first += ref.shape[0]


def stack(parts, after=()):
    rows = sum(part.shape[0] for part in parts)
    return pl.pallas_call(
        functools.partial(stack_kernel, len(parts)),
        out_shape=jax.ShapeDtypeStruct((rows, parts[0].shape[1]), BF16),
        in_specs=[VMEM] * len(parts) + [ANY] * len(after),
        out_specs=VMEM,
        compiler_params=LIMIT,
        name="stack",
    )(*parts, *after)


def assemble_kernel(held, rows, *refs):
    arrays, out_ref, sems = refs[: len(held)], refs[-2], refs[-1]
    me = lax.axis_index("dp")
    copies = []
    for array, bits in zip(arrays, held):
        for n, bit in enumerate(bits):
            source = me ^ bit
            high = source // (CORES * BLOCK)
            place = (block_of(source) * CORES + lax.rem(source, CORES)) * 2 + high
            first = pl.multiple_of(place * rows, rows)
            copy = pltpu.make_async_copy(
                array.at[pl.ds(n * rows, rows), :],
                out_ref.at[pl.ds(first, rows), :],
                sems.at[len(copies)],
            )
            copy.start()
            copies.append(copy)
    for copy in copies:
        copy.wait()


def assemble(pieces, total, begun=None):
    arrays = [array for array, _ in pieces]
    held = [bits for _, bits in pieces]
    rows = arrays[0].shape[0] // len(held[0])
    count = len(arrays)
    if begun is not None:
        arrays.append(begun)
    return pl.pallas_call(
        functools.partial(assemble_kernel, held, rows),
        out_shape=jax.ShapeDtypeStruct((total * rows, arrays[0].shape[1]), BF16),
        in_specs=[ANY] * len(arrays),
        out_specs=ANY,
        scratch_shapes=[pltpu.SemaphoreType.DMA((sum(len(bits) for bits in held),))],
        input_output_aliases={} if begun is None else {count: 0},
        compiler_params=LIMIT,
        name="weight_assemble" if begun is None else "weight_complete",
    )(*arrays)


def hop(value, bits):
    count = lax.axis_size("dp")
    return lax.ppermute(value, "dp", [(i, i ^ bits) for i in range(count)])


def per_device_16x2(tokens, queries, grad_out, w_kv, doc_ids, span_order):
    dp_size = lax.axis_size("dp")
    rows_dev = queries.shape[1]
    swap = [(0, 1), (1, 0)]
    near = (Y, Z1, Y | Z1)
    flat = tokens[0]
    both = (True, False)
    own, tok_y, tok_z, far_d = slice_tokens(
        flat, [(0, both), (1, both), (2, both), (3, (True,))], "slice_first"
    )
    tok_y, tok_z, far_d = hop(tok_y, Y), hop(tok_z, Z1), hop(far_d, Y | Z1)
    partial = project(flat, w_kv)
    other = lax.ppermute(partial, "seq", swap)
    docs = doc_ids.reshape(-1, rows_dev)
    attention, query_grad, terms, done = attend(
        span_order, docs, queries[0], grad_out[0], [partial, other]
    )
    grad = round_grad(terms, lax.ppermute(terms, "seq", swap), [done, tok_y, tok_z])
    grads = [grad] + [hop(grad, bits) for bits in near]
    keep, send = weight_part([own, tok_y, tok_z, far_d], grads, dp_size, [0, 0, 0, 0])
    part = fold(keep, hop(send, CORE))
    far = hop(part, Z2)
    (near_d,) = slice_tokens(flat, [(3, (False,))], "slice_near_diagonal")
    near_d = hop(near_d, Y | Z1)
    keep, send = weight_part([own, tok_y, tok_z, near_d], grads, dp_size, [2, 2, 2, 0])
    own = finish(fold(keep, far), hop(send, CORE))
    z1, z2, y = hop(own, Z1), hop(own, Z2), hop(own, Y)
    z12 = hop(z2, Z1)
    zy = hop(stack([z1, z2], [y]), Y)
    z12y = hop(z12, Y)
    first = hop(stack([own, z1, z2, y]), CORE)
    last = hop(stack([zy, z12, z12y]), CORE)
    pieces = [
        (own, [0]),
        (z1, [Z1]),
        (z2, [Z2]),
        (y, [Y]),
        (zy, [Z1 | Y, Z2 | Y]),
        (z12, [Z1 | Z2]),
        (z12y, [Z1 | Z2 | Y]),
    ]
    held = [[bit | CORE for _, bits in part for bit in bits] for part in (pieces[:4], pieces[4:])]
    weight_grad = assemble(pieces + [(first, held[0])], dp_size)
    weight_grad = assemble([(last, held[1])], dp_size, weight_grad)
    return (attention[None], query_grad[None], weight_grad)


def per_device(tokens, queries, grad_out, w_kv, doc_ids, span_order):
    dp_size = lax.axis_size("dp")
    rows_dev = queries.shape[1]
    flat = tokens[0]
    spread = lax.all_to_all(flat, "dp", split_axis=1, concat_axis=0, tiled=True)
    partial = jnp.dot(flat, w_kv, preferred_element_type=F32)
    own = lax.psum_scatter(partial, "seq", scatter_dimension=0, tiled=True).astype(BF16)
    kvs = [lax.all_gather(own, "seq", axis=0, tiled=True)]
    docs = doc_ids.reshape(-1, rows_dev)
    attention, query_grad, terms, done = attend(span_order, docs, queries[0], grad_out[0], kvs)
    grad_kv = lax.psum(terms.T, "seq").astype(BF16)
    all_grads = lax.all_gather(grad_kv, "dp", axis=0, tiled=True)
    piece = (_mm(spread, all_grads, TN) * (1.0 / dp_size)).astype(BF16)
    weight_grad = lax.all_gather(piece, "dp", axis=0, tiled=True)
    return (attention[None], query_grad[None], weight_grad)


def solution(mesh):
    small = mesh.shape["dp"] == 16 and mesh.shape["seq"] == 2
    return jax.shard_map(
        per_device_16x2 if small else per_device,
        mesh=mesh,
        in_specs=(
            P("dp", None, "seq"),
            P("dp", "seq", None),
            P("dp", "seq", None),
            P("seq", None),
            P("dp", None),
            P(),
        ),
        out_specs=(P("dp", "seq", None), P("dp", "seq", None), P("seq", None)),
        check_vma=False,
    )
```

```python
import functools
import math

import jax
import jax.numpy as jnp
from jax import lax
from jax.experimental import pallas as pl
from jax.experimental.pallas import tpu as pltpu
from jax.sharding import PartitionSpec as P

HEAD = 128
QH = 8
GROUP = 2
F32 = jnp.float32
BF16 = jnp.bfloat16
NT = (((1,), (1,)), ((), ()))
TN = (((0,), (0,)), ((), ()))
NN = (((1,), (0,)), ((), ()))


def _mm(a, b, dims):
    return lax.dot_general(a, b, dims, preferred_element_type=F32)


ANY = pl.BlockSpec(memory_space=pl.ANY)
VMEM = pl.BlockSpec(memory_space=pltpu.VMEM)
LIMIT = pltpu.CompilerParams(vmem_limit_bytes=48 * 1024 * 1024)


def terms_kernel(parts, own, order_ref, docs_ref, q_ref, g_ref, *refs):
    kv_refs = refs[:parts]
    kv_ref, low_ref, ds_ref, terms_ref = refs[-4:]
    rows = q_ref.shape[0]
    seq_len = kv_refs[0].shape[0]
    spans = seq_len // rows
    if parts == 1:
        kv = kv_refs[0][...]
    else:
        kv = (kv_refs[0][...] + kv_refs[1][...]).astype(BF16)
    kv_ref[...] = kv
    keys = kv[:, :HEAD]
    values = kv[:, HEAD:]
    scale = 1.0 / math.sqrt(HEAD)
    me = lax.axis_index(own)

    def row_docs(span):
        return docs_ref[pl.ds(order_ref[span], 1), :]

    masks = []
    q_docs = row_docs(me)
    q_span = order_ref[me]
    q_pos = lax.broadcasted_iota(jnp.int32, (rows, rows), 1)
    k_pos = lax.broadcasted_iota(jnp.int32, (rows, rows), 0)
    for span in range(spans):
        k_docs = jnp.broadcast_to(row_docs(span), (rows, rows)).T
        gap = (order_ref[span] - q_span) * rows
        masks.append((k_pos + gap <= q_pos) & (k_docs == q_docs))
    allowed = jnp.concatenate(masks, axis=0)
    allowed = jnp.concatenate([allowed] * GROUP, axis=1)

    key_grad = jnp.zeros((seq_len, HEAD), F32)
    value_grad = jnp.zeros((seq_len, HEAD), F32)
    for first in range(0, QH, GROUP):
        heads = range(first, first + GROUP)
        q = jnp.concatenate([q_ref[:, h * HEAD : (h + 1) * HEAD] for h in heads], axis=0)
        g = jnp.concatenate([g_ref[:, h * HEAD : (h + 1) * HEAD] for h in heads], axis=0)
        scores = jnp.where(allowed, _mm(keys, q, NT) * scale, F32(-1e30))
        expo = jnp.exp(scores - jnp.max(scores, axis=0, keepdims=True))
        probs = expo * (1.0 / jnp.sum(expo, axis=0, keepdims=True))
        low = probs.astype(BF16)
        grad_probs = _mm(values, g, NT)
        delta = jnp.sum(probs * grad_probs, axis=0, keepdims=True)
        grad_scores = (probs * (grad_probs - delta) * scale).astype(BF16)
        low_ref[:, first * rows : (first + GROUP) * rows] = low
        ds_ref[:, first * rows : (first + GROUP) * rows] = grad_scores
        key_grad += _mm(grad_scores, q, NN)
        value_grad += _mm(low, g, NN)
    terms_ref[:HEAD, :] = key_grad.T
    terms_ref[HEAD:, :] = value_grad.T


def outputs_kernel(kv_ref, low_ref, ds_ref, att_ref, qg_ref, done_ref):
    rows = att_ref.shape[0]
    done_ref[...] = jnp.zeros_like(done_ref)
    keys_t = kv_ref[:, :HEAD].T
    values_t = kv_ref[:, HEAD:].T
    for first in range(0, QH, GROUP):
        cols = slice(first * rows, (first + GROUP) * rows)
        att = _mm(values_t, low_ref[:, cols], NN)
        qg = _mm(keys_t, ds_ref[:, cols], NN)
        for i in range(GROUP):
            head = slice((first + i) * HEAD, (first + i + 1) * HEAD)
            att_ref[:, head] = att[:, i * rows : (i + 1) * rows].T.astype(BF16)
            qg_ref[:, head] = qg[:, i * rows : (i + 1) * rows].T.astype(BF16)


def attend(order, docs, q, g, kvs):
    seq_len, rows = kvs[0].shape[0], q.shape[0]
    kv, low, grad_scores, terms = pl.pallas_call(
        functools.partial(terms_kernel, len(kvs), "seq"),
        out_shape=(
            jax.ShapeDtypeStruct((seq_len, 2 * HEAD), BF16),
            jax.ShapeDtypeStruct((seq_len, QH * rows), BF16),
            jax.ShapeDtypeStruct((seq_len, QH * rows), BF16),
            jax.ShapeDtypeStruct((2 * HEAD, seq_len), F32),
        ),
        in_specs=[pl.BlockSpec(memory_space=pltpu.SMEM)] + [VMEM] * (3 + len(kvs)),
        out_specs=[VMEM] * 4,
        compiler_params=LIMIT,
        name="attention_terms",
    )(order, docs, q, g, *kvs)
    attention, query_grad, done = pl.pallas_call(
        outputs_kernel,
        out_shape=[jax.ShapeDtypeStruct(q.shape, BF16)] * 2 + [jax.ShapeDtypeStruct((8, HEAD), F32)],
        in_specs=[VMEM] * 3,
        out_specs=[VMEM] * 3,
        compiler_params=LIMIT,
        name="attention_outputs",
    )(kv, low, grad_scores)
    return attention, query_grad, terms, done


CORE, Y, Z1, Z2 = 1, 2, 4, 8
CORES = 2
BLOCK = 4


def block_of(device):
    return lax.rem(device // CORES, BLOCK)


def half_cols(device, k, core, far_half, width):
    high = device // (CORES * BLOCK)
    high = 1 - high if far_half else high
    return pl.multiple_of((((block_of(device) ^ k) * CORES + core) * 2 + high) * width, width)


def slice_kernel(wanted, tok_ref, *refs):
    slices, sems = refs[-1 - len(wanted) : -1], refs[-1]
    me = lax.axis_index("dp")
    copies = []
    for (k, halves), ref in zip(wanted, slices):
        width = ref.shape[1] // (CORES * len(halves))
        for n, far_half in enumerate(halves):
            for core in range(CORES):
                copy = pltpu.make_async_copy(
                    tok_ref.at[:, pl.ds(half_cols(me, k, core, far_half, width), width)],
                    ref.at[:, pl.ds((n * CORES + core) * width, width)],
                    sems.at[len(copies)],
                )
                copy.start()
                copies.append(copy)
    for copy in copies:
        copy.wait()


def slice_tokens(tokens, wanted, name, after=()):
    rows, features = tokens.shape
    half = features // (2 * BLOCK)
    return pl.pallas_call(
        functools.partial(slice_kernel, wanted),
        out_shape=[jax.ShapeDtypeStruct((rows, half * len(halves)), BF16) for _, halves in wanted],
        in_specs=[ANY] * (1 + len(after)),
        out_specs=[VMEM] * len(wanted),
        scratch_shapes=[pltpu.SemaphoreType.DMA((sum(2 * len(halves) for _, halves in wanted),))],
        compiler_params=LIMIT,
        name=name,
    )(tokens, *after)


def project_kernel(tok_ref, w_ref, out_ref):
    out_ref[...] = _mm(tok_ref[...], w_ref[...], NN)


def project(tokens, w_kv):
    return pl.pallas_call(
        project_kernel,
        out_shape=jax.ShapeDtypeStruct((tokens.shape[0], w_kv.shape[1]), F32),
        in_specs=[VMEM, VMEM],
        out_specs=VMEM,
        compiler_params=LIMIT,
        name="project",
    )(tokens, w_kv)


def round_kernel(a_ref, b_ref, *refs):
    refs[-1][...] = (a_ref[...] + b_ref[...]).astype(BF16)


def round_grad(a, b, arrived):
    return pl.pallas_call(
        round_kernel,
        out_shape=jax.ShapeDtypeStruct(a.shape, BF16),
        in_specs=[VMEM, VMEM] + [ANY] * len(arrived),
        out_specs=VMEM,
        compiler_params=LIMIT,
        name="round_grad",
    )(a, b, *arrived)


def weight_kernel(packs, starts, *refs):
    toks, grads = refs[:BLOCK], refs[BLOCK : 2 * BLOCK]
    keep_ref, send_ref = refs[2 * BLOCK :]
    width = keep_ref.shape[1]
    starts = [start * width for start in starts]
    core = lax.rem(lax.axis_index("dp"), CORES)
    for ref, which in ((send_ref, 1 - core), (keep_ref, core)):
        acc = None
        for k in range(BLOCK):
            first = pl.multiple_of(starts[k] + which * width, width)
            term = _mm(grads[k][...], toks[k][:, pl.ds(first, width)], NN)
            acc = term if acc is None else acc + term
        ref[...] = acc * (1.0 / packs)


def weight_part(toks, grads, packs, starts):
    part = jax.ShapeDtypeStruct((grads[0].shape[0], toks[-1].shape[1] // CORES), F32)
    return pl.pallas_call(
        functools.partial(weight_kernel, packs, starts),
        out_shape=[part, part],
        in_specs=[VMEM] * (2 * BLOCK),
        out_specs=[VMEM, VMEM],
        compiler_params=LIMIT,
        name="weight_part",
    )(*toks, *grads)


def fold_kernel(a_ref, b_ref, out_ref):
    out_ref[...] = a_ref[...] + b_ref[...]


def fold(a, b):
    return pl.pallas_call(
        fold_kernel,
        out_shape=jax.ShapeDtypeStruct(a.shape, F32),
        in_specs=[VMEM, VMEM],
        out_specs=VMEM,
        compiler_params=LIMIT,
        name="weight_fold",
    )(a, b)


def finish_kernel(a_ref, b_ref, out_ref):
    out_ref[...] = (a_ref[...] + b_ref[...]).T.astype(BF16)


def finish(a, b):
    return pl.pallas_call(
        finish_kernel,
        out_shape=jax.ShapeDtypeStruct((a.shape[1], a.shape[0]), BF16),
        in_specs=[VMEM] * 2,
        out_specs=VMEM,
        compiler_params=LIMIT,
        name="weight_finish",
    )(a, b)


def stack_kernel(count, *refs):
    out_ref = refs[-1]
    first = 0
    for ref in refs[:count]:
        out_ref[first : first + ref.shape[0], :] = ref[...]
        first += ref.shape[0]


def stack(parts, after=()):
    rows = sum(part.shape[0] for part in parts)
    return pl.pallas_call(
        functools.partial(stack_kernel, len(parts)),
        out_shape=jax.ShapeDtypeStruct((rows, parts[0].shape[1]), BF16),
        in_specs=[VMEM] * len(parts) + [ANY] * len(after),
        out_specs=VMEM,
        compiler_params=LIMIT,
        name="stack",
    )(*parts, *after)


def assemble_kernel(held, rows, *refs):
    arrays, out_ref, sems = refs[: len(held)], refs[-2], refs[-1]
    me = lax.axis_index("dp")
    copies = []
    for array, bits in zip(arrays, held):
        for n, bit in enumerate(bits):
            source = me ^ bit
            high = source // (CORES * BLOCK)
            place = (block_of(source) * CORES + lax.rem(source, CORES)) * 2 + high
            first = pl.multiple_of(place * rows, rows)
            copy = pltpu.make_async_copy(
                array.at[pl.ds(n * rows, rows), :],
                out_ref.at[pl.ds(first, rows), :],
                sems.at[len(copies)],
            )
            copy.start()
            copies.append(copy)
    for copy in copies:
        copy.wait()


def assemble(pieces, total, begun=None):
    arrays = [array for array, _ in pieces]
    held = [bits for _, bits in pieces]
    rows = arrays[0].shape[0] // len(held[0])
    count = len(arrays)
    if begun is not None:
        arrays.append(begun)
    return pl.pallas_call(
        functools.partial(assemble_kernel, held, rows),
        out_shape=jax.ShapeDtypeStruct((total * rows, arrays[0].shape[1]), BF16),
        in_specs=[ANY] * len(arrays),
        out_specs=ANY,
        scratch_shapes=[pltpu.SemaphoreType.DMA((sum(len(bits) for bits in held),))],
        input_output_aliases={} if begun is None else {count: 0},
        compiler_params=LIMIT,
        name="weight_assemble" if begun is None else "weight_complete",
    )(*arrays)


def hop(value, bits):
    count = lax.axis_size("dp")
    return lax.ppermute(value, "dp", [(i, i ^ bits) for i in range(count)])


def per_device_16x2(tokens, queries, grad_out, w_kv, doc_ids, span_order):
    dp_size = lax.axis_size("dp")
    rows_dev = queries.shape[1]
    swap = [(0, 1), (1, 0)]
    near = (Y, Z1, Y | Z1)
    flat = tokens[0]
    both = (True, False)
    own, tok_y, tok_z, far_d = slice_tokens(
        flat, [(0, both), (1, both), (2, both), (3, (True,))], "slice_first"
    )
    tok_y, tok_z, far_d = hop(tok_y, Y), hop(tok_z, Z1), hop(far_d, Y | Z1)
    partial = project(flat, w_kv)
    other = lax.ppermute(partial, "seq", swap)
    docs = doc_ids.reshape(-1, rows_dev)
    attention, query_grad, terms, done = attend(
        span_order, docs, queries[0], grad_out[0], [partial, other]
    )
    grad = round_grad(terms, lax.ppermute(terms, "seq", swap), [done, tok_y, tok_z])
    grads = [grad] + [hop(grad, bits) for bits in near]
    keep, send = weight_part([own, tok_y, tok_z, far_d], grads, dp_size, [0, 0, 0, 0])
    part = fold(keep, hop(send, CORE))
    far = hop(part, Z2)
    (near_d,) = slice_tokens(flat, [(3, (False,))], "slice_near_diagonal")
    near_d = hop(near_d, Y | Z1)
    keep, send = weight_part([own, tok_y, tok_z, near_d], grads, dp_size, [2, 2, 2, 0])
    own = finish(fold(keep, far), hop(send, CORE))
    z1, y, d, z2 = hop(own, Z1), hop(own, Y), hop(own, Y | Z1), hop(own, Z2)
    z21, z2y, z2d = hop(z2, Z1), hop(z2, Y), hop(z2, Y | Z1)
    first = hop(stack([own, z1, y, d]), CORE)
    last = hop(stack([z2, z21, z2y, z2d]), CORE)
    pieces = [
        (own, [0]),
        (z1, [Z1]),
        (y, [Y]),
        (d, [Y | Z1]),
        (z2, [Z2]),
        (z21, [Z2 | Z1]),
        (z2y, [Z2 | Y]),
        (z2d, [Z2 | Y | Z1]),
    ]
    held = [[bit | CORE for _, bits in part for bit in bits] for part in (pieces[:4], pieces[4:])]
    weight_grad = assemble(pieces + [(first, held[0])], dp_size)
    weight_grad = assemble([(last, held[1])], dp_size, weight_grad)
    return (attention[None], query_grad[None], weight_grad)


def per_device(tokens, queries, grad_out, w_kv, doc_ids, span_order):
    dp_size = lax.axis_size("dp")
    rows_dev = queries.shape[1]
    flat = tokens[0]
    spread = lax.all_to_all(flat, "dp", split_axis=1, concat_axis=0, tiled=True)
    partial = jnp.dot(flat, w_kv, preferred_element_type=F32)
    own = lax.psum_scatter(partial, "seq", scatter_dimension=0, tiled=True).astype(BF16)
    kvs = [lax.all_gather(own, "seq", axis=0, tiled=True)]
    docs = doc_ids.reshape(-1, rows_dev)
    attention, query_grad, terms, done = attend(span_order, docs, queries[0], grad_out[0], kvs)
    grad_kv = lax.psum(terms.T, "seq").astype(BF16)
    all_grads = lax.all_gather(grad_kv, "dp", axis=0, tiled=True)
    piece = (_mm(spread, all_grads, TN) * (1.0 / dp_size)).astype(BF16)
    weight_grad = lax.all_gather(piece, "dp", axis=0, tiled=True)
    return (attention[None], query_grad[None], weight_grad)


def solution(mesh):
    small = mesh.shape["dp"] == 16 and mesh.shape["seq"] == 2
    return jax.shard_map(
        per_device_16x2 if small else per_device,
        mesh=mesh,
        in_specs=(
            P("dp", None, "seq"),
            P("dp", "seq", None),
            P("dp", "seq", None),
            P("seq", None),
            P("dp", None),
            P(),
        ),
        out_specs=(P("dp", "seq", None), P("dp", "seq", None), P("seq", None)),
        check_vma=False,
    )
```

```python
import functools
import math

import jax
import jax.numpy as jnp
from jax import lax
from jax.experimental import pallas as pl
from jax.experimental.pallas import tpu as pltpu
from jax.sharding import PartitionSpec as P

HEAD = 128
QH = 8
GROUP = 2
F32 = jnp.float32
BF16 = jnp.bfloat16
NT = (((1,), (1,)), ((), ()))
TN = (((0,), (0,)), ((), ()))
NN = (((1,), (0,)), ((), ()))


def _mm(a, b, dims):
    return lax.dot_general(a, b, dims, preferred_element_type=F32)


ANY = pl.BlockSpec(memory_space=pl.ANY)
VMEM = pl.BlockSpec(memory_space=pltpu.VMEM)
LIMIT = pltpu.CompilerParams(vmem_limit_bytes=48 * 1024 * 1024)


def terms_kernel(parts, own, order_ref, docs_ref, q_ref, g_ref, *refs):
    kv_refs = refs[:parts]
    kv_ref, low_ref, ds_ref, terms_ref = refs[-4:]
    rows = q_ref.shape[0]
    seq_len = kv_refs[0].shape[0]
    spans = seq_len // rows
    if parts == 1:
        kv = kv_refs[0][...]
    else:
        kv = (kv_refs[0][...] + kv_refs[1][...]).astype(BF16)
    kv_ref[...] = kv
    keys = kv[:, :HEAD]
    values = kv[:, HEAD:]
    scale = 1.0 / math.sqrt(HEAD)
    me = lax.axis_index(own)

    def row_docs(span):
        return docs_ref[pl.ds(order_ref[span], 1), :]

    masks = []
    q_docs = row_docs(me)
    q_span = order_ref[me]
    q_pos = lax.broadcasted_iota(jnp.int32, (rows, rows), 1)
    k_pos = lax.broadcasted_iota(jnp.int32, (rows, rows), 0)
    for span in range(spans):
        k_docs = jnp.broadcast_to(row_docs(span), (rows, rows)).T
        gap = (order_ref[span] - q_span) * rows
        masks.append((k_pos + gap <= q_pos) & (k_docs == q_docs))
    allowed = jnp.concatenate(masks, axis=0)
    allowed = jnp.concatenate([allowed] * GROUP, axis=1)

    key_grad = jnp.zeros((seq_len, HEAD), F32)
    value_grad = jnp.zeros((seq_len, HEAD), F32)
    for first in range(0, QH, GROUP):
        heads = range(first, first + GROUP)
        q = jnp.concatenate([q_ref[:, h * HEAD : (h + 1) * HEAD] for h in heads], axis=0)
        g = jnp.concatenate([g_ref[:, h * HEAD : (h + 1) * HEAD] for h in heads], axis=0)
        scores = jnp.where(allowed, _mm(keys, q, NT) * scale, F32(-1e30))
        expo = jnp.exp(scores - jnp.max(scores, axis=0, keepdims=True))
        probs = expo * (1.0 / jnp.sum(expo, axis=0, keepdims=True))
        low = probs.astype(BF16)
        grad_probs = _mm(values, g, NT)
        delta = jnp.sum(probs * grad_probs, axis=0, keepdims=True)
        grad_scores = (probs * (grad_probs - delta) * scale).astype(BF16)
        low_ref[:, first * rows : (first + GROUP) * rows] = low
        ds_ref[:, first * rows : (first + GROUP) * rows] = grad_scores
        key_grad += _mm(grad_scores, q, NN)
        value_grad += _mm(low, g, NN)
    terms_ref[:HEAD, :] = key_grad.T
    terms_ref[HEAD:, :] = value_grad.T


def outputs_kernel(kv_ref, low_ref, ds_ref, att_ref, qg_ref, done_ref):
    rows = att_ref.shape[0]
    done_ref[...] = jnp.zeros_like(done_ref)
    keys_t = kv_ref[:, :HEAD].T
    values_t = kv_ref[:, HEAD:].T
    for first in range(0, QH, GROUP):
        cols = slice(first * rows, (first + GROUP) * rows)
        att = _mm(values_t, low_ref[:, cols], NN)
        qg = _mm(keys_t, ds_ref[:, cols], NN)
        for i in range(GROUP):
            head = slice((first + i) * HEAD, (first + i + 1) * HEAD)
            att_ref[:, head] = att[:, i * rows : (i + 1) * rows].T.astype(BF16)
            qg_ref[:, head] = qg[:, i * rows : (i + 1) * rows].T.astype(BF16)


def attend(order, docs, q, g, kvs):
    seq_len, rows = kvs[0].shape[0], q.shape[0]
    kv, low, grad_scores, terms = pl.pallas_call(
        functools.partial(terms_kernel, len(kvs), "seq"),
        out_shape=(
            jax.ShapeDtypeStruct((seq_len, 2 * HEAD), BF16),
            jax.ShapeDtypeStruct((seq_len, QH * rows), BF16),
            jax.ShapeDtypeStruct((seq_len, QH * rows), BF16),
            jax.ShapeDtypeStruct((2 * HEAD, seq_len), F32),
        ),
        in_specs=[pl.BlockSpec(memory_space=pltpu.SMEM)] + [VMEM] * (3 + len(kvs)),
        out_specs=[VMEM] * 4,
        compiler_params=LIMIT,
        name="attention_terms",
    )(order, docs, q, g, *kvs)
    attention, query_grad, done = pl.pallas_call(
        outputs_kernel,
        out_shape=[jax.ShapeDtypeStruct(q.shape, BF16)] * 2 + [jax.ShapeDtypeStruct((8, HEAD), F32)],
        in_specs=[VMEM] * 3,
        out_specs=[VMEM] * 3,
        compiler_params=LIMIT,
        name="attention_outputs",
    )(kv, low, grad_scores)
    return attention, query_grad, terms, done


CORE, Y, Z1, Z2 = 1, 2, 4, 8
CORES = 2
BLOCK = 4


def block_of(device):
    return lax.rem(device // CORES, BLOCK)


def half_cols(device, k, core, far_half, width):
    high = device // (CORES * BLOCK)
    high = 1 - high if far_half else high
    return pl.multiple_of((((block_of(device) ^ k) * CORES + core) * 2 + high) * width, width)


def slice_kernel(wanted, tok_ref, *refs):
    slices, sems = refs[-1 - len(wanted) : -1], refs[-1]
    me = lax.axis_index("dp")
    copies = []
    for (k, halves), ref in zip(wanted, slices):
        width = ref.shape[1] // (CORES * len(halves))
        for n, far_half in enumerate(halves):
            for core in range(CORES):
                copy = pltpu.make_async_copy(
                    tok_ref.at[:, pl.ds(half_cols(me, k, core, far_half, width), width)],
                    ref.at[:, pl.ds((n * CORES + core) * width, width)],
                    sems.at[len(copies)],
                )
                copy.start()
                copies.append(copy)
    for copy in copies:
        copy.wait()


def slice_tokens(tokens, wanted, name, after=()):
    rows, features = tokens.shape
    half = features // (2 * BLOCK)
    return pl.pallas_call(
        functools.partial(slice_kernel, wanted),
        out_shape=[jax.ShapeDtypeStruct((rows, half * len(halves)), BF16) for _, halves in wanted],
        in_specs=[ANY] * (1 + len(after)),
        out_specs=[VMEM] * len(wanted),
        scratch_shapes=[pltpu.SemaphoreType.DMA((sum(2 * len(halves) for _, halves in wanted),))],
        compiler_params=LIMIT,
        name=name,
    )(tokens, *after)


def project_kernel(tok_ref, w_ref, out_ref):
    out_ref[...] = _mm(tok_ref[...], w_ref[...], NN)


def project(tokens, w_kv):
    return pl.pallas_call(
        project_kernel,
        out_shape=jax.ShapeDtypeStruct((tokens.shape[0], w_kv.shape[1]), F32),
        in_specs=[VMEM, VMEM],
        out_specs=VMEM,
        compiler_params=LIMIT,
        name="project",
    )(tokens, w_kv)


def round_kernel(a_ref, b_ref, *refs):
    refs[-1][...] = (a_ref[...] + b_ref[...]).astype(BF16)


def round_grad(a, b, arrived):
    return pl.pallas_call(
        round_kernel,
        out_shape=jax.ShapeDtypeStruct(a.shape, BF16),
        in_specs=[VMEM, VMEM] + [ANY] * len(arrived),
        out_specs=VMEM,
        compiler_params=LIMIT,
        name="round_grad",
    )(a, b, *arrived)


def weight_kernel(packs, starts, *refs):
    toks, grads_ref, (keep_ref, send_ref) = refs[:BLOCK], refs[BLOCK], refs[BLOCK + 1 :]
    rows = grads_ref.shape[0] // BLOCK
    mine = block_of(lax.axis_index("dp"))
    grads = []
    for k in range(BLOCK):
        grads.append(grads_ref[pl.ds(pl.multiple_of((mine ^ k) * rows, rows), rows), :])
    width = keep_ref.shape[1]
    starts = [start * width for start in starts]
    core = lax.rem(lax.axis_index("dp"), CORES)
    for ref, which in ((send_ref, 1 - core), (keep_ref, core)):
        acc = None
        for k in range(BLOCK):
            first = pl.multiple_of(starts[k] + which * width, width)
            term = _mm(grads[k], toks[k][:, pl.ds(first, width)], NN)
            acc = term if acc is None else acc + term
        ref[...] = acc * (1.0 / packs)


def weight_part(toks, grads, packs, starts):
    part = jax.ShapeDtypeStruct((grads.shape[1], toks[-1].shape[1] // CORES), F32)
    return pl.pallas_call(
        functools.partial(weight_kernel, packs, starts),
        out_shape=[part, part],
        in_specs=[VMEM] * (BLOCK + 1),
        out_specs=[VMEM, VMEM],
        compiler_params=LIMIT,
        name="weight_part",
    )(*toks, grads)


def fold_kernel(a_ref, b_ref, out_ref):
    out_ref[...] = a_ref[...] + b_ref[...]


def fold(a, b):
    return pl.pallas_call(
        fold_kernel,
        out_shape=jax.ShapeDtypeStruct(a.shape, F32),
        in_specs=[VMEM, VMEM],
        out_specs=VMEM,
        compiler_params=LIMIT,
        name="weight_fold",
    )(a, b)


def finish_kernel(a_ref, b_ref, out_ref):
    out_ref[...] = (a_ref[...] + b_ref[...]).T.astype(BF16)


def finish(a, b):
    return pl.pallas_call(
        finish_kernel,
        out_shape=jax.ShapeDtypeStruct((a.shape[1], a.shape[0]), BF16),
        in_specs=[VMEM] * 2,
        out_specs=VMEM,
        compiler_params=LIMIT,
        name="weight_finish",
    )(a, b)


def stack_kernel(count, *refs):
    out_ref = refs[-1]
    first = 0
    for ref in refs[:count]:
        out_ref[first : first + ref.shape[0], :] = ref[...]
        first += ref.shape[0]


def stack(parts, after=()):
    rows = sum(part.shape[0] for part in parts)
    return pl.pallas_call(
        functools.partial(stack_kernel, len(parts)),
        out_shape=jax.ShapeDtypeStruct((rows, parts[0].shape[1]), BF16),
        in_specs=[VMEM] * len(parts) + [ANY] * len(after),
        out_specs=VMEM,
        compiler_params=LIMIT,
        name="stack",
    )(*parts, *after)


def assemble_kernel(held, rows, *refs):
    arrays, out_ref, sems = refs[: len(held)], refs[-2], refs[-1]
    me = lax.axis_index("dp")
    copies = []
    for array, bits in zip(arrays, held):
        for n, bit in enumerate(bits):
            source = me ^ bit
            high = source // (CORES * BLOCK)
            place = (block_of(source) * CORES + lax.rem(source, CORES)) * 2 + high
            first = pl.multiple_of(place * rows, rows)
            copy = pltpu.make_async_copy(
                array.at[pl.ds(n * rows, rows), :],
                out_ref.at[pl.ds(first, rows), :],
                sems.at[len(copies)],
            )
            copy.start()
            copies.append(copy)
    for copy in copies:
        copy.wait()


def assemble(pieces, total, begun=None):
    arrays = [array for array, _ in pieces]
    held = [bits for _, bits in pieces]
    rows = arrays[0].shape[0] // len(held[0])
    count = len(arrays)
    if begun is not None:
        arrays.append(begun)
    return pl.pallas_call(
        functools.partial(assemble_kernel, held, rows),
        out_shape=jax.ShapeDtypeStruct((total * rows, arrays[0].shape[1]), BF16),
        in_specs=[ANY] * len(arrays),
        out_specs=ANY,
        scratch_shapes=[pltpu.SemaphoreType.DMA((sum(len(bits) for bits in held),))],
        input_output_aliases={} if begun is None else {count: 0},
        compiler_params=LIMIT,
        name="weight_assemble" if begun is None else "weight_complete",
    )(*arrays)


def hop(value, bits):
    count = lax.axis_size("dp")
    return lax.ppermute(value, "dp", [(i, i ^ bits) for i in range(count)])


def copies_kernel(in_ref, out_ref):
    rows = in_ref.shape[0]
    for k in range(BLOCK):
        out_ref[k * rows : (k + 1) * rows, :] = in_ref[...]


def spread(value):
    copies = pl.pallas_call(
        copies_kernel,
        out_shape=jax.ShapeDtypeStruct((BLOCK * value.shape[0], value.shape[1]), value.dtype),
        in_specs=[VMEM],
        out_specs=VMEM,
        compiler_params=LIMIT,
        name="copies",
    )(value)
    count = lax.axis_size("dp")
    groups = [
        [high + block * CORES + core for block in range(BLOCK)]
        for high in range(0, count, CORES * BLOCK)
        for core in range(CORES)
    ]
    return lax.all_to_all(
        copies, "dp", split_axis=0, concat_axis=0, axis_index_groups=groups, tiled=True
    )


def per_device_16x2(tokens, queries, grad_out, w_kv, doc_ids, span_order):
    dp_size = lax.axis_size("dp")
    rows_dev = queries.shape[1]
    swap = [(0, 1), (1, 0)]
    near = (Y, Z1, Y | Z1)
    flat = tokens[0]
    both = (True, False)
    own, tok_y, tok_z, far_d = slice_tokens(
        flat, [(0, both), (1, both), (2, both), (3, (True,))], "slice_first"
    )
    tok_y, tok_z, far_d = hop(tok_y, Y), hop(tok_z, Z1), hop(far_d, Y | Z1)
    partial = project(flat, w_kv)
    other = lax.ppermute(partial, "seq", swap)
    docs = doc_ids.reshape(-1, rows_dev)
    attention, query_grad, terms, done = attend(
        span_order, docs, queries[0], grad_out[0], [partial, other]
    )
    grad = round_grad(terms, lax.ppermute(terms, "seq", swap), [done, tok_y, tok_z])
    grads = spread(grad)
    keep, send = weight_part([own, tok_y, tok_z, far_d], grads, dp_size, [0, 0, 0, 0])
    part = fold(keep, hop(send, CORE))
    far = hop(part, Z2)
    (near_d,) = slice_tokens(flat, [(3, (False,))], "slice_near_diagonal")
    near_d = hop(near_d, Y | Z1)
    keep, send = weight_part([own, tok_y, tok_z, near_d], grads, dp_size, [2, 2, 2, 0])
    own = finish(fold(keep, far), hop(send, CORE))
    z1, y, d, z2 = hop(own, Z1), hop(own, Y), hop(own, Y | Z1), hop(own, Z2)
    z21, z2y, z2d = hop(z2, Z1), hop(z2, Y), hop(z2, Y | Z1)
    first = hop(stack([own, z1, y, d]), CORE)
    last = hop(stack([z2, z21, z2y, z2d]), CORE)
    pieces = [
        (own, [0]),
        (z1, [Z1]),
        (y, [Y]),
        (d, [Y | Z1]),
        (z2, [Z2]),
        (z21, [Z2 | Z1]),
        (z2y, [Z2 | Y]),
        (z2d, [Z2 | Y | Z1]),
    ]
    held = [[bit | CORE for _, bits in part for bit in bits] for part in (pieces[:4], pieces[4:])]
    weight_grad = assemble(pieces + [(first, held[0])], dp_size)
    weight_grad = assemble([(last, held[1])], dp_size, weight_grad)
    return (attention[None], query_grad[None], weight_grad)


def per_device(tokens, queries, grad_out, w_kv, doc_ids, span_order):
    dp_size = lax.axis_size("dp")
    rows_dev = queries.shape[1]
    flat = tokens[0]
    spread = lax.all_to_all(flat, "dp", split_axis=1, concat_axis=0, tiled=True)
    partial = jnp.dot(flat, w_kv, preferred_element_type=F32)
    own = lax.psum_scatter(partial, "seq", scatter_dimension=0, tiled=True).astype(BF16)
    kvs = [lax.all_gather(own, "seq", axis=0, tiled=True)]
    docs = doc_ids.reshape(-1, rows_dev)
    attention, query_grad, terms, done = attend(span_order, docs, queries[0], grad_out[0], kvs)
    grad_kv = lax.psum(terms.T, "seq").astype(BF16)
    all_grads = lax.all_gather(grad_kv, "dp", axis=0, tiled=True)
    piece = (_mm(spread, all_grads, TN) * (1.0 / dp_size)).astype(BF16)
    weight_grad = lax.all_gather(piece, "dp", axis=0, tiled=True)
    return (attention[None], query_grad[None], weight_grad)


def solution(mesh):
    small = mesh.shape["dp"] == 16 and mesh.shape["seq"] == 2
    return jax.shard_map(
        per_device_16x2 if small else per_device,
        mesh=mesh,
        in_specs=(
            P("dp", None, "seq"),
            P("dp", "seq", None),
            P("dp", "seq", None),
            P("seq", None),
            P("dp", None),
            P(),
        ),
        out_specs=(P("dp", "seq", None), P("dp", "seq", None), P("seq", None)),
        check_vma=False,
    )
```

```python
import functools
import math

import jax
import jax.numpy as jnp
from jax import lax
from jax.experimental import pallas as pl
from jax.experimental.pallas import tpu as pltpu
from jax.sharding import PartitionSpec as P

HEAD = 128
LOG2E = math.log2(math.e)
QH = 8
GROUP = 4
F32 = jnp.float32
BF16 = jnp.bfloat16
NT = (((1,), (1,)), ((), ()))
TN = (((0,), (0,)), ((), ()))
NN = (((1,), (0,)), ((), ()))


def _mm(a, b, dims):
    return lax.dot_general(a, b, dims, preferred_element_type=F32)


ANY = pl.BlockSpec(memory_space=pl.ANY)
VMEM = pl.BlockSpec(memory_space=pltpu.VMEM)
LIMIT = pltpu.CompilerParams(vmem_limit_bytes=48 * 1024 * 1024)


def terms_kernel(parts, own, order_ref, docs_ref, q_ref, g_ref, *refs):
    kv_refs = refs[:parts]
    kv_ref, low_ref, ds_ref, terms_ref = refs[-4:]
    rows = q_ref.shape[0]
    seq_len = kv_refs[0].shape[0]
    spans = seq_len // rows
    if parts == 1:
        kv = kv_refs[0][...]
    else:
        kv = (kv_refs[0][...] + kv_refs[1][...]).astype(BF16)
    kv_ref[...] = kv
    keys = kv[:, :HEAD]
    values = kv[:, HEAD:]
    scale = 1.0 / math.sqrt(HEAD)
    me = lax.axis_index(own)

    def row_docs(span):
        return docs_ref[pl.ds(order_ref[span], 1), :]

    masks = []
    q_docs = row_docs(me)
    q_span = order_ref[me]
    q_pos = lax.broadcasted_iota(jnp.int32, (rows, rows), 1)
    k_pos = lax.broadcasted_iota(jnp.int32, (rows, rows), 0)
    for span in range(spans):
        k_docs = jnp.broadcast_to(row_docs(span), (rows, rows)).T
        gap = (order_ref[span] - q_span) * rows
        masks.append((k_pos + gap <= q_pos) & (k_docs == q_docs))
    allowed = jnp.concatenate(masks, axis=0)
    allowed = jnp.concatenate([allowed] * GROUP, axis=1)

    key_grad = jnp.zeros((seq_len, HEAD), F32)
    value_grad = jnp.zeros((seq_len, HEAD), F32)
    for first in range(0, QH, GROUP):
        heads = range(first, first + GROUP)
        q = jnp.concatenate([q_ref[:, h * HEAD : (h + 1) * HEAD] for h in heads], axis=0)
        g = jnp.concatenate([g_ref[:, h * HEAD : (h + 1) * HEAD] for h in heads], axis=0)
        scores = jnp.where(allowed, _mm(keys, q, NT), F32(-1e30))
        expo = jnp.exp2((scores - jnp.max(scores, axis=0, keepdims=True)) * (scale * LOG2E))
        probs = expo * (1.0 / jnp.sum(expo, axis=0, keepdims=True))
        low = probs.astype(BF16)
        grad_probs = _mm(values, g, NT)
        delta = jnp.sum(probs * grad_probs, axis=0, keepdims=True)
        grad_scores = (probs * (grad_probs - delta) * scale).astype(BF16)
        low_ref[:, first * rows : (first + GROUP) * rows] = low
        ds_ref[:, first * rows : (first + GROUP) * rows] = grad_scores
        key_grad += _mm(grad_scores, q, NN)
        value_grad += _mm(low, g, NN)
    terms_ref[:HEAD, :] = key_grad.T
    terms_ref[HEAD:, :] = value_grad.T


def outputs_kernel(kv_ref, low_ref, ds_ref, att_ref, qg_ref, done_ref):
    rows = att_ref.shape[0]
    done_ref[...] = jnp.zeros_like(done_ref)
    keys_t = kv_ref[:, :HEAD].T
    values_t = kv_ref[:, HEAD:].T
    for first in range(0, QH, GROUP):
        cols = slice(first * rows, (first + GROUP) * rows)
        att = _mm(values_t, low_ref[:, cols], NN)
        qg = _mm(keys_t, ds_ref[:, cols], NN)
        for i in range(GROUP):
            head = slice((first + i) * HEAD, (first + i + 1) * HEAD)
            att_ref[:, head] = att[:, i * rows : (i + 1) * rows].T.astype(BF16)
            qg_ref[:, head] = qg[:, i * rows : (i + 1) * rows].T.astype(BF16)


def attend(order, docs, q, g, kvs):
    seq_len, rows = kvs[0].shape[0], q.shape[0]
    kv, low, grad_scores, terms = pl.pallas_call(
        functools.partial(terms_kernel, len(kvs), "seq"),
        out_shape=(
            jax.ShapeDtypeStruct((seq_len, 2 * HEAD), BF16),
            jax.ShapeDtypeStruct((seq_len, QH * rows), BF16),
            jax.ShapeDtypeStruct((seq_len, QH * rows), BF16),
            jax.ShapeDtypeStruct((2 * HEAD, seq_len), F32),
        ),
        in_specs=[pl.BlockSpec(memory_space=pltpu.SMEM)] + [VMEM] * (3 + len(kvs)),
        out_specs=[VMEM] * 4,
        compiler_params=LIMIT,
        name="attention_terms",
    )(order, docs, q, g, *kvs)
    attention, query_grad, done = pl.pallas_call(
        outputs_kernel,
        out_shape=[jax.ShapeDtypeStruct(q.shape, BF16)] * 2 + [jax.ShapeDtypeStruct((8, HEAD), F32)],
        in_specs=[VMEM] * 3,
        out_specs=[VMEM] * 3,
        compiler_params=LIMIT,
        name="attention_outputs",
    )(kv, low, grad_scores)
    return attention, query_grad, terms, done


CORE, Y, Z1, Z2 = 1, 2, 4, 8
CORES = 2
BLOCK = 4


def block_of(device):
    return lax.rem(device // CORES, BLOCK)


def half_cols(device, k, core, far_half, width):
    high = device // (CORES * BLOCK)
    high = 1 - high if far_half else high
    return pl.multiple_of((((block_of(device) ^ k) * CORES + core) * 2 + high) * width, width)


def slice_kernel(wanted, tok_ref, *refs):
    slices, sems = refs[-1 - len(wanted) : -1], refs[-1]
    me = lax.axis_index("dp")
    copies = []
    for (k, halves), ref in zip(wanted, slices):
        width = ref.shape[1] // (CORES * len(halves))
        for n, far_half in enumerate(halves):
            for core in range(CORES):
                copy = pltpu.make_async_copy(
                    tok_ref.at[:, pl.ds(half_cols(me, k, core, far_half, width), width)],
                    ref.at[:, pl.ds((n * CORES + core) * width, width)],
                    sems.at[len(copies)],
                )
                copy.start()
                copies.append(copy)
    for copy in copies:
        copy.wait()


def slice_tokens(tokens, wanted, name, after=()):
    rows, features = tokens.shape
    half = features // (2 * BLOCK)
    return pl.pallas_call(
        functools.partial(slice_kernel, wanted),
        out_shape=[jax.ShapeDtypeStruct((rows, half * len(halves)), BF16) for _, halves in wanted],
        in_specs=[ANY] * (1 + len(after)),
        out_specs=[VMEM] * len(wanted),
        scratch_shapes=[pltpu.SemaphoreType.DMA((sum(2 * len(halves) for _, halves in wanted),))],
        compiler_params=LIMIT,
        name=name,
    )(tokens, *after)


def project_kernel(tok_ref, w_ref, out_ref):
    out_ref[...] = _mm(tok_ref[...], w_ref[...], NN)


def project(tokens, w_kv):
    return pl.pallas_call(
        project_kernel,
        out_shape=jax.ShapeDtypeStruct((tokens.shape[0], w_kv.shape[1]), F32),
        in_specs=[VMEM, VMEM],
        out_specs=VMEM,
        compiler_params=LIMIT,
        name="project",
    )(tokens, w_kv)


def round_kernel(a_ref, b_ref, *refs):
    refs[-1][...] = (a_ref[...] + b_ref[...]).astype(BF16)


def round_grad(a, b, arrived):
    return pl.pallas_call(
        round_kernel,
        out_shape=jax.ShapeDtypeStruct(a.shape, BF16),
        in_specs=[VMEM, VMEM] + [ANY] * len(arrived),
        out_specs=VMEM,
        compiler_params=LIMIT,
        name="round_grad",
    )(a, b, *arrived)


def weight_kernel(packs, starts, *refs):
    toks, grads = refs[:BLOCK], refs[BLOCK : 2 * BLOCK]
    keep_ref, send_ref = refs[2 * BLOCK :]
    width = keep_ref.shape[1]
    starts = [start * width for start in starts]
    core = lax.rem(lax.axis_index("dp"), CORES)
    for ref, which in ((send_ref, 1 - core), (keep_ref, core)):
        acc = None
        for k in range(BLOCK):
            first = pl.multiple_of(starts[k] + which * width, width)
            term = _mm(grads[k][...], toks[k][:, pl.ds(first, width)], NN)
            acc = term if acc is None else acc + term
        ref[...] = acc * (1.0 / packs)


def weight_part(toks, grads, packs, starts):
    part = jax.ShapeDtypeStruct((grads[0].shape[0], toks[-1].shape[1] // CORES), F32)
    return pl.pallas_call(
        functools.partial(weight_kernel, packs, starts),
        out_shape=[part, part],
        in_specs=[VMEM] * (2 * BLOCK),
        out_specs=[VMEM, VMEM],
        compiler_params=LIMIT,
        name="weight_part",
    )(*toks, *grads)


def fold_kernel(a_ref, b_ref, out_ref):
    out_ref[...] = a_ref[...] + b_ref[...]


def fold(a, b):
    return pl.pallas_call(
        fold_kernel,
        out_shape=jax.ShapeDtypeStruct(a.shape, F32),
        in_specs=[VMEM, VMEM],
        out_specs=VMEM,
        compiler_params=LIMIT,
        name="weight_fold",
    )(a, b)


def finish_kernel(a_ref, b_ref, out_ref):
    out_ref[...] = (a_ref[...] + b_ref[...]).T.astype(BF16)


def finish(a, b):
    return pl.pallas_call(
        finish_kernel,
        out_shape=jax.ShapeDtypeStruct((a.shape[1], a.shape[0]), BF16),
        in_specs=[VMEM] * 2,
        out_specs=VMEM,
        compiler_params=LIMIT,
        name="weight_finish",
    )(a, b)


def stack_kernel(count, *refs):
    out_ref = refs[-1]
    first = 0
    for ref in refs[:count]:
        out_ref[first : first + ref.shape[0], :] = ref[...]
        first += ref.shape[0]


def stack(parts, after=()):
    rows = sum(part.shape[0] for part in parts)
    return pl.pallas_call(
        functools.partial(stack_kernel, len(parts)),
        out_shape=jax.ShapeDtypeStruct((rows, parts[0].shape[1]), BF16),
        in_specs=[VMEM] * len(parts) + [ANY] * len(after),
        out_specs=VMEM,
        compiler_params=LIMIT,
        name="stack",
    )(*parts, *after)


def assemble_kernel(held, rows, *refs):
    arrays, out_ref, sems = refs[: len(held)], refs[-2], refs[-1]
    me = lax.axis_index("dp")
    copies = []
    for array, bits in zip(arrays, held):
        for n, bit in enumerate(bits):
            source = me ^ bit
            high = source // (CORES * BLOCK)
            place = (block_of(source) * CORES + lax.rem(source, CORES)) * 2 + high
            first = pl.multiple_of(place * rows, rows)
            copy = pltpu.make_async_copy(
                array.at[pl.ds(n * rows, rows), :],
                out_ref.at[pl.ds(first, rows), :],
                sems.at[len(copies)],
            )
            copy.start()
            copies.append(copy)
    for copy in copies:
        copy.wait()


def assemble(pieces, total, begun=None):
    arrays = [array for array, _ in pieces]
    held = [bits for _, bits in pieces]
    rows = arrays[0].shape[0] // len(held[0])
    count = len(arrays)
    if begun is not None:
        arrays.append(begun)
    return pl.pallas_call(
        functools.partial(assemble_kernel, held, rows),
        out_shape=jax.ShapeDtypeStruct((total * rows, arrays[0].shape[1]), BF16),
        in_specs=[ANY] * len(arrays),
        out_specs=ANY,
        scratch_shapes=[pltpu.SemaphoreType.DMA((sum(len(bits) for bits in held),))],
        input_output_aliases={} if begun is None else {count: 0},
        compiler_params=LIMIT,
        name="weight_assemble" if begun is None else "weight_complete",
    )(*arrays)


def hop(value, bits):
    count = lax.axis_size("dp")
    return lax.ppermute(value, "dp", [(i, i ^ bits) for i in range(count)])


def per_device_16x2(tokens, queries, grad_out, w_kv, doc_ids, span_order):
    dp_size = lax.axis_size("dp")
    rows_dev = queries.shape[1]
    swap = [(0, 1), (1, 0)]
    near = (Y, Z1, Y | Z1)
    flat = tokens[0]
    both = (True, False)
    own, tok_y, tok_z, far_d = slice_tokens(
        flat, [(0, both), (1, both), (2, both), (3, (True,))], "slice_first"
    )
    tok_y, tok_z, far_d = hop(tok_y, Y), hop(tok_z, Z1), hop(far_d, Y | Z1)
    partial = project(flat, w_kv)
    other = lax.ppermute(partial, "seq", swap)
    docs = doc_ids.reshape(-1, rows_dev)
    attention, query_grad, terms, done = attend(
        span_order, docs, queries[0], grad_out[0], [partial, other]
    )
    grad = round_grad(terms, lax.ppermute(terms, "seq", swap), [done, tok_y, tok_z])
    grads = [grad] + [hop(grad, bits) for bits in near]
    keep, send = weight_part([own, tok_y, tok_z, far_d], grads, dp_size, [0, 0, 0, 0])
    part = fold(keep, hop(send, CORE))
    far = hop(part, Z2)
    (near_d,) = slice_tokens(flat, [(3, (False,))], "slice_near_diagonal")
    near_d = hop(near_d, Y | Z1)
    keep, send = weight_part([own, tok_y, tok_z, near_d], grads, dp_size, [2, 2, 2, 0])
    own = finish(fold(keep, far), hop(send, CORE))
    z1, y, d, z2 = hop(own, Z1), hop(own, Y), hop(own, Y | Z1), hop(own, Z2)
    z21, z2y, z2d = hop(z2, Z1), hop(z2, Y), hop(z2, Y | Z1)
    first = hop(stack([own, z1, y, d]), CORE)
    last = hop(stack([z2, z21, z2y, z2d]), CORE)
    pieces = [
        (own, [0]),
        (z1, [Z1]),
        (y, [Y]),
        (d, [Y | Z1]),
        (z2, [Z2]),
        (z21, [Z2 | Z1]),
        (z2y, [Z2 | Y]),
        (z2d, [Z2 | Y | Z1]),
    ]
    held = [[bit | CORE for _, bits in part for bit in bits] for part in (pieces[:4], pieces[4:])]
    weight_grad = assemble(pieces + [(first, held[0])], dp_size)
    weight_grad = assemble([(last, held[1])], dp_size, weight_grad)
    return (attention[None], query_grad[None], weight_grad)


def per_device(tokens, queries, grad_out, w_kv, doc_ids, span_order):
    dp_size = lax.axis_size("dp")
    rows_dev = queries.shape[1]
    flat = tokens[0]
    spread = lax.all_to_all(flat, "dp", split_axis=1, concat_axis=0, tiled=True)
    partial = jnp.dot(flat, w_kv, preferred_element_type=F32)
    own = lax.psum_scatter(partial, "seq", scatter_dimension=0, tiled=True).astype(BF16)
    kvs = [lax.all_gather(own, "seq", axis=0, tiled=True)]
    docs = doc_ids.reshape(-1, rows_dev)
    attention, query_grad, terms, done = attend(span_order, docs, queries[0], grad_out[0], kvs)
    grad_kv = lax.psum(terms.T, "seq").astype(BF16)
    all_grads = lax.all_gather(grad_kv, "dp", axis=0, tiled=True)
    piece = (_mm(spread, all_grads, TN) * (1.0 / dp_size)).astype(BF16)
    weight_grad = lax.all_gather(piece, "dp", axis=0, tiled=True)
    return (attention[None], query_grad[None], weight_grad)


def solution(mesh):
    small = mesh.shape["dp"] == 16 and mesh.shape["seq"] == 2
    return jax.shard_map(
        per_device_16x2 if small else per_device,
        mesh=mesh,
        in_specs=(
            P("dp", None, "seq"),
            P("dp", "seq", None),
            P("dp", "seq", None),
            P("seq", None),
            P("dp", None),
            P(),
        ),
        out_specs=(P("dp", "seq", None), P("dp", "seq", None), P("seq", None)),
        check_vma=False,
    )
```

```python
import functools
import math

import jax
import jax.numpy as jnp
from jax import lax
from jax.experimental import pallas as pl
from jax.experimental.pallas import tpu as pltpu
from jax.sharding import PartitionSpec as P

HEAD = 128
LOG2E = math.log2(math.e)
QH = 8
GROUP = 4
F32 = jnp.float32
BF16 = jnp.bfloat16
NT = (((1,), (1,)), ((), ()))
TN = (((0,), (0,)), ((), ()))
NN = (((1,), (0,)), ((), ()))


def _mm(a, b, dims):
    return lax.dot_general(a, b, dims, preferred_element_type=F32)


ANY = pl.BlockSpec(memory_space=pl.ANY)
VMEM = pl.BlockSpec(memory_space=pltpu.VMEM)
LIMIT = pltpu.CompilerParams(vmem_limit_bytes=48 * 1024 * 1024)


def terms_kernel(parts, own, order_ref, docs_ref, q_ref, g_ref, *refs):
    kv_refs = refs[:parts]
    kv_ref, low_ref, ds_ref, terms_ref = refs[-4:]
    rows = q_ref.shape[0]
    seq_len = kv_refs[0].shape[0]
    spans = seq_len // rows
    if parts == 1:
        kv = kv_refs[0][...]
    else:
        kv = (kv_refs[0][...] + kv_refs[1][...]).astype(BF16)
    kv_ref[...] = kv
    keys = kv[:, :HEAD]
    values = kv[:, HEAD:]
    scale = 1.0 / math.sqrt(HEAD)
    me = lax.axis_index(own)

    def row_docs(span):
        return docs_ref[pl.ds(order_ref[span], 1), :]

    masks = []
    q_docs = row_docs(me)
    q_span = order_ref[me]
    q_pos = lax.broadcasted_iota(jnp.int32, (rows, rows), 1)
    k_pos = lax.broadcasted_iota(jnp.int32, (rows, rows), 0)
    for span in range(spans):
        k_docs = jnp.broadcast_to(row_docs(span), (rows, rows)).T
        gap = (order_ref[span] - q_span) * rows
        masks.append((k_pos + gap <= q_pos) & (k_docs == q_docs))
    allowed = jnp.concatenate(masks, axis=0)
    allowed = jnp.concatenate([allowed] * GROUP, axis=1)

    key_grad = jnp.zeros((seq_len, HEAD), F32)
    value_grad = jnp.zeros((seq_len, HEAD), F32)
    for first in range(0, QH, GROUP):
        heads = range(first, first + GROUP)
        q = jnp.concatenate([q_ref[:, h * HEAD : (h + 1) * HEAD] for h in heads], axis=0)
        g = jnp.concatenate([g_ref[:, h * HEAD : (h + 1) * HEAD] for h in heads], axis=0)
        scores = jnp.where(allowed, _mm(keys, q, NT), F32(-1e30))
        expo = jnp.exp2((scores - jnp.max(scores, axis=0, keepdims=True)) * (scale * LOG2E))
        probs = expo * (1.0 / jnp.sum(expo, axis=0, keepdims=True))
        low = probs.astype(BF16)
        grad_probs = _mm(values, g, NT)
        delta = jnp.sum(probs * grad_probs, axis=0, keepdims=True)
        grad_scores = (probs * (grad_probs - delta) * scale).astype(BF16)
        low_ref[:, first * rows : (first + GROUP) * rows] = low
        ds_ref[:, first * rows : (first + GROUP) * rows] = grad_scores
        key_grad += _mm(grad_scores, q, NN)
        value_grad += _mm(low, g, NN)
    terms_ref[:HEAD, :] = key_grad.T
    terms_ref[HEAD:, :] = value_grad.T


def outputs_kernel(kv_ref, low_ref, ds_ref, att_ref, qg_ref, done_ref):
    rows = att_ref.shape[0]
    done_ref[...] = jnp.zeros_like(done_ref)
    keys_t = kv_ref[:, :HEAD].T
    values_t = kv_ref[:, HEAD:].T
    for first in range(0, QH, GROUP):
        cols = slice(first * rows, (first + GROUP) * rows)
        att = _mm(values_t, low_ref[:, cols], NN)
        qg = _mm(keys_t, ds_ref[:, cols], NN)
        for i in range(GROUP):
            head = slice((first + i) * HEAD, (first + i + 1) * HEAD)
            att_ref[:, head] = att[:, i * rows : (i + 1) * rows].T.astype(BF16)
            qg_ref[:, head] = qg[:, i * rows : (i + 1) * rows].T.astype(BF16)


def attend(order, docs, q, g, kvs):
    seq_len, rows = kvs[0].shape[0], q.shape[0]
    kv, low, grad_scores, terms = pl.pallas_call(
        functools.partial(terms_kernel, len(kvs), "seq"),
        out_shape=(
            jax.ShapeDtypeStruct((seq_len, 2 * HEAD), BF16),
            jax.ShapeDtypeStruct((seq_len, QH * rows), BF16),
            jax.ShapeDtypeStruct((seq_len, QH * rows), BF16),
            jax.ShapeDtypeStruct((2 * HEAD, seq_len), F32),
        ),
        in_specs=[pl.BlockSpec(memory_space=pltpu.SMEM)] + [VMEM] * (3 + len(kvs)),
        out_specs=[VMEM] * 4,
        compiler_params=LIMIT,
        name="attention_terms",
    )(order, docs, q, g, *kvs)
    attention, query_grad, done = pl.pallas_call(
        outputs_kernel,
        out_shape=[jax.ShapeDtypeStruct(q.shape, BF16)] * 2 + [jax.ShapeDtypeStruct((8, HEAD), F32)],
        in_specs=[VMEM] * 3,
        out_specs=[VMEM] * 3,
        compiler_params=LIMIT,
        name="attention_outputs",
    )(kv, low, grad_scores)
    return attention, query_grad, terms, done


CORE, Y, Z1, Z2 = 1, 2, 4, 8
CHUNKS = 8
CORES = 2
BLOCK = 4


def block_of(device):
    return lax.rem(device // CORES, BLOCK)


def half_cols(device, k, core, far_half, width):
    high = device // (CORES * BLOCK)
    high = 1 - high if far_half else high
    return pl.multiple_of((((block_of(device) ^ k) * CORES + core) * 2 + high) * width, width)


def start_slices(wanted, tok_ref, slices, sems):
    me = lax.axis_index("dp")
    copies = []
    for (k, halves), ref in zip(wanted, slices):
        width = ref.shape[1] // (CORES * len(halves))
        for n, far_half in enumerate(halves):
            for core in range(CORES):
                copy = pltpu.make_async_copy(
                    tok_ref.at[:, pl.ds(half_cols(me, k, core, far_half, width), width)],
                    ref.at[:, pl.ds((n * CORES + core) * width, width)],
                    sems.at[len(copies)],
                )
                copy.start()
                copies.append(copy)
    return copies


def slice_kernel(wanted, tok_ref, *refs):
    for copy in start_slices(wanted, tok_ref, refs[-1 - len(wanted) : -1], refs[-1]):
        copy.wait()


def slice_tokens(tokens, wanted, name, after=()):
    rows, features = tokens.shape
    half = features // (2 * BLOCK)
    return pl.pallas_call(
        functools.partial(slice_kernel, wanted),
        out_shape=[jax.ShapeDtypeStruct((rows, half * len(halves)), BF16) for _, halves in wanted],
        in_specs=[ANY] * (1 + len(after)),
        out_specs=[VMEM] * len(wanted),
        scratch_shapes=[pltpu.SemaphoreType.DMA((sum(2 * len(halves) for _, halves in wanted),))],
        compiler_params=LIMIT,
        name=name,
    )(tokens, *after)


def project_kernel(wanted, tok_ref, w_ref, out_ref, *refs):
    slices, (slice_sems, w_v, w_sems) = refs[:-3], refs[-3:]
    chunk = w_ref.shape[0] // CHUNKS
    loads = []
    for k in range(CHUNKS):
        cut = pl.ds(k * chunk, chunk)
        load = pltpu.make_async_copy(w_ref.at[cut, :], w_v.at[cut, :], w_sems.at[k])
        load.start()
        loads.append(load)
    copies = start_slices(wanted, tok_ref, slices, slice_sems)
    total = None
    for k, load in enumerate(loads):
        load.wait()
        cut = slice(k * chunk, (k + 1) * chunk)
        term = _mm(tok_ref[:, cut], w_v[cut, :], NN)
        total = term if total is None else total + term
    out_ref[...] = total
    for copy in copies:
        copy.wait()


def project(tokens, w_kv, wanted):
    rows, features = tokens.shape
    half = features // (2 * BLOCK)
    return pl.pallas_call(
        functools.partial(project_kernel, wanted),
        out_shape=[jax.ShapeDtypeStruct((rows, w_kv.shape[1]), F32)]
        + [jax.ShapeDtypeStruct((rows, half * len(halves)), BF16) for _, halves in wanted],
        in_specs=[VMEM, ANY],
        out_specs=[VMEM] * (1 + len(wanted)),
        scratch_shapes=[
            pltpu.SemaphoreType.DMA((sum(2 * len(halves) for _, halves in wanted),)),
            pltpu.VMEM(w_kv.shape, BF16),
            pltpu.SemaphoreType.DMA((CHUNKS,)),
        ],
        compiler_params=LIMIT,
        name="project",
    )(tokens, w_kv)


def round_kernel(a_ref, b_ref, *refs):
    refs[-1][...] = (a_ref[...] + b_ref[...]).astype(BF16)


def round_grad(a, b, arrived):
    return pl.pallas_call(
        round_kernel,
        out_shape=jax.ShapeDtypeStruct(a.shape, BF16),
        in_specs=[VMEM, VMEM] + [ANY] * len(arrived),
        out_specs=VMEM,
        compiler_params=LIMIT,
        name="round_grad",
    )(a, b, *arrived)


def weight_kernel(packs, starts, *refs):
    toks, grads = refs[:BLOCK], refs[BLOCK : 2 * BLOCK]
    keep_ref, send_ref = refs[2 * BLOCK :]
    width = keep_ref.shape[1]
    starts = [start * width for start in starts]
    core = lax.rem(lax.axis_index("dp"), CORES)
    for ref, which in ((send_ref, 1 - core), (keep_ref, core)):
        acc = None
        for k in range(BLOCK):
            first = pl.multiple_of(starts[k] + which * width, width)
            term = _mm(grads[k][...], toks[k][:, pl.ds(first, width)], NN)
            acc = term if acc is None else acc + term
        ref[...] = acc * (1.0 / packs)


def weight_part(toks, grads, packs, starts):
    part = jax.ShapeDtypeStruct((grads[0].shape[0], toks[-1].shape[1] // CORES), F32)
    return pl.pallas_call(
        functools.partial(weight_kernel, packs, starts),
        out_shape=[part, part],
        in_specs=[VMEM] * (2 * BLOCK),
        out_specs=[VMEM, VMEM],
        compiler_params=LIMIT,
        name="weight_part",
    )(*toks, *grads)


def fold_kernel(a_ref, b_ref, out_ref):
    out_ref[...] = a_ref[...] + b_ref[...]


def fold(a, b):
    return pl.pallas_call(
        fold_kernel,
        out_shape=jax.ShapeDtypeStruct(a.shape, F32),
        in_specs=[VMEM, VMEM],
        out_specs=VMEM,
        compiler_params=LIMIT,
        name="weight_fold",
    )(a, b)


def finish_kernel(a_ref, b_ref, out_ref):
    out_ref[...] = (a_ref[...] + b_ref[...]).T.astype(BF16)


def finish(a, b):
    return pl.pallas_call(
        finish_kernel,
        out_shape=jax.ShapeDtypeStruct((a.shape[1], a.shape[0]), BF16),
        in_specs=[VMEM] * 2,
        out_specs=VMEM,
        compiler_params=LIMIT,
        name="weight_finish",
    )(a, b)


def stack_kernel(count, *refs):
    out_ref = refs[-1]
    first = 0
    for ref in refs[:count]:
        out_ref[first : first + ref.shape[0], :] = ref[...]
        first += ref.shape[0]


def stack(parts, after=()):
    rows = sum(part.shape[0] for part in parts)
    return pl.pallas_call(
        functools.partial(stack_kernel, len(parts)),
        out_shape=jax.ShapeDtypeStruct((rows, parts[0].shape[1]), BF16),
        in_specs=[VMEM] * len(parts) + [ANY] * len(after),
        out_specs=VMEM,
        compiler_params=LIMIT,
        name="stack",
    )(*parts, *after)


def assemble_kernel(held, rows, *refs):
    arrays, out_ref, sems = refs[: len(held)], refs[-2], refs[-1]
    me = lax.axis_index("dp")
    copies = []
    for array, bits in zip(arrays, held):
        for n, bit in enumerate(bits):
            source = me ^ bit
            high = source // (CORES * BLOCK)
            place = (block_of(source) * CORES + lax.rem(source, CORES)) * 2 + high
            first = pl.multiple_of(place * rows, rows)
            copy = pltpu.make_async_copy(
                array.at[pl.ds(n * rows, rows), :],
                out_ref.at[pl.ds(first, rows), :],
                sems.at[len(copies)],
            )
            copy.start()
            copies.append(copy)
    for copy in copies:
        copy.wait()


def assemble(pieces, total, begun=None):
    arrays = [array for array, _ in pieces]
    held = [bits for _, bits in pieces]
    rows = arrays[0].shape[0] // len(held[0])
    count = len(arrays)
    if begun is not None:
        arrays.append(begun)
    return pl.pallas_call(
        functools.partial(assemble_kernel, held, rows),
        out_shape=jax.ShapeDtypeStruct((total * rows, arrays[0].shape[1]), BF16),
        in_specs=[ANY] * len(arrays),
        out_specs=ANY,
        scratch_shapes=[pltpu.SemaphoreType.DMA((sum(len(bits) for bits in held),))],
        input_output_aliases={} if begun is None else {count: 0},
        compiler_params=LIMIT,
        name="weight_assemble" if begun is None else "weight_complete",
    )(*arrays)


def hop(value, bits):
    count = lax.axis_size("dp")
    return lax.ppermute(value, "dp", [(i, i ^ bits) for i in range(count)])


def per_device_16x2(tokens, queries, grad_out, w_kv, doc_ids, span_order):
    dp_size = lax.axis_size("dp")
    rows_dev = queries.shape[1]
    swap = [(0, 1), (1, 0)]
    near = (Y, Z1, Y | Z1)
    flat = tokens[0]
    both = (True, False)
    partial, own, tok_y, tok_z, far_d = project(
        flat, w_kv, [(0, both), (1, both), (2, both), (3, (True,))]
    )
    tok_y, tok_z, far_d = hop(tok_y, Y), hop(tok_z, Z1), hop(far_d, Y | Z1)
    other = lax.ppermute(partial, "seq", swap)
    docs = doc_ids.reshape(-1, rows_dev)
    attention, query_grad, terms, done = attend(
        span_order, docs, queries[0], grad_out[0], [partial, other]
    )
    grad = round_grad(terms, lax.ppermute(terms, "seq", swap), [done, tok_y, tok_z])
    grads = [grad] + [hop(grad, bits) for bits in near]
    keep, send = weight_part([own, tok_y, tok_z, far_d], grads, dp_size, [0, 0, 0, 0])
    part = fold(keep, hop(send, CORE))
    far = hop(part, Z2)
    (near_d,) = slice_tokens(flat, [(3, (False,))], "slice_near_diagonal")
    near_d = hop(near_d, Y | Z1)
    keep, send = weight_part([own, tok_y, tok_z, near_d], grads, dp_size, [2, 2, 2, 0])
    own = finish(fold(keep, far), hop(send, CORE))
    z1, y, d, z2 = hop(own, Z1), hop(own, Y), hop(own, Y | Z1), hop(own, Z2)
    z21, z2y, z2d = hop(z2, Z1), hop(z2, Y), hop(z2, Y | Z1)
    first = hop(stack([own, z1, y, d]), CORE)
    last = hop(stack([z2, z21, z2y, z2d]), CORE)
    pieces = [
        (own, [0]),
        (z1, [Z1]),
        (y, [Y]),
        (d, [Y | Z1]),
        (z2, [Z2]),
        (z21, [Z2 | Z1]),
        (z2y, [Z2 | Y]),
        (z2d, [Z2 | Y | Z1]),
    ]
    held = [[bit | CORE for _, bits in part for bit in bits] for part in (pieces[:4], pieces[4:])]
    weight_grad = assemble(pieces + [(first, held[0])], dp_size)
    weight_grad = assemble([(last, held[1])], dp_size, weight_grad)
    return (attention[None], query_grad[None], weight_grad)


def per_device(tokens, queries, grad_out, w_kv, doc_ids, span_order):
    dp_size = lax.axis_size("dp")
    rows_dev = queries.shape[1]
    flat = tokens[0]
    spread = lax.all_to_all(flat, "dp", split_axis=1, concat_axis=0, tiled=True)
    partial = jnp.dot(flat, w_kv, preferred_element_type=F32)
    own = lax.psum_scatter(partial, "seq", scatter_dimension=0, tiled=True).astype(BF16)
    kvs = [lax.all_gather(own, "seq", axis=0, tiled=True)]
    docs = doc_ids.reshape(-1, rows_dev)
    attention, query_grad, terms, done = attend(span_order, docs, queries[0], grad_out[0], kvs)
    grad_kv = lax.psum(terms.T, "seq").astype(BF16)
    all_grads = lax.all_gather(grad_kv, "dp", axis=0, tiled=True)
    piece = (_mm(spread, all_grads, TN) * (1.0 / dp_size)).astype(BF16)
    weight_grad = lax.all_gather(piece, "dp", axis=0, tiled=True)
    return (attention[None], query_grad[None], weight_grad)


def solution(mesh):
    small = mesh.shape["dp"] == 16 and mesh.shape["seq"] == 2
    return jax.shard_map(
        per_device_16x2 if small else per_device,
        mesh=mesh,
        in_specs=(
            P("dp", None, "seq"),
            P("dp", "seq", None),
            P("dp", "seq", None),
            P("seq", None),
            P("dp", None),
            P(),
        ),
        out_specs=(P("dp", "seq", None), P("dp", "seq", None), P("seq", None)),
        check_vma=False,
    )
```

```python
import functools
import math

import jax
import jax.numpy as jnp
from jax import lax
from jax.experimental import pallas as pl
from jax.experimental.pallas import tpu as pltpu
from jax.sharding import PartitionSpec as P

HEAD = 128
LOG2E = math.log2(math.e)
QH = 8
GROUP = 4
F32 = jnp.float32
BF16 = jnp.bfloat16
NT = (((1,), (1,)), ((), ()))
TN = (((0,), (0,)), ((), ()))
NN = (((1,), (0,)), ((), ()))


def _mm(a, b, dims):
    return lax.dot_general(a, b, dims, preferred_element_type=F32)


ANY = pl.BlockSpec(memory_space=pl.ANY)
VMEM = pl.BlockSpec(memory_space=pltpu.VMEM)
LIMIT = pltpu.CompilerParams(vmem_limit_bytes=48 * 1024 * 1024)


def terms_kernel(parts, own, order_ref, docs_ref, q_ref, g_ref, *refs):
    kv_refs = refs[:parts]
    kv_ref, low_ref, ds_ref, terms_ref = refs[-4:]
    rows = q_ref.shape[0]
    seq_len = kv_refs[0].shape[0]
    spans = seq_len // rows
    if parts == 1:
        kv = kv_refs[0][...]
    else:
        kv = (kv_refs[0][...] + kv_refs[1][...]).astype(BF16)
    kv_ref[...] = kv
    keys = kv[:, :HEAD]
    values = kv[:, HEAD:]
    scale = 1.0 / math.sqrt(HEAD)
    me = lax.axis_index(own)

    def row_docs(span):
        return docs_ref[pl.ds(order_ref[span], 1), :]

    masks = []
    q_docs = row_docs(me)
    q_span = order_ref[me]
    q_pos = lax.broadcasted_iota(jnp.int32, (rows, rows), 1)
    k_pos = lax.broadcasted_iota(jnp.int32, (rows, rows), 0)
    for span in range(spans):
        k_docs = jnp.broadcast_to(row_docs(span), (rows, rows)).T
        gap = (order_ref[span] - q_span) * rows
        masks.append((k_pos + gap <= q_pos) & (k_docs == q_docs))
    allowed = jnp.concatenate(masks, axis=0)
    allowed = jnp.concatenate([allowed] * GROUP, axis=1)

    key_grad = jnp.zeros((seq_len, HEAD), F32)
    value_grad = jnp.zeros((seq_len, HEAD), F32)
    for first in range(0, QH, GROUP):
        heads = range(first, first + GROUP)
        q = jnp.concatenate([q_ref[:, h * HEAD : (h + 1) * HEAD] for h in heads], axis=0)
        g = jnp.concatenate([g_ref[:, h * HEAD : (h + 1) * HEAD] for h in heads], axis=0)
        scores = jnp.where(allowed, _mm(keys, q, NT), F32(-1e30))
        expo = jnp.exp2((scores - jnp.max(scores, axis=0, keepdims=True)) * (scale * LOG2E))
        probs = expo * (1.0 / jnp.sum(expo, axis=0, keepdims=True))
        low = probs.astype(BF16)
        grad_probs = _mm(values, g, NT)
        delta = jnp.sum(probs * grad_probs, axis=0, keepdims=True)
        grad_scores = (probs * (grad_probs - delta) * scale).astype(BF16)
        low_ref[:, first * rows : (first + GROUP) * rows] = low
        ds_ref[:, first * rows : (first + GROUP) * rows] = grad_scores
        key_grad += _mm(grad_scores, q, NN)
        value_grad += _mm(low, g, NN)
    terms_ref[:HEAD, :] = key_grad.T
    terms_ref[HEAD:, :] = value_grad.T


def outputs_kernel(kv_ref, low_ref, ds_ref, att_ref, qg_ref, done_ref):
    rows = att_ref.shape[0]
    done_ref[...] = jnp.zeros_like(done_ref)
    keys_t = kv_ref[:, :HEAD].T
    values_t = kv_ref[:, HEAD:].T
    for first in range(0, QH, GROUP):
        cols = slice(first * rows, (first + GROUP) * rows)
        att = _mm(values_t, low_ref[:, cols], NN)
        qg = _mm(keys_t, ds_ref[:, cols], NN)
        for i in range(GROUP):
            head = slice((first + i) * HEAD, (first + i + 1) * HEAD)
            att_ref[:, head] = att[:, i * rows : (i + 1) * rows].T.astype(BF16)
            qg_ref[:, head] = qg[:, i * rows : (i + 1) * rows].T.astype(BF16)


def attend(order, docs, q, g, kvs):
    seq_len, rows = kvs[0].shape[0], q.shape[0]
    kv, low, grad_scores, terms = pl.pallas_call(
        functools.partial(terms_kernel, len(kvs), "seq"),
        out_shape=(
            jax.ShapeDtypeStruct((seq_len, 2 * HEAD), BF16),
            jax.ShapeDtypeStruct((seq_len, QH * rows), BF16),
            jax.ShapeDtypeStruct((seq_len, QH * rows), BF16),
            jax.ShapeDtypeStruct((2 * HEAD, seq_len), F32),
        ),
        in_specs=[pl.BlockSpec(memory_space=pltpu.SMEM)] + [VMEM] * (3 + len(kvs)),
        out_specs=[VMEM] * 4,
        compiler_params=LIMIT,
        name="attention_terms",
    )(order, docs, q, g, *kvs)
    attention, query_grad, done = pl.pallas_call(
        outputs_kernel,
        out_shape=[jax.ShapeDtypeStruct(q.shape, BF16)] * 2 + [jax.ShapeDtypeStruct((8, HEAD), F32)],
        in_specs=[VMEM] * 3,
        out_specs=[VMEM] * 3,
        compiler_params=LIMIT,
        name="attention_outputs",
    )(kv, low, grad_scores)
    return attention, query_grad, terms, done


CORE, Y, Z1, Z2 = 1, 2, 4, 8
CHUNKS = 8
CORES = 2
BLOCK = 4


def block_of(device):
    return lax.rem(device // CORES, BLOCK)


def half_cols(device, k, core, far_half, width):
    high = device // (CORES * BLOCK)
    high = 1 - high if far_half else high
    return pl.multiple_of((((block_of(device) ^ k) * CORES + core) * 2 + high) * width, width)


def slice_kernel(wanted, tok_ref, *refs):
    slices, sems = refs[-1 - len(wanted) : -1], refs[-1]
    me = lax.axis_index("dp")
    copies = []
    for (k, halves), ref in zip(wanted, slices):
        width = ref.shape[1] // (CORES * len(halves))
        for n, far_half in enumerate(halves):
            for core in range(CORES):
                copy = pltpu.make_async_copy(
                    tok_ref.at[:, pl.ds(half_cols(me, k, core, far_half, width), width)],
                    ref.at[:, pl.ds((n * CORES + core) * width, width)],
                    sems.at[len(copies)],
                )
                copy.start()
                copies.append(copy)
    for copy in copies:
        copy.wait()


def slice_tokens(tokens, wanted, name, after=()):
    rows, features = tokens.shape
    half = features // (2 * BLOCK)
    return pl.pallas_call(
        functools.partial(slice_kernel, wanted),
        out_shape=[jax.ShapeDtypeStruct((rows, half * len(halves)), BF16) for _, halves in wanted],
        in_specs=[ANY] * (1 + len(after)),
        out_specs=[VMEM] * len(wanted),
        scratch_shapes=[pltpu.SemaphoreType.DMA((sum(2 * len(halves) for _, halves in wanted),))],
        compiler_params=LIMIT,
        name=name,
    )(tokens, *after)


def project_kernel(wanted, tok_ref, w_ref, out_ref, *refs):
    slices, (w_v, w_sems) = refs[:-2], refs[-2:]
    chunk = w_ref.shape[0] // CHUNKS
    loads = []
    for k in range(CHUNKS):
        cut = pl.ds(k * chunk, chunk)
        load = pltpu.make_async_copy(w_ref.at[cut, :], w_v.at[cut, :], w_sems.at[k])
        load.start()
        loads.append(load)
    me = lax.axis_index("dp")
    for (k, halves), ref in zip(wanted, slices):
        width = ref.shape[1] // (CORES * len(halves))
        for n, far_half in enumerate(halves):
            for core in range(CORES):
                first = (n * CORES + core) * width
                source = pl.ds(half_cols(me, k, core, far_half, width), width)
                ref[:, first : first + width] = tok_ref[:, source]
    total = None
    for k, load in enumerate(loads):
        load.wait()
        cut = slice(k * chunk, (k + 1) * chunk)
        term = _mm(tok_ref[:, cut], w_v[cut, :], NN)
        total = term if total is None else total + term
    out_ref[...] = total


def project(tokens, w_kv, wanted):
    rows, features = tokens.shape
    half = features // (2 * BLOCK)
    return pl.pallas_call(
        functools.partial(project_kernel, wanted),
        out_shape=[jax.ShapeDtypeStruct((rows, w_kv.shape[1]), F32)]
        + [jax.ShapeDtypeStruct((rows, half * len(halves)), BF16) for _, halves in wanted],
        in_specs=[VMEM, ANY],
        out_specs=[VMEM] * (1 + len(wanted)),
        scratch_shapes=[
            pltpu.VMEM(w_kv.shape, BF16),
            pltpu.SemaphoreType.DMA((CHUNKS,)),
        ],
        compiler_params=LIMIT,
        name="project",
    )(tokens, w_kv)


def round_kernel(a_ref, b_ref, *refs):
    refs[-1][...] = (a_ref[...] + b_ref[...]).astype(BF16)


def round_grad(a, b, arrived):
    return pl.pallas_call(
        round_kernel,
        out_shape=jax.ShapeDtypeStruct(a.shape, BF16),
        in_specs=[VMEM, VMEM] + [ANY] * len(arrived),
        out_specs=VMEM,
        compiler_params=LIMIT,
        name="round_grad",
    )(a, b, *arrived)


def weight_kernel(packs, starts, *refs):
    toks, grads = refs[:BLOCK], refs[BLOCK : 2 * BLOCK]
    keep_ref, send_ref = refs[2 * BLOCK :]
    width = keep_ref.shape[1]
    starts = [start * width for start in starts]
    core = lax.rem(lax.axis_index("dp"), CORES)
    for ref, which in ((send_ref, 1 - core), (keep_ref, core)):
        acc = None
        for k in range(BLOCK):
            first = pl.multiple_of(starts[k] + which * width, width)
            term = _mm(grads[k][...], toks[k][:, pl.ds(first, width)], NN)
            acc = term if acc is None else acc + term
        ref[...] = acc * (1.0 / packs)


def weight_part(toks, grads, packs, starts):
    part = jax.ShapeDtypeStruct((grads[0].shape[0], toks[-1].shape[1] // CORES), F32)
    return pl.pallas_call(
        functools.partial(weight_kernel, packs, starts),
        out_shape=[part, part],
        in_specs=[VMEM] * (2 * BLOCK),
        out_specs=[VMEM, VMEM],
        compiler_params=LIMIT,
        name="weight_part",
    )(*toks, *grads)


def fold_kernel(a_ref, b_ref, out_ref):
    out_ref[...] = a_ref[...] + b_ref[...]


def fold(a, b):
    return pl.pallas_call(
        fold_kernel,
        out_shape=jax.ShapeDtypeStruct(a.shape, F32),
        in_specs=[VMEM, VMEM],
        out_specs=VMEM,
        compiler_params=LIMIT,
        name="weight_fold",
    )(a, b)


def finish_kernel(a_ref, b_ref, out_ref):
    out_ref[...] = (a_ref[...] + b_ref[...]).T.astype(BF16)


def finish(a, b):
    return pl.pallas_call(
        finish_kernel,
        out_shape=jax.ShapeDtypeStruct((a.shape[1], a.shape[0]), BF16),
        in_specs=[VMEM] * 2,
        out_specs=VMEM,
        compiler_params=LIMIT,
        name="weight_finish",
    )(a, b)


def stack_kernel(count, *refs):
    out_ref = refs[-1]
    first = 0
    for ref in refs[:count]:
        out_ref[first : first + ref.shape[0], :] = ref[...]
        first += ref.shape[0]


def stack(parts, after=()):
    rows = sum(part.shape[0] for part in parts)
    return pl.pallas_call(
        functools.partial(stack_kernel, len(parts)),
        out_shape=jax.ShapeDtypeStruct((rows, parts[0].shape[1]), BF16),
        in_specs=[VMEM] * len(parts) + [ANY] * len(after),
        out_specs=VMEM,
        compiler_params=LIMIT,
        name="stack",
    )(*parts, *after)


def assemble_kernel(held, rows, *refs):
    arrays, out_ref, sems = refs[: len(held)], refs[-2], refs[-1]
    me = lax.axis_index("dp")
    copies = []
    for array, bits in zip(arrays, held):
        for n, bit in enumerate(bits):
            source = me ^ bit
            high = source // (CORES * BLOCK)
            place = (block_of(source) * CORES + lax.rem(source, CORES)) * 2 + high
            first = pl.multiple_of(place * rows, rows)
            copy = pltpu.make_async_copy(
                array.at[pl.ds(n * rows, rows), :],
                out_ref.at[pl.ds(first, rows), :],
                sems.at[len(copies)],
            )
            copy.start()
            copies.append(copy)
    for copy in copies:
        copy.wait()


def assemble(pieces, total, begun=None):
    arrays = [array for array, _ in pieces]
    held = [bits for _, bits in pieces]
    rows = arrays[0].shape[0] // len(held[0])
    count = len(arrays)
    if begun is not None:
        arrays.append(begun)
    return pl.pallas_call(
        functools.partial(assemble_kernel, held, rows),
        out_shape=jax.ShapeDtypeStruct((total * rows, arrays[0].shape[1]), BF16),
        in_specs=[ANY] * len(arrays),
        out_specs=ANY,
        scratch_shapes=[pltpu.SemaphoreType.DMA((sum(len(bits) for bits in held),))],
        input_output_aliases={} if begun is None else {count: 0},
        compiler_params=LIMIT,
        name="weight_assemble" if begun is None else "weight_complete",
    )(*arrays)


def hop(value, bits):
    count = lax.axis_size("dp")
    return lax.ppermute(value, "dp", [(i, i ^ bits) for i in range(count)])


def per_device_16x2(tokens, queries, grad_out, w_kv, doc_ids, span_order):
    dp_size = lax.axis_size("dp")
    rows_dev = queries.shape[1]
    swap = [(0, 1), (1, 0)]
    near = (Y, Z1, Y | Z1)
    flat = tokens[0]
    both = (True, False)
    partial, own, tok_y, tok_z, far_d = project(
        flat, w_kv, [(0, both), (1, both), (2, both), (3, (True,))]
    )
    tok_y, tok_z, far_d = hop(tok_y, Y), hop(tok_z, Z1), hop(far_d, Y | Z1)
    other = lax.ppermute(partial, "seq", swap)
    docs = doc_ids.reshape(-1, rows_dev)
    attention, query_grad, terms, done = attend(
        span_order, docs, queries[0], grad_out[0], [partial, other]
    )
    grad = round_grad(terms, lax.ppermute(terms, "seq", swap), [done, tok_y, tok_z])
    grads = [grad] + [hop(grad, bits) for bits in near]
    keep, send = weight_part([own, tok_y, tok_z, far_d], grads, dp_size, [0, 0, 0, 0])
    part = fold(keep, hop(send, CORE))
    far = hop(part, Z2)
    (near_d,) = slice_tokens(flat, [(3, (False,))], "slice_near_diagonal")
    near_d = hop(near_d, Y | Z1)
    keep, send = weight_part([own, tok_y, tok_z, near_d], grads, dp_size, [2, 2, 2, 0])
    own = finish(fold(keep, far), hop(send, CORE))
    z1, y, d, z2 = hop(own, Z1), hop(own, Y), hop(own, Y | Z1), hop(own, Z2)
    z21, z2y, z2d = hop(z2, Z1), hop(z2, Y), hop(z2, Y | Z1)
    first = hop(stack([own, z1, y, d]), CORE)
    last = hop(stack([z2, z21, z2y, z2d]), CORE)
    pieces = [
        (own, [0]),
        (z1, [Z1]),
        (y, [Y]),
        (d, [Y | Z1]),
        (z2, [Z2]),
        (z21, [Z2 | Z1]),
        (z2y, [Z2 | Y]),
        (z2d, [Z2 | Y | Z1]),
    ]
    held = [[bit | CORE for _, bits in part for bit in bits] for part in (pieces[:4], pieces[4:])]
    weight_grad = assemble(pieces + [(first, held[0])], dp_size)
    weight_grad = assemble([(last, held[1])], dp_size, weight_grad)
    return (attention[None], query_grad[None], weight_grad)


def per_device(tokens, queries, grad_out, w_kv, doc_ids, span_order):
    dp_size = lax.axis_size("dp")
    rows_dev = queries.shape[1]
    flat = tokens[0]
    spread = lax.all_to_all(flat, "dp", split_axis=1, concat_axis=0, tiled=True)
    partial = jnp.dot(flat, w_kv, preferred_element_type=F32)
    own = lax.psum_scatter(partial, "seq", scatter_dimension=0, tiled=True).astype(BF16)
    kvs = [lax.all_gather(own, "seq", axis=0, tiled=True)]
    docs = doc_ids.reshape(-1, rows_dev)
    attention, query_grad, terms, done = attend(span_order, docs, queries[0], grad_out[0], kvs)
    grad_kv = lax.psum(terms.T, "seq").astype(BF16)
    all_grads = lax.all_gather(grad_kv, "dp", axis=0, tiled=True)
    piece = (_mm(spread, all_grads, TN) * (1.0 / dp_size)).astype(BF16)
    weight_grad = lax.all_gather(piece, "dp", axis=0, tiled=True)
    return (attention[None], query_grad[None], weight_grad)


def solution(mesh):
    small = mesh.shape["dp"] == 16 and mesh.shape["seq"] == 2
    return jax.shard_map(
        per_device_16x2 if small else per_device,
        mesh=mesh,
        in_specs=(
            P("dp", None, "seq"),
            P("dp", "seq", None),
            P("dp", "seq", None),
            P("seq", None),
            P("dp", None),
            P(),
        ),
        out_specs=(P("dp", "seq", None), P("dp", "seq", None), P("seq", None)),
        check_vma=False,
    )
```

```python
import functools
import math

import jax
import jax.numpy as jnp
from jax import lax
from jax.experimental import pallas as pl
from jax.experimental.pallas import tpu as pltpu
from jax.sharding import PartitionSpec as P

HEAD = 128
LOG2E = math.log2(math.e)
QH = 8
GROUP = 4
F32 = jnp.float32
BF16 = jnp.bfloat16
NT = (((1,), (1,)), ((), ()))
TN = (((0,), (0,)), ((), ()))
NN = (((1,), (0,)), ((), ()))


def _mm(a, b, dims):
    return lax.dot_general(a, b, dims, preferred_element_type=F32)


ANY = pl.BlockSpec(memory_space=pl.ANY)
VMEM = pl.BlockSpec(memory_space=pltpu.VMEM)
LIMIT = pltpu.CompilerParams(vmem_limit_bytes=48 * 1024 * 1024)


def terms_kernel(parts, own, order_ref, docs_ref, q_ref, g_ref, *refs):
    kv_refs = refs[:parts]
    kv_ref, low_ref, ds_ref, terms_ref = refs[-4:]
    rows = q_ref.shape[0]
    seq_len = kv_refs[0].shape[0]
    spans = seq_len // rows
    if parts == 1:
        kv = kv_refs[0][...]
    else:
        kv = (kv_refs[0][...] + kv_refs[1][...]).astype(BF16)
    kv_ref[...] = kv
    keys = kv[:, :HEAD]
    values = kv[:, HEAD:]
    scale = 1.0 / math.sqrt(HEAD)
    me = lax.axis_index(own)

    def row_docs(span):
        return docs_ref[pl.ds(order_ref[span], 1), :]

    masks = []
    q_docs = row_docs(me)
    q_span = order_ref[me]
    q_pos = lax.broadcasted_iota(jnp.int32, (rows, rows), 1)
    k_pos = lax.broadcasted_iota(jnp.int32, (rows, rows), 0)
    for span in range(spans):
        k_docs = jnp.broadcast_to(row_docs(span), (rows, rows)).T
        gap = (order_ref[span] - q_span) * rows
        masks.append((k_pos + gap <= q_pos) & (k_docs == q_docs))
    allowed = jnp.concatenate(masks, axis=0)
    allowed = jnp.concatenate([allowed] * GROUP, axis=1)

    key_grad = jnp.zeros((seq_len, HEAD), F32)
    value_grad = jnp.zeros((seq_len, HEAD), F32)
    for first in range(0, QH, GROUP):
        heads = range(first, first + GROUP)
        q = jnp.concatenate([q_ref[:, h * HEAD : (h + 1) * HEAD] for h in heads], axis=0)
        g = jnp.concatenate([g_ref[:, h * HEAD : (h + 1) * HEAD] for h in heads], axis=0)
        scores = jnp.where(allowed, _mm(keys, q, NT), F32(-1e30))
        expo = jnp.exp2((scores - jnp.max(scores, axis=0, keepdims=True)) * (scale * LOG2E))
        probs = expo * (1.0 / jnp.sum(expo, axis=0, keepdims=True))
        low = probs.astype(BF16)
        grad_probs = _mm(values, g, NT)
        delta = jnp.sum(probs * grad_probs, axis=0, keepdims=True)
        grad_scores = (probs * (grad_probs - delta) * scale).astype(BF16)
        low_ref[:, first * rows : (first + GROUP) * rows] = low
        ds_ref[:, first * rows : (first + GROUP) * rows] = grad_scores
        key_grad += _mm(grad_scores, q, NN)
        value_grad += _mm(low, g, NN)
    terms_ref[:HEAD, :] = key_grad.T
    terms_ref[HEAD:, :] = value_grad.T


def outputs_kernel(kv_ref, low_ref, ds_ref, att_ref, qg_ref, done_ref):
    rows = att_ref.shape[0]
    done_ref[...] = jnp.zeros_like(done_ref)
    keys_t = kv_ref[:, :HEAD].T
    values_t = kv_ref[:, HEAD:].T
    for first in range(0, QH, GROUP):
        cols = slice(first * rows, (first + GROUP) * rows)
        att = _mm(values_t, low_ref[:, cols], NN)
        qg = _mm(keys_t, ds_ref[:, cols], NN)
        for i in range(GROUP):
            head = slice((first + i) * HEAD, (first + i + 1) * HEAD)
            att_ref[:, head] = att[:, i * rows : (i + 1) * rows].T.astype(BF16)
            qg_ref[:, head] = qg[:, i * rows : (i + 1) * rows].T.astype(BF16)


def attend(order, docs, q, g, kvs):
    seq_len, rows = kvs[0].shape[0], q.shape[0]
    kv, low, grad_scores, terms = pl.pallas_call(
        functools.partial(terms_kernel, len(kvs), "seq"),
        out_shape=(
            jax.ShapeDtypeStruct((seq_len, 2 * HEAD), BF16),
            jax.ShapeDtypeStruct((seq_len, QH * rows), BF16),
            jax.ShapeDtypeStruct((seq_len, QH * rows), BF16),
            jax.ShapeDtypeStruct((2 * HEAD, seq_len), F32),
        ),
        in_specs=[pl.BlockSpec(memory_space=pltpu.SMEM)] + [VMEM] * (3 + len(kvs)),
        out_specs=[VMEM] * 4,
        compiler_params=LIMIT,
        name="attention_terms",
    )(order, docs, q, g, *kvs)
    attention, query_grad, done = pl.pallas_call(
        outputs_kernel,
        out_shape=[jax.ShapeDtypeStruct(q.shape, BF16)] * 2 + [jax.ShapeDtypeStruct((8, HEAD), F32)],
        in_specs=[VMEM] * 3,
        out_specs=[VMEM] * 3,
        compiler_params=LIMIT,
        name="attention_outputs",
    )(kv, low, grad_scores)
    return attention, query_grad, terms, done


CORE, Y, Z1, Z2 = 1, 2, 4, 8
CHUNKS = 8
CORES = 2
BLOCK = 4


def block_of(device):
    return lax.rem(device // CORES, BLOCK)


def half_cols(device, k, core, far_half, width):
    high = device // (CORES * BLOCK)
    high = 1 - high if far_half else high
    return pl.multiple_of((((block_of(device) ^ k) * CORES + core) * 2 + high) * width, width)


def slice_kernel(wanted, tok_ref, *refs):
    slices, sems = refs[-1 - len(wanted) : -1], refs[-1]
    me = lax.axis_index("dp")
    copies = []
    for (k, halves), ref in zip(wanted, slices):
        width = ref.shape[1] // (CORES * len(halves))
        for n, far_half in enumerate(halves):
            for core in range(CORES):
                copy = pltpu.make_async_copy(
                    tok_ref.at[:, pl.ds(half_cols(me, k, core, far_half, width), width)],
                    ref.at[:, pl.ds((n * CORES + core) * width, width)],
                    sems.at[len(copies)],
                )
                copy.start()
                copies.append(copy)
    for copy in copies:
        copy.wait()


def slice_tokens(tokens, wanted, name, after=()):
    rows, features = tokens.shape
    half = features // (2 * BLOCK)
    return pl.pallas_call(
        functools.partial(slice_kernel, wanted),
        out_shape=[jax.ShapeDtypeStruct((rows, half * len(halves)), BF16) for _, halves in wanted],
        in_specs=[ANY] * (1 + len(after)),
        out_specs=[VMEM] * len(wanted),
        scratch_shapes=[pltpu.SemaphoreType.DMA((sum(2 * len(halves) for _, halves in wanted),))],
        compiler_params=LIMIT,
        name=name,
    )(tokens, *after)


def project_kernel(wanted, tok_ref, w_ref, out_ref, *refs):
    slices, (w_v, w_sems) = refs[:-2], refs[-2:]
    chunk = w_ref.shape[0] // CHUNKS
    loads = []
    for k in range(CHUNKS):
        cut = pl.ds(k * chunk, chunk)
        load = pltpu.make_async_copy(w_ref.at[cut, :], w_v.at[cut, :], w_sems.at[k])
        load.start()
        loads.append(load)
    me = lax.axis_index("dp")
    for (k, halves), ref in zip(wanted, slices):
        width = ref.shape[1] // (CORES * len(halves))
        for n, far_half in enumerate(halves):
            for core in range(CORES):
                first = (n * CORES + core) * width
                source = pl.ds(half_cols(me, k, core, far_half, width), width)
                ref[:, first : first + width] = tok_ref[:, source]
    total = None
    for k, load in enumerate(loads):
        load.wait()
        cut = slice(k * chunk, (k + 1) * chunk)
        term = _mm(tok_ref[:, cut], w_v[cut, :], NN)
        total = term if total is None else total + term
    out_ref[...] = total


def project(tokens, w_kv, wanted):
    rows, features = tokens.shape
    half = features // (2 * BLOCK)
    return pl.pallas_call(
        functools.partial(project_kernel, wanted),
        out_shape=[jax.ShapeDtypeStruct((rows, w_kv.shape[1]), F32)]
        + [jax.ShapeDtypeStruct((rows, half * len(halves)), BF16) for _, halves in wanted],
        in_specs=[VMEM, ANY],
        out_specs=[VMEM] * (1 + len(wanted)),
        scratch_shapes=[
            pltpu.VMEM(w_kv.shape, BF16),
            pltpu.SemaphoreType.DMA((CHUNKS,)),
        ],
        compiler_params=LIMIT,
        name="project",
    )(tokens, w_kv)


def round_kernel(a_ref, b_ref, *refs):
    refs[-1][...] = (a_ref[...] + b_ref[...]).astype(BF16)


def round_grad(a, b, arrived):
    return pl.pallas_call(
        round_kernel,
        out_shape=jax.ShapeDtypeStruct(a.shape, BF16),
        in_specs=[VMEM, VMEM] + [ANY] * len(arrived),
        out_specs=VMEM,
        compiler_params=LIMIT,
        name="round_grad",
    )(a, b, *arrived)


def weight_kernel(packs, starts, *refs):
    toks, grads = refs[:BLOCK], refs[BLOCK : 2 * BLOCK]
    keep_ref, send_ref = refs[2 * BLOCK :]
    width = keep_ref.shape[1]
    starts = [start * width for start in starts]
    core = lax.rem(lax.axis_index("dp"), CORES)
    for ref, which in ((send_ref, 1 - core), (keep_ref, core)):
        acc = None
        for k in range(BLOCK):
            first = pl.multiple_of(starts[k] + which * width, width)
            term = _mm(grads[k][...], toks[k][:, pl.ds(first, width)], NN)
            acc = term if acc is None else acc + term
        ref[...] = acc * (1.0 / packs)


def weight_part(toks, grads, packs, starts):
    part = jax.ShapeDtypeStruct((grads[0].shape[0], toks[-1].shape[1] // CORES), F32)
    return pl.pallas_call(
        functools.partial(weight_kernel, packs, starts),
        out_shape=[part, part],
        in_specs=[VMEM] * (2 * BLOCK),
        out_specs=[VMEM, VMEM],
        compiler_params=LIMIT,
        name="weight_part",
    )(*toks, *grads)


def fold_kernel(a_ref, b_ref, out_ref):
    out_ref[...] = a_ref[...] + b_ref[...]


def fold(a, b):
    return pl.pallas_call(
        fold_kernel,
        out_shape=jax.ShapeDtypeStruct(a.shape, F32),
        in_specs=[VMEM, VMEM],
        out_specs=VMEM,
        compiler_params=LIMIT,
        name="weight_fold",
    )(a, b)


def finish_kernel(a_ref, b_ref, out_ref):
    out_ref[...] = (a_ref[...] + b_ref[...]).T.astype(BF16)


def finish(a, b):
    return pl.pallas_call(
        finish_kernel,
        out_shape=jax.ShapeDtypeStruct((a.shape[1], a.shape[0]), BF16),
        in_specs=[VMEM] * 2,
        out_specs=VMEM,
        compiler_params=LIMIT,
        name="weight_finish",
    )(a, b)


def stack_kernel(count, *refs):
    out_ref = refs[-1]
    first = 0
    for ref in refs[:count]:
        out_ref[first : first + ref.shape[0], :] = ref[...]
        first += ref.shape[0]


def stack(parts, after=()):
    rows = sum(part.shape[0] for part in parts)
    return pl.pallas_call(
        functools.partial(stack_kernel, len(parts)),
        out_shape=jax.ShapeDtypeStruct((rows, parts[0].shape[1]), BF16),
        in_specs=[VMEM] * len(parts) + [ANY] * len(after),
        out_specs=VMEM,
        compiler_params=LIMIT,
        name="stack",
    )(*parts, *after)


def assemble_kernel(held, rows, *refs):
    arrays, out_ref, sems = refs[: len(held)], refs[-2], refs[-1]
    me = lax.axis_index("dp")
    copies = []
    for array, bits in zip(arrays, held):
        for n, bit in enumerate(bits):
            source = me ^ bit
            high = source // (CORES * BLOCK)
            place = (block_of(source) * CORES + lax.rem(source, CORES)) * 2 + high
            first = pl.multiple_of(place * rows, rows)
            copy = pltpu.make_async_copy(
                array.at[pl.ds(n * rows, rows), :],
                out_ref.at[pl.ds(first, rows), :],
                sems.at[len(copies)],
            )
            copy.start()
            copies.append(copy)
    for copy in copies:
        copy.wait()


def assemble(pieces, total, begun=None):
    arrays = [array for array, _ in pieces]
    held = [bits for _, bits in pieces]
    rows = arrays[0].shape[0] // len(held[0])
    count = len(arrays)
    if begun is not None:
        arrays.append(begun)
    return pl.pallas_call(
        functools.partial(assemble_kernel, held, rows),
        out_shape=jax.ShapeDtypeStruct((total * rows, arrays[0].shape[1]), BF16),
        in_specs=[ANY] * len(arrays),
        out_specs=ANY,
        scratch_shapes=[pltpu.SemaphoreType.DMA((sum(len(bits) for bits in held),))],
        input_output_aliases={} if begun is None else {count: 0},
        compiler_params=LIMIT,
        name="weight_assemble" if begun is None else "weight_complete",
    )(*arrays)


def hop(value, bits):
    count = lax.axis_size("dp")
    return lax.ppermute(value, "dp", [(i, i ^ bits) for i in range(count)])


def per_device_16x2(tokens, queries, grad_out, w_kv, doc_ids, span_order):
    dp_size = lax.axis_size("dp")
    rows_dev = queries.shape[1]
    swap = [(0, 1), (1, 0)]
    near = (Y, Z1, Y | Z1)
    flat = tokens[0]
    both = (True, False)
    partial, own, tok_y, tok_z, far_d = project(
        flat, w_kv, [(0, both), (1, both), (2, both), (3, (True,))]
    )
    tok_y, tok_z, far_d = hop(tok_y, Y), hop(tok_z, Z1), hop(far_d, Y | Z1)
    other = lax.ppermute(partial, "seq", swap)
    docs = doc_ids.reshape(-1, rows_dev)
    attention, query_grad, terms, done = attend(
        span_order, docs, queries[0], grad_out[0], [partial, other]
    )
    grad = round_grad(terms, lax.ppermute(terms, "seq", swap), [done, tok_y, tok_z])
    grads = [grad] + [hop(grad, bits) for bits in near]
    keep, send = weight_part([own, tok_y, tok_z, far_d], grads, dp_size, [0, 0, 0, 0])
    part = fold(keep, hop(send, CORE))
    far = hop(part, Z2)
    (near_d,) = slice_tokens(flat, [(3, (False,))], "slice_near_diagonal")
    near_d = hop(near_d, Y | Z1)
    keep, send = weight_part([own, tok_y, tok_z, near_d], grads, dp_size, [2, 2, 2, 0])
    own = finish(fold(keep, far), hop(send, CORE))
    z1, d, y, z2 = hop(own, Z1), hop(own, Y | Z1), hop(own, Y), hop(own, Z2)
    z21, z2y, z2d = hop(z2, Z1), hop(z2, Y), hop(z2, Y | Z1)
    first = hop(stack([own, z1, d, y]), CORE)
    last = hop(stack([z2, z21, z2y, z2d]), CORE)
    pieces = [
        (own, [0]),
        (z1, [Z1]),
        (d, [Y | Z1]),
        (y, [Y]),
        (z2, [Z2]),
        (z21, [Z2 | Z1]),
        (z2y, [Z2 | Y]),
        (z2d, [Z2 | Y | Z1]),
    ]
    held = [[bit | CORE for _, bits in part for bit in bits] for part in (pieces[:4], pieces[4:])]
    weight_grad = assemble(pieces + [(first, held[0])], dp_size)
    weight_grad = assemble([(last, held[1])], dp_size, weight_grad)
    return (attention[None], query_grad[None], weight_grad)


def per_device(tokens, queries, grad_out, w_kv, doc_ids, span_order):
    dp_size = lax.axis_size("dp")
    rows_dev = queries.shape[1]
    flat = tokens[0]
    spread = lax.all_to_all(flat, "dp", split_axis=1, concat_axis=0, tiled=True)
    partial = jnp.dot(flat, w_kv, preferred_element_type=F32)
    own = lax.psum_scatter(partial, "seq", scatter_dimension=0, tiled=True).astype(BF16)
    kvs = [lax.all_gather(own, "seq", axis=0, tiled=True)]
    docs = doc_ids.reshape(-1, rows_dev)
    attention, query_grad, terms, done = attend(span_order, docs, queries[0], grad_out[0], kvs)
    grad_kv = lax.psum(terms.T, "seq").astype(BF16)
    all_grads = lax.all_gather(grad_kv, "dp", axis=0, tiled=True)
    piece = (_mm(spread, all_grads, TN) * (1.0 / dp_size)).astype(BF16)
    weight_grad = lax.all_gather(piece, "dp", axis=0, tiled=True)
    return (attention[None], query_grad[None], weight_grad)


def solution(mesh):
    small = mesh.shape["dp"] == 16 and mesh.shape["seq"] == 2
    return jax.shard_map(
        per_device_16x2 if small else per_device,
        mesh=mesh,
        in_specs=(
            P("dp", None, "seq"),
            P("dp", "seq", None),
            P("dp", "seq", None),
            P("seq", None),
            P("dp", None),
            P(),
        ),
        out_specs=(P("dp", "seq", None), P("dp", "seq", None), P("seq", None)),
        check_vma=False,
    )
```

```python
import functools
import math

import jax
import jax.numpy as jnp
from jax import lax
from jax.experimental import pallas as pl
from jax.experimental.pallas import tpu as pltpu
from jax.sharding import PartitionSpec as P

HEAD = 128
LOG2E = math.log2(math.e)
QH = 8
GROUP = 4
F32 = jnp.float32
BF16 = jnp.bfloat16
NT = (((1,), (1,)), ((), ()))
TN = (((0,), (0,)), ((), ()))
NN = (((1,), (0,)), ((), ()))


def _mm(a, b, dims):
    return lax.dot_general(a, b, dims, preferred_element_type=F32)


ANY = pl.BlockSpec(memory_space=pl.ANY)
VMEM = pl.BlockSpec(memory_space=pltpu.VMEM)
LIMIT = pltpu.CompilerParams(vmem_limit_bytes=48 * 1024 * 1024)


def terms_kernel(parts, own, order_ref, docs_ref, q_ref, g_ref, *refs):
    kv_refs = refs[:parts]
    kv_ref, low_ref, ds_ref, terms_ref = refs[-4:]
    rows = q_ref.shape[0]
    seq_len = kv_refs[0].shape[0]
    spans = seq_len // rows
    if parts == 1:
        kv = kv_refs[0][...]
    else:
        kv = jnp.concatenate(
            [(kv_refs[n][...] + kv_refs[n + 1][...]).astype(BF16) for n in (0, 2)], axis=1
        )
    kv_ref[...] = kv
    keys = kv[:, :HEAD]
    values = kv[:, HEAD:]
    scale = 1.0 / math.sqrt(HEAD)
    me = lax.axis_index(own)

    def row_docs(span):
        return docs_ref[pl.ds(order_ref[span], 1), :]

    masks = []
    q_docs = row_docs(me)
    q_span = order_ref[me]
    q_pos = lax.broadcasted_iota(jnp.int32, (rows, rows), 1)
    k_pos = lax.broadcasted_iota(jnp.int32, (rows, rows), 0)
    for span in range(spans):
        k_docs = jnp.broadcast_to(row_docs(span), (rows, rows)).T
        gap = (order_ref[span] - q_span) * rows
        masks.append((k_pos + gap <= q_pos) & (k_docs == q_docs))
    allowed = jnp.concatenate(masks, axis=0)
    allowed = jnp.concatenate([allowed] * GROUP, axis=1)

    key_grad = jnp.zeros((seq_len, HEAD), F32)
    value_grad = jnp.zeros((seq_len, HEAD), F32)
    for first in range(0, QH, GROUP):
        heads = range(first, first + GROUP)
        q = jnp.concatenate([q_ref[:, h * HEAD : (h + 1) * HEAD] for h in heads], axis=0)
        g = jnp.concatenate([g_ref[:, h * HEAD : (h + 1) * HEAD] for h in heads], axis=0)
        scores = jnp.where(allowed, _mm(keys, q, NT), F32(-1e30))
        expo = jnp.exp2((scores - jnp.max(scores, axis=0, keepdims=True)) * (scale * LOG2E))
        probs = expo * (1.0 / jnp.sum(expo, axis=0, keepdims=True))
        low = probs.astype(BF16)
        grad_probs = _mm(values, g, NT)
        delta = jnp.sum(probs * grad_probs, axis=0, keepdims=True)
        grad_scores = (probs * (grad_probs - delta) * scale).astype(BF16)
        low_ref[:, first * rows : (first + GROUP) * rows] = low
        ds_ref[:, first * rows : (first + GROUP) * rows] = grad_scores
        key_grad += _mm(grad_scores, q, NN)
        value_grad += _mm(low, g, NN)
    terms_ref[:HEAD, :] = key_grad.T
    terms_ref[HEAD:, :] = value_grad.T


def outputs_kernel(kv_ref, low_ref, ds_ref, *refs):
    att_ref, qg_ref, done_ref = refs[-3:]
    rows = att_ref.shape[0]
    done_ref[...] = jnp.zeros_like(done_ref)
    keys_t = kv_ref[:, :HEAD].T
    values_t = kv_ref[:, HEAD:].T
    for first in range(0, QH, GROUP):
        cols = slice(first * rows, (first + GROUP) * rows)
        att = _mm(values_t, low_ref[:, cols], NN)
        qg = _mm(keys_t, ds_ref[:, cols], NN)
        for i in range(GROUP):
            head = slice((first + i) * HEAD, (first + i + 1) * HEAD)
            att_ref[:, head] = att[:, i * rows : (i + 1) * rows].T.astype(BF16)
            qg_ref[:, head] = qg[:, i * rows : (i + 1) * rows].T.astype(BF16)


def attend(order, docs, q, g, kvs, arrived=()):
    seq_len, rows = kvs[0].shape[0], q.shape[0]
    kv, low, grad_scores, terms = pl.pallas_call(
        functools.partial(terms_kernel, len(kvs), "seq"),
        out_shape=(
            jax.ShapeDtypeStruct((seq_len, 2 * HEAD), BF16),
            jax.ShapeDtypeStruct((seq_len, QH * rows), BF16),
            jax.ShapeDtypeStruct((seq_len, QH * rows), BF16),
            jax.ShapeDtypeStruct((2 * HEAD, seq_len), F32),
        ),
        in_specs=[pl.BlockSpec(memory_space=pltpu.SMEM)] + [VMEM] * (3 + len(kvs)),
        out_specs=[VMEM] * 4,
        compiler_params=LIMIT,
        name="attention_terms",
    )(order, docs, q, g, *kvs)
    attention, query_grad, done = pl.pallas_call(
        outputs_kernel,
        out_shape=[jax.ShapeDtypeStruct(q.shape, BF16)] * 2 + [jax.ShapeDtypeStruct((8, HEAD), F32)],
        in_specs=[VMEM] * 3 + [ANY] * len(arrived),
        out_specs=[VMEM] * 3,
        compiler_params=LIMIT,
        name="attention_outputs",
    )(kv, low, grad_scores, *arrived)
    return attention, query_grad, terms, done


CORE, Y, Z1, Z2 = 1, 2, 4, 8
CORES = 2
BLOCK = 4


def block_of(device):
    return lax.rem(device // CORES, BLOCK)


def half_cols(device, k, core, far_half, width):
    high = device // (CORES * BLOCK)
    high = 1 - high if far_half else high
    return pl.multiple_of((((block_of(device) ^ k) * CORES + core) * 2 + high) * width, width)


def slice_kernel(wanted, tok_ref, *refs):
    slices, sems = refs[-1 - len(wanted) : -1], refs[-1]
    me = lax.axis_index("dp")
    copies = []
    for (k, halves), ref in zip(wanted, slices):
        width = ref.shape[1] // (CORES * len(halves))
        for n, far_half in enumerate(halves):
            for core in range(CORES):
                copy = pltpu.make_async_copy(
                    tok_ref.at[:, pl.ds(half_cols(me, k, core, far_half, width), width)],
                    ref.at[:, pl.ds((n * CORES + core) * width, width)],
                    sems.at[len(copies)],
                )
                copy.start()
                copies.append(copy)
    for copy in copies:
        copy.wait()


def slice_tokens(tokens, wanted, name, after=()):
    rows, features = tokens.shape
    half = features // (2 * BLOCK)
    return pl.pallas_call(
        functools.partial(slice_kernel, wanted),
        out_shape=[jax.ShapeDtypeStruct((rows, half * len(halves)), BF16) for _, halves in wanted],
        in_specs=[ANY] * (1 + len(after)),
        out_specs=[VMEM] * len(wanted),
        scratch_shapes=[pltpu.SemaphoreType.DMA((sum(2 * len(halves) for _, halves in wanted),))],
        compiler_params=LIMIT,
        name=name,
    )(tokens, *after)


def project_kernel(tok_ref, w_ref, key_ref, value_ref):
    total = _mm(tok_ref[...], w_ref[...], NN)
    key_ref[...] = total[:, :HEAD]
    value_ref[...] = total[:, HEAD:]


def project(tokens, w_kv):
    half = jax.ShapeDtypeStruct((tokens.shape[0], w_kv.shape[1] // 2), F32)
    return pl.pallas_call(
        project_kernel,
        out_shape=[half, half],
        in_specs=[VMEM, VMEM],
        out_specs=[VMEM, VMEM],
        compiler_params=LIMIT,
        name="project",
    )(tokens, w_kv)


def round_kernel(a_ref, b_ref, *refs):
    refs[-1][...] = (a_ref[...] + b_ref[...]).astype(BF16)


def round_grad(a, b, arrived):
    return pl.pallas_call(
        round_kernel,
        out_shape=jax.ShapeDtypeStruct(a.shape, BF16),
        in_specs=[VMEM, VMEM] + [ANY] * len(arrived),
        out_specs=VMEM,
        compiler_params=LIMIT,
        name="round_grad",
    )(a, b, *arrived)


def weight_kernel(packs, starts, *refs):
    toks, grads = refs[:BLOCK], refs[BLOCK : 2 * BLOCK]
    keep_ref, send_ref = refs[2 * BLOCK :]
    width = keep_ref.shape[1]
    starts = [start * width for start in starts]
    core = lax.rem(lax.axis_index("dp"), CORES)
    for ref, which in ((send_ref, 1 - core), (keep_ref, core)):
        acc = None
        for k in range(BLOCK):
            first = pl.multiple_of(starts[k] + which * width, width)
            term = _mm(grads[k][...], toks[k][:, pl.ds(first, width)], NN)
            acc = term if acc is None else acc + term
        ref[...] = acc * (1.0 / packs)


def weight_part(toks, grads, packs, starts):
    part = jax.ShapeDtypeStruct((grads[0].shape[0], toks[-1].shape[1] // CORES), F32)
    return pl.pallas_call(
        functools.partial(weight_kernel, packs, starts),
        out_shape=[part, part],
        in_specs=[VMEM] * (2 * BLOCK),
        out_specs=[VMEM, VMEM],
        compiler_params=LIMIT,
        name="weight_part",
    )(*toks, *grads)


def fold_kernel(a_ref, b_ref, out_ref):
    out_ref[...] = a_ref[...] + b_ref[...]


def fold(a, b):
    return pl.pallas_call(
        fold_kernel,
        out_shape=jax.ShapeDtypeStruct(a.shape, F32),
        in_specs=[VMEM, VMEM],
        out_specs=VMEM,
        compiler_params=LIMIT,
        name="weight_fold",
    )(a, b)


def finish_kernel(a_ref, b_ref, out_ref):
    out_ref[...] = (a_ref[...] + b_ref[...]).T.astype(BF16)


def finish(a, b):
    return pl.pallas_call(
        finish_kernel,
        out_shape=jax.ShapeDtypeStruct((a.shape[1], a.shape[0]), BF16),
        in_specs=[VMEM] * 2,
        out_specs=VMEM,
        compiler_params=LIMIT,
        name="weight_finish",
    )(a, b)


def stack_kernel(count, *refs):
    out_ref = refs[-1]
    first = 0
    for ref in refs[:count]:
        out_ref[first : first + ref.shape[0], :] = ref[...]
        first += ref.shape[0]


def stack(parts, after=()):
    rows = sum(part.shape[0] for part in parts)
    return pl.pallas_call(
        functools.partial(stack_kernel, len(parts)),
        out_shape=jax.ShapeDtypeStruct((rows, parts[0].shape[1]), BF16),
        in_specs=[VMEM] * len(parts) + [ANY] * len(after),
        out_specs=VMEM,
        compiler_params=LIMIT,
        name="stack",
    )(*parts, *after)


def assemble_kernel(held, rows, *refs):
    arrays, out_ref, sems = refs[: len(held)], refs[-2], refs[-1]
    me = lax.axis_index("dp")
    copies = []
    for array, bits in zip(arrays, held):
        for n, bit in enumerate(bits):
            source = me ^ bit
            high = source // (CORES * BLOCK)
            place = (block_of(source) * CORES + lax.rem(source, CORES)) * 2 + high
            first = pl.multiple_of(place * rows, rows)
            copy = pltpu.make_async_copy(
                array.at[pl.ds(n * rows, rows), :],
                out_ref.at[pl.ds(first, rows), :],
                sems.at[len(copies)],
            )
            copy.start()
            copies.append(copy)
    for copy in copies:
        copy.wait()


def assemble(pieces, total, begun=None):
    arrays = [array for array, _ in pieces]
    held = [bits for _, bits in pieces]
    rows = arrays[0].shape[0] // len(held[0])
    count = len(arrays)
    if begun is not None:
        arrays.append(begun)
    return pl.pallas_call(
        functools.partial(assemble_kernel, held, rows),
        out_shape=jax.ShapeDtypeStruct((total * rows, arrays[0].shape[1]), BF16),
        in_specs=[ANY] * len(arrays),
        out_specs=ANY,
        scratch_shapes=[pltpu.SemaphoreType.DMA((sum(len(bits) for bits in held),))],
        input_output_aliases={} if begun is None else {count: 0},
        compiler_params=LIMIT,
        name="weight_assemble" if begun is None else "weight_complete",
    )(*arrays)


def hop(value, bits):
    count = lax.axis_size("dp")
    return lax.ppermute(value, "dp", [(i, i ^ bits) for i in range(count)])


def per_device_16x2(tokens, queries, grad_out, w_kv, doc_ids, span_order):
    dp_size = lax.axis_size("dp")
    rows_dev = queries.shape[1]
    swap = [(0, 1), (1, 0)]
    near = (Y, Z1, Y | Z1)
    flat = tokens[0]
    both = (True, False)
    own, tok_y, tok_z, far_d = slice_tokens(
        flat, [(0, both), (1, both), (2, both), (3, (True,))], "slice_first"
    )
    tok_y, tok_z, far_d = hop(tok_y, Y), hop(tok_z, Z1), hop(far_d, Y | Z1)
    keys, values = project(flat, w_kv)
    keys_in, values_in = lax.ppermute(keys, "seq", swap), lax.ppermute(values, "seq", swap)
    docs = doc_ids.reshape(-1, rows_dev)
    attention, query_grad, terms, done = attend(
        span_order, docs, queries[0], grad_out[0], [keys, keys_in, values, values_in], [tok_y, tok_z]
    )
    grad = round_grad(terms, lax.ppermute(terms, "seq", swap), [done])
    grads = [grad] + [hop(grad, bits) for bits in near]
    keep, send = weight_part([own, tok_y, tok_z, far_d], grads, dp_size, [0, 0, 0, 0])
    part = fold(keep, hop(send, CORE))
    far = hop(part, Z2)
    (near_d,) = slice_tokens(flat, [(3, (False,))], "slice_near_diagonal")
    near_d = hop(near_d, Y | Z1)
    keep, send = weight_part([own, tok_y, tok_z, near_d], grads, dp_size, [2, 2, 2, 0])
    own = finish(fold(keep, far), hop(send, CORE))
    z1, y, d, z2 = hop(own, Z1), hop(own, Y), hop(own, Y | Z1), hop(own, Z2)
    z21, z2y, z2d = hop(z2, Z1), hop(z2, Y), hop(z2, Y | Z1)
    first = hop(stack([own, z1, y, d]), CORE)
    last = hop(stack([z2, z21, z2y, z2d]), CORE)
    pieces = [
        (own, [0]),
        (z1, [Z1]),
        (y, [Y]),
        (d, [Y | Z1]),
        (z2, [Z2]),
        (z21, [Z2 | Z1]),
        (z2y, [Z2 | Y]),
        (z2d, [Z2 | Y | Z1]),
    ]
    held = [[bit | CORE for _, bits in part for bit in bits] for part in (pieces[:4], pieces[4:])]
    weight_grad = assemble(pieces + [(first, held[0])], dp_size)
    weight_grad = assemble([(last, held[1])], dp_size, weight_grad)
    return (attention[None], query_grad[None], weight_grad)


def per_device(tokens, queries, grad_out, w_kv, doc_ids, span_order):
    dp_size = lax.axis_size("dp")
    rows_dev = queries.shape[1]
    flat = tokens[0]
    spread = lax.all_to_all(flat, "dp", split_axis=1, concat_axis=0, tiled=True)
    partial = jnp.dot(flat, w_kv, preferred_element_type=F32)
    own = lax.psum_scatter(partial, "seq", scatter_dimension=0, tiled=True).astype(BF16)
    kvs = [lax.all_gather(own, "seq", axis=0, tiled=True)]
    docs = doc_ids.reshape(-1, rows_dev)
    attention, query_grad, terms, done = attend(span_order, docs, queries[0], grad_out[0], kvs)
    grad_kv = lax.psum(terms.T, "seq").astype(BF16)
    all_grads = lax.all_gather(grad_kv, "dp", axis=0, tiled=True)
    piece = (_mm(spread, all_grads, TN) * (1.0 / dp_size)).astype(BF16)
    weight_grad = lax.all_gather(piece, "dp", axis=0, tiled=True)
    return (attention[None], query_grad[None], weight_grad)


def solution(mesh):
    small = mesh.shape["dp"] == 16 and mesh.shape["seq"] == 2
    return jax.shard_map(
        per_device_16x2 if small else per_device,
        mesh=mesh,
        in_specs=(
            P("dp", None, "seq"),
            P("dp", "seq", None),
            P("dp", "seq", None),
            P("seq", None),
            P("dp", None),
            P(),
        ),
        out_specs=(P("dp", "seq", None), P("dp", "seq", None), P("seq", None)),
        check_vma=False,
    )
```

```python
import functools
import math

import jax
import jax.numpy as jnp
from jax import lax
from jax.experimental import pallas as pl
from jax.experimental.pallas import tpu as pltpu
from jax.sharding import PartitionSpec as P

HEAD = 128
LOG2E = math.log2(math.e)
QH = 8
GROUP = 8
F32 = jnp.float32
BF16 = jnp.bfloat16
NT = (((1,), (1,)), ((), ()))
TN = (((0,), (0,)), ((), ()))
NN = (((1,), (0,)), ((), ()))


def _mm(a, b, dims):
    return lax.dot_general(a, b, dims, preferred_element_type=F32)


ANY = pl.BlockSpec(memory_space=pl.ANY)
VMEM = pl.BlockSpec(memory_space=pltpu.VMEM)
LIMIT = pltpu.CompilerParams(vmem_limit_bytes=48 * 1024 * 1024)


def terms_kernel(parts, own, order_ref, docs_ref, q_ref, g_ref, *refs):
    kv_refs = refs[:parts]
    kv_ref, low_ref, ds_ref, terms_ref = refs[-4:]
    rows = q_ref.shape[0]
    seq_len = kv_refs[0].shape[0]
    spans = seq_len // rows
    if parts == 1:
        kv = kv_refs[0][...]
    else:
        kv = jnp.concatenate(
            [(kv_refs[n][...] + kv_refs[n + 1][...]).astype(BF16) for n in (0, 2)], axis=1
        )
    kv_ref[...] = kv
    keys = kv[:, :HEAD]
    values = kv[:, HEAD:]
    scale = 1.0 / math.sqrt(HEAD)
    me = lax.axis_index(own)

    def row_docs(span):
        return docs_ref[pl.ds(order_ref[span], 1), :]

    masks = []
    q_docs = row_docs(me)
    q_span = order_ref[me]
    q_pos = lax.broadcasted_iota(jnp.int32, (rows, rows), 1)
    k_pos = lax.broadcasted_iota(jnp.int32, (rows, rows), 0)
    for span in range(spans):
        k_docs = jnp.broadcast_to(row_docs(span), (rows, rows)).T
        gap = (order_ref[span] - q_span) * rows
        masks.append((k_pos + gap <= q_pos) & (k_docs == q_docs))
    allowed = jnp.concatenate(masks, axis=0)
    allowed = jnp.concatenate([allowed] * GROUP, axis=1)

    key_grad = jnp.zeros((seq_len, HEAD), F32)
    value_grad = jnp.zeros((seq_len, HEAD), F32)
    for first in range(0, QH, GROUP):
        heads = range(first, first + GROUP)
        q = jnp.concatenate([q_ref[:, h * HEAD : (h + 1) * HEAD] for h in heads], axis=0)
        g = jnp.concatenate([g_ref[:, h * HEAD : (h + 1) * HEAD] for h in heads], axis=0)
        scores = jnp.where(allowed, _mm(keys, q, NT), F32(-1e30))
        expo = jnp.exp2((scores - jnp.max(scores, axis=0, keepdims=True)) * (scale * LOG2E))
        probs = expo * (1.0 / jnp.sum(expo, axis=0, keepdims=True))
        low = probs.astype(BF16)
        grad_probs = _mm(values, g, NT)
        delta = jnp.sum(probs * grad_probs, axis=0, keepdims=True)
        grad_scores = (probs * (grad_probs - delta) * scale).astype(BF16)
        low_ref[:, first * rows : (first + GROUP) * rows] = low
        ds_ref[:, first * rows : (first + GROUP) * rows] = grad_scores
        key_grad += _mm(grad_scores, q, NN)
        value_grad += _mm(low, g, NN)
    terms_ref[:HEAD, :] = key_grad.T
    terms_ref[HEAD:, :] = value_grad.T


def outputs_kernel(kv_ref, low_ref, ds_ref, *refs):
    att_ref, qg_ref, done_ref = refs[-3:]
    rows = att_ref.shape[0]
    done_ref[...] = jnp.zeros_like(done_ref)
    keys_t = kv_ref[:, :HEAD].T
    values_t = kv_ref[:, HEAD:].T
    for first in range(0, QH, GROUP):
        cols = slice(first * rows, (first + GROUP) * rows)
        att = _mm(values_t, low_ref[:, cols], NN)
        qg = _mm(keys_t, ds_ref[:, cols], NN)
        for i in range(GROUP):
            head = slice((first + i) * HEAD, (first + i + 1) * HEAD)
            att_ref[:, head] = att[:, i * rows : (i + 1) * rows].T.astype(BF16)
            qg_ref[:, head] = qg[:, i * rows : (i + 1) * rows].T.astype(BF16)


def attend(order, docs, q, g, kvs, arrived=()):
    seq_len, rows = kvs[0].shape[0], q.shape[0]
    kv, low, grad_scores, terms = pl.pallas_call(
        functools.partial(terms_kernel, len(kvs), "seq"),
        out_shape=(
            jax.ShapeDtypeStruct((seq_len, 2 * HEAD), BF16),
            jax.ShapeDtypeStruct((seq_len, QH * rows), BF16),
            jax.ShapeDtypeStruct((seq_len, QH * rows), BF16),
            jax.ShapeDtypeStruct((2 * HEAD, seq_len), F32),
        ),
        in_specs=[pl.BlockSpec(memory_space=pltpu.SMEM)] + [VMEM] * (3 + len(kvs)),
        out_specs=[VMEM] * 4,
        compiler_params=LIMIT,
        name="attention_terms",
    )(order, docs, q, g, *kvs)
    attention, query_grad, done = pl.pallas_call(
        outputs_kernel,
        out_shape=[jax.ShapeDtypeStruct(q.shape, BF16)] * 2 + [jax.ShapeDtypeStruct((8, HEAD), F32)],
        in_specs=[VMEM] * 3 + [ANY] * len(arrived),
        out_specs=[VMEM] * 3,
        compiler_params=LIMIT,
        name="attention_outputs",
    )(kv, low, grad_scores, *arrived)
    return attention, query_grad, terms, done


CORE, Y, Z1, Z2 = 1, 2, 4, 8
CORES = 2
BLOCK = 4


def block_of(device):
    return lax.rem(device // CORES, BLOCK)


def half_cols(device, k, core, far_half, width):
    high = device // (CORES * BLOCK)
    high = 1 - high if far_half else high
    return pl.multiple_of((((block_of(device) ^ k) * CORES + core) * 2 + high) * width, width)


def slice_kernel(wanted, tok_ref, *refs):
    slices, sems = refs[-1 - len(wanted) : -1], refs[-1]
    me = lax.axis_index("dp")
    copies = []
    for (k, halves), ref in zip(wanted, slices):
        width = ref.shape[1] // (CORES * len(halves))
        for n, far_half in enumerate(halves):
            for core in range(CORES):
                copy = pltpu.make_async_copy(
                    tok_ref.at[:, pl.ds(half_cols(me, k, core, far_half, width), width)],
                    ref.at[:, pl.ds((n * CORES + core) * width, width)],
                    sems.at[len(copies)],
                )
                copy.start()
                copies.append(copy)
    for copy in copies:
        copy.wait()


def slice_tokens(tokens, wanted, name, after=()):
    rows, features = tokens.shape
    half = features // (2 * BLOCK)
    return pl.pallas_call(
        functools.partial(slice_kernel, wanted),
        out_shape=[jax.ShapeDtypeStruct((rows, half * len(halves)), BF16) for _, halves in wanted],
        in_specs=[ANY] * (1 + len(after)),
        out_specs=[VMEM] * len(wanted),
        scratch_shapes=[pltpu.SemaphoreType.DMA((sum(2 * len(halves) for _, halves in wanted),))],
        compiler_params=LIMIT,
        name=name,
    )(tokens, *after)


def project_kernel(tok_ref, w_ref, key_ref, value_ref):
    total = _mm(tok_ref[...], w_ref[...], NN)
    key_ref[...] = total[:, :HEAD]
    value_ref[...] = total[:, HEAD:]


def project(tokens, w_kv):
    half = jax.ShapeDtypeStruct((tokens.shape[0], w_kv.shape[1] // 2), F32)
    return pl.pallas_call(
        project_kernel,
        out_shape=[half, half],
        in_specs=[VMEM, VMEM],
        out_specs=[VMEM, VMEM],
        compiler_params=LIMIT,
        name="project",
    )(tokens, w_kv)


def round_kernel(a_ref, b_ref, *refs):
    refs[-1][...] = (a_ref[...] + b_ref[...]).astype(BF16)


def round_grad(a, b, arrived):
    return pl.pallas_call(
        round_kernel,
        out_shape=jax.ShapeDtypeStruct(a.shape, BF16),
        in_specs=[VMEM, VMEM] + [ANY] * len(arrived),
        out_specs=VMEM,
        compiler_params=LIMIT,
        name="round_grad",
    )(a, b, *arrived)


def weight_kernel(packs, starts, *refs):
    toks, grads = refs[:BLOCK], refs[BLOCK : 2 * BLOCK]
    keep_ref, send_ref = refs[2 * BLOCK :]
    width = keep_ref.shape[1]
    starts = [start * width for start in starts]
    core = lax.rem(lax.axis_index("dp"), CORES)
    for ref, which in ((send_ref, 1 - core), (keep_ref, core)):
        acc = None
        for k in range(BLOCK):
            first = pl.multiple_of(starts[k] + which * width, width)
            term = _mm(grads[k][...], toks[k][:, pl.ds(first, width)], NN)
            acc = term if acc is None else acc + term
        ref[...] = acc * (1.0 / packs)


def weight_part(toks, grads, packs, starts):
    part = jax.ShapeDtypeStruct((grads[0].shape[0], toks[-1].shape[1] // CORES), F32)
    return pl.pallas_call(
        functools.partial(weight_kernel, packs, starts),
        out_shape=[part, part],
        in_specs=[VMEM] * (2 * BLOCK),
        out_specs=[VMEM, VMEM],
        compiler_params=LIMIT,
        name="weight_part",
    )(*toks, *grads)


def fold_kernel(a_ref, b_ref, out_ref):
    out_ref[...] = a_ref[...] + b_ref[...]


def fold(a, b):
    return pl.pallas_call(
        fold_kernel,
        out_shape=jax.ShapeDtypeStruct(a.shape, F32),
        in_specs=[VMEM, VMEM],
        out_specs=VMEM,
        compiler_params=LIMIT,
        name="weight_fold",
    )(a, b)


def finish_kernel(a_ref, b_ref, out_ref):
    out_ref[...] = (a_ref[...] + b_ref[...]).T.astype(BF16)


def finish(a, b):
    return pl.pallas_call(
        finish_kernel,
        out_shape=jax.ShapeDtypeStruct((a.shape[1], a.shape[0]), BF16),
        in_specs=[VMEM] * 2,
        out_specs=VMEM,
        compiler_params=LIMIT,
        name="weight_finish",
    )(a, b)


def stack_kernel(count, *refs):
    out_ref = refs[-1]
    first = 0
    for ref in refs[:count]:
        out_ref[first : first + ref.shape[0], :] = ref[...]
        first += ref.shape[0]


def stack(parts, after=()):
    rows = sum(part.shape[0] for part in parts)
    return pl.pallas_call(
        functools.partial(stack_kernel, len(parts)),
        out_shape=jax.ShapeDtypeStruct((rows, parts[0].shape[1]), BF16),
        in_specs=[VMEM] * len(parts) + [ANY] * len(after),
        out_specs=VMEM,
        compiler_params=LIMIT,
        name="stack",
    )(*parts, *after)


def assemble_kernel(held, rows, *refs):
    arrays, out_ref, sems = refs[: len(held)], refs[-2], refs[-1]
    me = lax.axis_index("dp")
    copies = []
    for array, bits in zip(arrays, held):
        for n, bit in enumerate(bits):
            source = me ^ bit
            high = source // (CORES * BLOCK)
            place = (block_of(source) * CORES + lax.rem(source, CORES)) * 2 + high
            first = pl.multiple_of(place * rows, rows)
            copy = pltpu.make_async_copy(
                array.at[pl.ds(n * rows, rows), :],
                out_ref.at[pl.ds(first, rows), :],
                sems.at[len(copies)],
            )
            copy.start()
            copies.append(copy)
    for copy in copies:
        copy.wait()


def assemble(pieces, total, begun=None):
    arrays = [array for array, _ in pieces]
    held = [bits for _, bits in pieces]
    rows = arrays[0].shape[0] // len(held[0])
    count = len(arrays)
    if begun is not None:
        arrays.append(begun)
    return pl.pallas_call(
        functools.partial(assemble_kernel, held, rows),
        out_shape=jax.ShapeDtypeStruct((total * rows, arrays[0].shape[1]), BF16),
        in_specs=[ANY] * len(arrays),
        out_specs=ANY,
        scratch_shapes=[pltpu.SemaphoreType.DMA((sum(len(bits) for bits in held),))],
        input_output_aliases={} if begun is None else {count: 0},
        compiler_params=LIMIT,
        name="weight_assemble" if begun is None else "weight_complete",
    )(*arrays)


def hop(value, bits):
    count = lax.axis_size("dp")
    return lax.ppermute(value, "dp", [(i, i ^ bits) for i in range(count)])


def per_device_16x2(tokens, queries, grad_out, w_kv, doc_ids, span_order):
    dp_size = lax.axis_size("dp")
    rows_dev = queries.shape[1]
    swap = [(0, 1), (1, 0)]
    near = (Y, Z1, Y | Z1)
    flat = tokens[0]
    both = (True, False)
    own, tok_y, tok_z, far_d = slice_tokens(
        flat, [(0, both), (1, both), (2, both), (3, (True,))], "slice_first"
    )
    tok_y, tok_z, far_d = hop(tok_y, Y), hop(tok_z, Z1), hop(far_d, Y | Z1)
    keys, values = project(flat, w_kv)
    keys_in, values_in = lax.ppermute(keys, "seq", swap), lax.ppermute(values, "seq", swap)
    docs = doc_ids.reshape(-1, rows_dev)
    attention, query_grad, terms, done = attend(
        span_order, docs, queries[0], grad_out[0], [keys, keys_in, values, values_in], [tok_y, tok_z]
    )
    grad = round_grad(terms, lax.ppermute(terms, "seq", swap), [done])
    grads = [grad] + [hop(grad, bits) for bits in near]
    keep, send = weight_part([own, tok_y, tok_z, far_d], grads, dp_size, [0, 0, 0, 0])
    part = fold(keep, hop(send, CORE))
    far = hop(part, Z2)
    (near_d,) = slice_tokens(flat, [(3, (False,))], "slice_near_diagonal")
    near_d = hop(near_d, Y | Z1)
    keep, send = weight_part([own, tok_y, tok_z, near_d], grads, dp_size, [2, 2, 2, 0])
    own = finish(fold(keep, far), hop(send, CORE))
    z1, y, d, z2 = hop(own, Z1), hop(own, Y), hop(own, Y | Z1), hop(own, Z2)
    z21, z2y, z2d = hop(z2, Z1), hop(z2, Y), hop(z2, Y | Z1)
    first = hop(stack([own, z1, y, d]), CORE)
    last = hop(stack([z2, z21, z2y, z2d]), CORE)
    pieces = [
        (own, [0]),
        (z1, [Z1]),
        (y, [Y]),
        (d, [Y | Z1]),
        (z2, [Z2]),
        (z21, [Z2 | Z1]),
        (z2y, [Z2 | Y]),
        (z2d, [Z2 | Y | Z1]),
    ]
    held = [[bit | CORE for _, bits in part for bit in bits] for part in (pieces[:4], pieces[4:])]
    weight_grad = assemble(pieces + [(first, held[0])], dp_size)
    weight_grad = assemble([(last, held[1])], dp_size, weight_grad)
    return (attention[None], query_grad[None], weight_grad)


def per_device(tokens, queries, grad_out, w_kv, doc_ids, span_order):
    dp_size = lax.axis_size("dp")
    rows_dev = queries.shape[1]
    flat = tokens[0]
    spread = lax.all_to_all(flat, "dp", split_axis=1, concat_axis=0, tiled=True)
    partial = jnp.dot(flat, w_kv, preferred_element_type=F32)
    own = lax.psum_scatter(partial, "seq", scatter_dimension=0, tiled=True).astype(BF16)
    kvs = [lax.all_gather(own, "seq", axis=0, tiled=True)]
    docs = doc_ids.reshape(-1, rows_dev)
    attention, query_grad, terms, done = attend(span_order, docs, queries[0], grad_out[0], kvs)
    grad_kv = lax.psum(terms.T, "seq").astype(BF16)
    all_grads = lax.all_gather(grad_kv, "dp", axis=0, tiled=True)
    piece = (_mm(spread, all_grads, TN) * (1.0 / dp_size)).astype(BF16)
    weight_grad = lax.all_gather(piece, "dp", axis=0, tiled=True)
    return (attention[None], query_grad[None], weight_grad)


def solution(mesh):
    small = mesh.shape["dp"] == 16 and mesh.shape["seq"] == 2
    return jax.shard_map(
        per_device_16x2 if small else per_device,
        mesh=mesh,
        in_specs=(
            P("dp", None, "seq"),
            P("dp", "seq", None),
            P("dp", "seq", None),
            P("seq", None),
            P("dp", None),
            P(),
        ),
        out_specs=(P("dp", "seq", None), P("dp", "seq", None), P("seq", None)),
        check_vma=False,
    )
```

```python
import functools
import math

import jax
import jax.numpy as jnp
from jax import lax
from jax.experimental import pallas as pl
from jax.experimental.pallas import tpu as pltpu
from jax.sharding import PartitionSpec as P

HEAD = 128
LOG2E = math.log2(math.e)
QH = 8
GROUP = 8
F32 = jnp.float32
BF16 = jnp.bfloat16
NT = (((1,), (1,)), ((), ()))
TN = (((0,), (0,)), ((), ()))
NN = (((1,), (0,)), ((), ()))


def _mm(a, b, dims):
    return lax.dot_general(a, b, dims, preferred_element_type=F32)


ANY = pl.BlockSpec(memory_space=pl.ANY)
VMEM = pl.BlockSpec(memory_space=pltpu.VMEM)
LIMIT = pltpu.CompilerParams(vmem_limit_bytes=48 * 1024 * 1024)


def terms_kernel(parts, own, order_ref, docs_ref, q_ref, g_ref, *refs):
    kv_refs = refs[:parts]
    kv_ref, low_ref, ds_ref, terms_ref = refs[-4:]
    rows = q_ref.shape[0]
    seq_len = kv_refs[0].shape[0]
    spans = seq_len // rows
    if parts == 1:
        kv = kv_refs[0][...]
    else:
        kv = jnp.concatenate(
            [(kv_refs[n][...] + kv_refs[n + 1][...]).astype(BF16) for n in (0, 2)], axis=1
        )
    kv_ref[...] = kv
    keys = kv[:, :HEAD]
    values = kv[:, HEAD:]
    scale = 1.0 / math.sqrt(HEAD)
    me = lax.axis_index(own)

    def row_docs(span):
        return docs_ref[pl.ds(order_ref[span], 1), :]

    masks = []
    q_docs = row_docs(me)
    q_span = order_ref[me]
    q_pos = lax.broadcasted_iota(jnp.int32, (rows, rows), 1)
    k_pos = lax.broadcasted_iota(jnp.int32, (rows, rows), 0)
    for span in range(spans):
        k_docs = jnp.broadcast_to(row_docs(span), (rows, rows)).T
        gap = (order_ref[span] - q_span) * rows
        masks.append((k_pos + gap <= q_pos) & (k_docs == q_docs))
    allowed = jnp.concatenate(masks, axis=0)
    allowed = jnp.concatenate([allowed] * GROUP, axis=1)

    key_grad = jnp.zeros((seq_len, HEAD), F32)
    value_grad = jnp.zeros((seq_len, HEAD), F32)
    for first in range(0, QH, GROUP):
        heads = range(first, first + GROUP)
        q = jnp.concatenate([q_ref[:, h * HEAD : (h + 1) * HEAD] for h in heads], axis=0)
        g = jnp.concatenate([g_ref[:, h * HEAD : (h + 1) * HEAD] for h in heads], axis=0)
        scores = jnp.where(allowed, _mm(keys, q, NT), F32(-1e30))
        expo = jnp.exp2((scores - jnp.max(scores, axis=0, keepdims=True)) * (scale * LOG2E))
        probs = expo * (1.0 / jnp.sum(expo, axis=0, keepdims=True))
        low = probs.astype(BF16)
        grad_probs = _mm(values, g, NT)
        delta = jnp.sum(probs * grad_probs, axis=0, keepdims=True)
        grad_scores = (probs * (grad_probs - delta) * scale).astype(BF16)
        low_ref[:, first * rows : (first + GROUP) * rows] = low
        ds_ref[:, first * rows : (first + GROUP) * rows] = grad_scores
        key_grad += _mm(grad_scores, q, NN)
        value_grad += _mm(low, g, NN)
    terms_ref[:HEAD, :] = key_grad.T
    terms_ref[HEAD:, :] = value_grad.T


def outputs_kernel(kv_ref, low_ref, ds_ref, *refs):
    att_ref, qg_ref, done_ref = refs[-3:]
    rows = att_ref.shape[0]
    done_ref[...] = jnp.zeros_like(done_ref)
    keys_t = kv_ref[:, :HEAD].T
    values_t = kv_ref[:, HEAD:].T
    for first in range(0, QH, GROUP):
        cols = slice(first * rows, (first + GROUP) * rows)
        att = _mm(values_t, low_ref[:, cols], NN)
        qg = _mm(keys_t, ds_ref[:, cols], NN)
        for i in range(GROUP):
            head = slice((first + i) * HEAD, (first + i + 1) * HEAD)
            att_ref[:, head] = att[:, i * rows : (i + 1) * rows].T.astype(BF16)
            qg_ref[:, head] = qg[:, i * rows : (i + 1) * rows].T.astype(BF16)


def attend(order, docs, q, g, kvs, arrived=()):
    seq_len, rows = kvs[0].shape[0], q.shape[0]
    kv, low, grad_scores, terms = pl.pallas_call(
        functools.partial(terms_kernel, len(kvs), "seq"),
        out_shape=(
            jax.ShapeDtypeStruct((seq_len, 2 * HEAD), BF16),
            jax.ShapeDtypeStruct((seq_len, QH * rows), BF16),
            jax.ShapeDtypeStruct((seq_len, QH * rows), BF16),
            jax.ShapeDtypeStruct((2 * HEAD, seq_len), F32),
        ),
        in_specs=[pl.BlockSpec(memory_space=pltpu.SMEM)] + [VMEM] * (3 + len(kvs)),
        out_specs=[VMEM] * 4,
        compiler_params=LIMIT,
        name="attention_terms",
    )(order, docs, q, g, *kvs)
    attention, query_grad, done = pl.pallas_call(
        outputs_kernel,
        out_shape=[jax.ShapeDtypeStruct(q.shape, BF16)] * 2 + [jax.ShapeDtypeStruct((8, HEAD), F32)],
        in_specs=[VMEM] * 3 + [ANY] * len(arrived),
        out_specs=[VMEM] * 3,
        compiler_params=LIMIT,
        name="attention_outputs",
    )(kv, low, grad_scores, *arrived)
    return attention, query_grad, terms, done


CORE, Y, Z1, Z2 = 1, 2, 4, 8
CORES = 2
BLOCK = 4


def block_of(device):
    return lax.rem(device // CORES, BLOCK)


def half_cols(device, k, core, far_half, width):
    high = device // (CORES * BLOCK)
    high = 1 - high if far_half else high
    return pl.multiple_of((((block_of(device) ^ k) * CORES + core) * 2 + high) * width, width)


def slice_kernel(wanted, tok_ref, *refs):
    slices, sems = refs[-1 - len(wanted) : -1], refs[-1]
    me = lax.axis_index("dp")
    copies = []
    for (k, halves), ref in zip(wanted, slices):
        width = ref.shape[1] // (CORES * len(halves))
        for n, far_half in enumerate(halves):
            for core in range(CORES):
                copy = pltpu.make_async_copy(
                    tok_ref.at[:, pl.ds(half_cols(me, k, core, far_half, width), width)],
                    ref.at[:, pl.ds((n * CORES + core) * width, width)],
                    sems.at[len(copies)],
                )
                copy.start()
                copies.append(copy)
    for copy in copies:
        copy.wait()


def slice_tokens(tokens, wanted, name, after=()):
    rows, features = tokens.shape
    half = features // (2 * BLOCK)
    return pl.pallas_call(
        functools.partial(slice_kernel, wanted),
        out_shape=[jax.ShapeDtypeStruct((rows, half * len(halves)), BF16) for _, halves in wanted],
        in_specs=[ANY] * (1 + len(after)),
        out_specs=[VMEM] * len(wanted),
        scratch_shapes=[pltpu.SemaphoreType.DMA((sum(2 * len(halves) for _, halves in wanted),))],
        compiler_params=LIMIT,
        name=name,
    )(tokens, *after)


def project_kernel(tok_ref, w_ref, key_ref, value_ref):
    total = _mm(tok_ref[...], w_ref[...], NN)
    key_ref[...] = total[:, :HEAD]
    value_ref[...] = total[:, HEAD:]


def project(tokens, w_kv):
    half = jax.ShapeDtypeStruct((tokens.shape[0], w_kv.shape[1] // 2), F32)
    return pl.pallas_call(
        project_kernel,
        out_shape=[half, half],
        in_specs=[VMEM, VMEM],
        out_specs=[VMEM, VMEM],
        compiler_params=LIMIT,
        name="project",
    )(tokens, w_kv)


def round_kernel(a_ref, b_ref, *refs):
    refs[-1][...] = (a_ref[...] + b_ref[...]).astype(BF16)


def round_grad(a, b, arrived):
    return pl.pallas_call(
        round_kernel,
        out_shape=jax.ShapeDtypeStruct(a.shape, BF16),
        in_specs=[VMEM, VMEM] + [ANY] * len(arrived),
        out_specs=VMEM,
        compiler_params=LIMIT,
        name="round_grad",
    )(a, b, *arrived)


def weight_kernel(packs, starts, *refs):
    toks, grads = refs[:BLOCK], refs[BLOCK : 2 * BLOCK]
    keep_ref, send_ref = refs[2 * BLOCK :]
    width = keep_ref.shape[1]
    starts = [start * width for start in starts]
    core = lax.rem(lax.axis_index("dp"), CORES)
    for ref, which in ((send_ref, 1 - core), (keep_ref, core)):
        acc = None
        for k in range(BLOCK):
            first = pl.multiple_of(starts[k] + which * width, width)
            term = _mm(grads[k][...], toks[k][:, pl.ds(first, width)], NN)
            acc = term if acc is None else acc + term
        ref[...] = acc * (1.0 / packs)


def weight_part(toks, grads, packs, starts):
    part = jax.ShapeDtypeStruct((grads[0].shape[0], toks[-1].shape[1] // CORES), F32)
    return pl.pallas_call(
        functools.partial(weight_kernel, packs, starts),
        out_shape=[part, part],
        in_specs=[VMEM] * (2 * BLOCK),
        out_specs=[VMEM, VMEM],
        compiler_params=LIMIT,
        name="weight_part",
    )(*toks, *grads)


def fold_kernel(a_ref, b_ref, out_ref):
    out_ref[...] = a_ref[...] + b_ref[...]


def fold(a, b):
    return pl.pallas_call(
        fold_kernel,
        out_shape=jax.ShapeDtypeStruct(a.shape, F32),
        in_specs=[VMEM, VMEM],
        out_specs=VMEM,
        compiler_params=LIMIT,
        name="weight_fold",
    )(a, b)


def finish_kernel(a_ref, b_ref, out_ref):
    out_ref[...] = (a_ref[...] + b_ref[...]).T.astype(BF16)


def finish(a, b):
    return pl.pallas_call(
        finish_kernel,
        out_shape=jax.ShapeDtypeStruct((a.shape[1], a.shape[0]), BF16),
        in_specs=[VMEM] * 2,
        out_specs=VMEM,
        compiler_params=LIMIT,
        name="weight_finish",
    )(a, b)


def stack_kernel(count, *refs):
    out_ref = refs[-1]
    first = 0
    for ref in refs[:count]:
        out_ref[first : first + ref.shape[0], :] = ref[...]
        first += ref.shape[0]


def stack(parts, after=()):
    rows = sum(part.shape[0] for part in parts)
    return pl.pallas_call(
        functools.partial(stack_kernel, len(parts)),
        out_shape=jax.ShapeDtypeStruct((rows, parts[0].shape[1]), BF16),
        in_specs=[VMEM] * len(parts) + [ANY] * len(after),
        out_specs=VMEM,
        compiler_params=LIMIT,
        name="stack",
    )(*parts, *after)


def assemble_kernel(held, rows, *refs):
    arrays, out_ref, sems = refs[: len(held)], refs[-2], refs[-1]
    me = lax.axis_index("dp")
    copies = []
    for array, bits in zip(arrays, held):
        for n, bit in enumerate(bits):
            source = me ^ bit
            high = source // (CORES * BLOCK)
            place = (block_of(source) * CORES + lax.rem(source, CORES)) * 2 + high
            first = pl.multiple_of(place * rows, rows)
            copy = pltpu.make_async_copy(
                array.at[pl.ds(n * rows, rows), :],
                out_ref.at[pl.ds(first, rows), :],
                sems.at[len(copies)],
            )
            copy.start()
            copies.append(copy)
    for copy in copies:
        copy.wait()


def assemble(pieces, total, begun=None):
    arrays = [array for array, _ in pieces]
    held = [bits for _, bits in pieces]
    rows = arrays[0].shape[0] // len(held[0])
    count = len(arrays)
    if begun is not None:
        arrays.append(begun)
    return pl.pallas_call(
        functools.partial(assemble_kernel, held, rows),
        out_shape=jax.ShapeDtypeStruct((total * rows, arrays[0].shape[1]), BF16),
        in_specs=[ANY] * len(arrays),
        out_specs=ANY,
        scratch_shapes=[pltpu.SemaphoreType.DMA((sum(len(bits) for bits in held),))],
        input_output_aliases={} if begun is None else {count: 0},
        compiler_params=LIMIT,
        name="weight_assemble" if begun is None else "weight_complete",
    )(*arrays)


def hop(value, bits):
    count = lax.axis_size("dp")
    return lax.ppermute(value, "dp", [(i, i ^ bits) for i in range(count)])


def per_device_16x2(tokens, queries, grad_out, w_kv, doc_ids, span_order):
    dp_size = lax.axis_size("dp")
    rows_dev = queries.shape[1]
    swap = [(0, 1), (1, 0)]
    near = (Y, Z1, Y | Z1)
    flat = tokens[0]
    both = (True, False)
    own, tok_y, tok_z, far_d = slice_tokens(
        flat, [(0, both), (1, both), (2, both), (3, (True,))], "slice_first"
    )
    tok_y, tok_z, far_d = hop(tok_y, Y), hop(tok_z, Z1), hop(far_d, Y | Z1)
    keys, values = project(flat, w_kv)
    keys_in, values_in = lax.ppermute(keys, "seq", swap), lax.ppermute(values, "seq", swap)
    docs = doc_ids.reshape(-1, rows_dev)
    attention, query_grad, terms, done = attend(
        span_order, docs, queries[0], grad_out[0], [keys, keys_in, values, values_in], [tok_y]
    )
    grad = round_grad(terms, lax.ppermute(terms, "seq", swap), [done, tok_z])
    grads = [grad] + [hop(grad, bits) for bits in near]
    keep, send = weight_part([own, tok_y, tok_z, far_d], grads, dp_size, [0, 0, 0, 0])
    part = fold(keep, hop(send, CORE))
    far = hop(part, Z2)
    (near_d,) = slice_tokens(flat, [(3, (False,))], "slice_near_diagonal")
    near_d = hop(near_d, Y | Z1)
    keep, send = weight_part([own, tok_y, tok_z, near_d], grads, dp_size, [2, 2, 2, 0])
    own = finish(fold(keep, far), hop(send, CORE))
    z1, y, d, z2 = hop(own, Z1), hop(own, Y), hop(own, Y | Z1), hop(own, Z2)
    z21, z2y, z2d = hop(z2, Z1), hop(z2, Y), hop(z2, Y | Z1)
    first = hop(stack([own, z1, y, d]), CORE)
    last = hop(stack([z2, z21, z2y, z2d]), CORE)
    pieces = [
        (own, [0]),
        (z1, [Z1]),
        (y, [Y]),
        (d, [Y | Z1]),
        (z2, [Z2]),
        (z21, [Z2 | Z1]),
        (z2y, [Z2 | Y]),
        (z2d, [Z2 | Y | Z1]),
    ]
    held = [[bit | CORE for _, bits in part for bit in bits] for part in (pieces[:4], pieces[4:])]
    weight_grad = assemble(pieces + [(first, held[0])], dp_size)
    weight_grad = assemble([(last, held[1])], dp_size, weight_grad)
    return (attention[None], query_grad[None], weight_grad)


def per_device(tokens, queries, grad_out, w_kv, doc_ids, span_order):
    dp_size = lax.axis_size("dp")
    rows_dev = queries.shape[1]
    flat = tokens[0]
    spread = lax.all_to_all(flat, "dp", split_axis=1, concat_axis=0, tiled=True)
    partial = jnp.dot(flat, w_kv, preferred_element_type=F32)
    own = lax.psum_scatter(partial, "seq", scatter_dimension=0, tiled=True).astype(BF16)
    kvs = [lax.all_gather(own, "seq", axis=0, tiled=True)]
    docs = doc_ids.reshape(-1, rows_dev)
    attention, query_grad, terms, done = attend(span_order, docs, queries[0], grad_out[0], kvs)
    grad_kv = lax.psum(terms.T, "seq").astype(BF16)
    all_grads = lax.all_gather(grad_kv, "dp", axis=0, tiled=True)
    piece = (_mm(spread, all_grads, TN) * (1.0 / dp_size)).astype(BF16)
    weight_grad = lax.all_gather(piece, "dp", axis=0, tiled=True)
    return (attention[None], query_grad[None], weight_grad)


def solution(mesh):
    small = mesh.shape["dp"] == 16 and mesh.shape["seq"] == 2
    return jax.shard_map(
        per_device_16x2 if small else per_device,
        mesh=mesh,
        in_specs=(
            P("dp", None, "seq"),
            P("dp", "seq", None),
            P("dp", "seq", None),
            P("seq", None),
            P("dp", None),
            P(),
        ),
        out_specs=(P("dp", "seq", None), P("dp", "seq", None), P("seq", None)),
        check_vma=False,
    )
```

```python
import functools
import math

import jax
import jax.numpy as jnp
from jax import lax
from jax.experimental import pallas as pl
from jax.experimental.pallas import tpu as pltpu
from jax.sharding import PartitionSpec as P

HEAD = 128
LOG2E = math.log2(math.e)
QH = 8
GROUP = 8
F32 = jnp.float32
BF16 = jnp.bfloat16
NT = (((1,), (1,)), ((), ()))
TN = (((0,), (0,)), ((), ()))
NN = (((1,), (0,)), ((), ()))


def _mm(a, b, dims):
    return lax.dot_general(a, b, dims, preferred_element_type=F32)


ANY = pl.BlockSpec(memory_space=pl.ANY)
VMEM = pl.BlockSpec(memory_space=pltpu.VMEM)
LIMIT = pltpu.CompilerParams(vmem_limit_bytes=48 * 1024 * 1024)


def terms_kernel(parts, own, order_ref, docs_ref, q_ref, g_ref, *refs):
    kv_refs = refs[:parts]
    kv_ref, low_ref, ds_ref, terms_ref = refs[-4:]
    rows = q_ref.shape[0]
    seq_len = kv_refs[0].shape[0]
    spans = seq_len // rows
    if parts == 1:
        kv = kv_refs[0][...]
    else:
        kv = jnp.concatenate(
            [(kv_refs[n][...] + kv_refs[n + 1][...]).astype(BF16) for n in (0, 2)], axis=1
        )
    kv_ref[...] = kv
    keys = kv[:, :HEAD]
    values = kv[:, HEAD:]
    scale = 1.0 / math.sqrt(HEAD)
    me = lax.axis_index(own)

    def row_docs(span):
        return docs_ref[pl.ds(order_ref[span], 1), :]

    masks = []
    q_docs = row_docs(me)
    q_span = order_ref[me]
    q_pos = lax.broadcasted_iota(jnp.int32, (rows, rows), 1)
    k_pos = lax.broadcasted_iota(jnp.int32, (rows, rows), 0)
    for span in range(spans):
        k_docs = jnp.broadcast_to(row_docs(span), (rows, rows)).T
        gap = (order_ref[span] - q_span) * rows
        masks.append((k_pos + gap <= q_pos) & (k_docs == q_docs))
    allowed = jnp.concatenate(masks, axis=0)
    allowed = jnp.concatenate([allowed] * GROUP, axis=1)

    key_grad = jnp.zeros((seq_len, HEAD), F32)
    value_grad = jnp.zeros((seq_len, HEAD), F32)
    for first in range(0, QH, GROUP):
        heads = range(first, first + GROUP)
        q = jnp.concatenate([q_ref[:, h * HEAD : (h + 1) * HEAD] for h in heads], axis=0)
        g = jnp.concatenate([g_ref[:, h * HEAD : (h + 1) * HEAD] for h in heads], axis=0)
        scores = jnp.where(allowed, _mm(keys, q, NT), F32(-1e30))
        expo = jnp.exp2((scores - jnp.max(scores, axis=0, keepdims=True)) * (scale * LOG2E))
        probs = expo * (1.0 / jnp.sum(expo, axis=0, keepdims=True))
        low = probs.astype(BF16)
        grad_probs = _mm(values, g, NT)
        delta = jnp.sum(probs * grad_probs, axis=0, keepdims=True)
        grad_scores = (probs * (grad_probs - delta) * scale).astype(BF16)
        low_ref[:, first * rows : (first + GROUP) * rows] = low
        ds_ref[:, first * rows : (first + GROUP) * rows] = grad_scores
        key_grad += _mm(grad_scores, q, NN)
        value_grad += _mm(low, g, NN)
    terms_ref[:HEAD, :] = key_grad.T
    terms_ref[HEAD:, :] = value_grad.T


def outputs_kernel(kv_ref, low_ref, ds_ref, *refs):
    att_ref, qg_ref, done_ref = refs[-3:]
    rows = att_ref.shape[0]
    done_ref[...] = jnp.zeros_like(done_ref)
    keys_t = kv_ref[:, :HEAD].T
    values_t = kv_ref[:, HEAD:].T
    for first in range(0, QH, GROUP):
        cols = slice(first * rows, (first + GROUP) * rows)
        att = _mm(values_t, low_ref[:, cols], NN)
        qg = _mm(keys_t, ds_ref[:, cols], NN)
        for i in range(GROUP):
            head = slice((first + i) * HEAD, (first + i + 1) * HEAD)
            att_ref[:, head] = att[:, i * rows : (i + 1) * rows].T.astype(BF16)
            qg_ref[:, head] = qg[:, i * rows : (i + 1) * rows].T.astype(BF16)


def attend(order, docs, q, g, kvs, arrived=()):
    seq_len, rows = kvs[0].shape[0], q.shape[0]
    kv, low, grad_scores, terms = pl.pallas_call(
        functools.partial(terms_kernel, len(kvs), "seq"),
        out_shape=(
            jax.ShapeDtypeStruct((seq_len, 2 * HEAD), BF16),
            jax.ShapeDtypeStruct((seq_len, QH * rows), BF16),
            jax.ShapeDtypeStruct((seq_len, QH * rows), BF16),
            jax.ShapeDtypeStruct((2 * HEAD, seq_len), F32),
        ),
        in_specs=[pl.BlockSpec(memory_space=pltpu.SMEM)] + [VMEM] * (3 + len(kvs)),
        out_specs=[VMEM] * 4,
        compiler_params=LIMIT,
        name="attention_terms",
    )(order, docs, q, g, *kvs)
    attention, query_grad, done = pl.pallas_call(
        outputs_kernel,
        out_shape=[jax.ShapeDtypeStruct(q.shape, BF16)] * 2 + [jax.ShapeDtypeStruct((8, HEAD), F32)],
        in_specs=[VMEM] * 3 + [ANY] * len(arrived),
        out_specs=[VMEM] * 3,
        compiler_params=LIMIT,
        name="attention_outputs",
    )(kv, low, grad_scores, *arrived)
    return attention, query_grad, terms, done


CORE, Y, Z1, Z2 = 1, 2, 4, 8
CORES = 2
BLOCK = 4


def block_of(device):
    return lax.rem(device // CORES, BLOCK)


def half_cols(device, k, core, far_half, width):
    high = device // (CORES * BLOCK)
    high = 1 - high if far_half else high
    return pl.multiple_of((((block_of(device) ^ k) * CORES + core) * 2 + high) * width, width)


def slice_kernel(wanted, tok_ref, *slices):
    me = lax.axis_index("dp")
    for (k, halves), ref in zip(wanted, slices):
        width = ref.shape[1] // (CORES * len(halves))
        for n, far_half in enumerate(halves):
            for core in range(CORES):
                first = (n * CORES + core) * width
                source = pl.ds(half_cols(me, k, core, far_half, width), width)
                ref[:, first : first + width] = tok_ref[:, source]


def slice_tokens(tokens, wanted, name):
    rows, features = tokens.shape
    half = features // (2 * BLOCK)
    return pl.pallas_call(
        functools.partial(slice_kernel, wanted),
        out_shape=[jax.ShapeDtypeStruct((rows, half * len(halves)), BF16) for _, halves in wanted],
        in_specs=[VMEM],
        out_specs=[VMEM] * len(wanted),
        compiler_params=LIMIT,
        name=name,
    )(tokens)


def project_kernel(tok_ref, w_ref, key_ref, value_ref):
    total = _mm(tok_ref[...], w_ref[...], NN)
    key_ref[...] = total[:, :HEAD]
    value_ref[...] = total[:, HEAD:]


def project(tokens, w_kv):
    half = jax.ShapeDtypeStruct((tokens.shape[0], w_kv.shape[1] // 2), F32)
    return pl.pallas_call(
        project_kernel,
        out_shape=[half, half],
        in_specs=[VMEM, VMEM],
        out_specs=[VMEM, VMEM],
        compiler_params=LIMIT,
        name="project",
    )(tokens, w_kv)


def round_kernel(a_ref, b_ref, *refs):
    refs[-1][...] = (a_ref[...] + b_ref[...]).astype(BF16)


def round_grad(a, b, arrived):
    return pl.pallas_call(
        round_kernel,
        out_shape=jax.ShapeDtypeStruct(a.shape, BF16),
        in_specs=[VMEM, VMEM] + [ANY] * len(arrived),
        out_specs=VMEM,
        compiler_params=LIMIT,
        name="round_grad",
    )(a, b, *arrived)


def weight_kernel(packs, starts, *refs):
    toks, grads = refs[:BLOCK], refs[BLOCK : 2 * BLOCK]
    keep_ref, send_ref = refs[2 * BLOCK :]
    width = keep_ref.shape[1]
    starts = [start * width for start in starts]
    core = lax.rem(lax.axis_index("dp"), CORES)
    for ref, which in ((send_ref, 1 - core), (keep_ref, core)):
        acc = None
        for k in range(BLOCK):
            first = pl.multiple_of(starts[k] + which * width, width)
            term = _mm(grads[k][...], toks[k][:, pl.ds(first, width)], NN)
            acc = term if acc is None else acc + term
        ref[...] = acc * (1.0 / packs)


def weight_part(toks, grads, packs, starts):
    part = jax.ShapeDtypeStruct((grads[0].shape[0], toks[-1].shape[1] // CORES), F32)
    return pl.pallas_call(
        functools.partial(weight_kernel, packs, starts),
        out_shape=[part, part],
        in_specs=[VMEM] * (2 * BLOCK),
        out_specs=[VMEM, VMEM],
        compiler_params=LIMIT,
        name="weight_part",
    )(*toks, *grads)


def fold_kernel(a_ref, b_ref, out_ref):
    out_ref[...] = a_ref[...] + b_ref[...]


def fold(a, b):
    return pl.pallas_call(
        fold_kernel,
        out_shape=jax.ShapeDtypeStruct(a.shape, F32),
        in_specs=[VMEM, VMEM],
        out_specs=VMEM,
        compiler_params=LIMIT,
        name="weight_fold",
    )(a, b)


def finish_kernel(a_ref, b_ref, out_ref):
    out_ref[...] = (a_ref[...] + b_ref[...]).T.astype(BF16)


def finish(a, b):
    return pl.pallas_call(
        finish_kernel,
        out_shape=jax.ShapeDtypeStruct((a.shape[1], a.shape[0]), BF16),
        in_specs=[VMEM] * 2,
        out_specs=VMEM,
        compiler_params=LIMIT,
        name="weight_finish",
    )(a, b)


def stack_kernel(count, *refs):
    out_ref = refs[-1]
    first = 0
    for ref in refs[:count]:
        out_ref[first : first + ref.shape[0], :] = ref[...]
        first += ref.shape[0]


def stack(parts, after=()):
    rows = sum(part.shape[0] for part in parts)
    return pl.pallas_call(
        functools.partial(stack_kernel, len(parts)),
        out_shape=jax.ShapeDtypeStruct((rows, parts[0].shape[1]), BF16),
        in_specs=[VMEM] * len(parts) + [ANY] * len(after),
        out_specs=VMEM,
        compiler_params=LIMIT,
        name="stack",
    )(*parts, *after)


def assemble_kernel(held, rows, *refs):
    arrays, out_ref, sems = refs[: len(held)], refs[-2], refs[-1]
    me = lax.axis_index("dp")
    copies = []
    for array, bits in zip(arrays, held):
        for n, bit in enumerate(bits):
            source = me ^ bit
            high = source // (CORES * BLOCK)
            place = (block_of(source) * CORES + lax.rem(source, CORES)) * 2 + high
            first = pl.multiple_of(place * rows, rows)
            copy = pltpu.make_async_copy(
                array.at[pl.ds(n * rows, rows), :],
                out_ref.at[pl.ds(first, rows), :],
                sems.at[len(copies)],
            )
            copy.start()
            copies.append(copy)
    for copy in copies:
        copy.wait()


def assemble(pieces, total, begun=None):
    arrays = [array for array, _ in pieces]
    held = [bits for _, bits in pieces]
    rows = arrays[0].shape[0] // len(held[0])
    count = len(arrays)
    if begun is not None:
        arrays.append(begun)
    return pl.pallas_call(
        functools.partial(assemble_kernel, held, rows),
        out_shape=jax.ShapeDtypeStruct((total * rows, arrays[0].shape[1]), BF16),
        in_specs=[ANY] * len(arrays),
        out_specs=ANY,
        scratch_shapes=[pltpu.SemaphoreType.DMA((sum(len(bits) for bits in held),))],
        input_output_aliases={} if begun is None else {count: 0},
        compiler_params=LIMIT,
        name="weight_assemble" if begun is None else "weight_complete",
    )(*arrays)


def hop(value, bits):
    count = lax.axis_size("dp")
    return lax.ppermute(value, "dp", [(i, i ^ bits) for i in range(count)])


def per_device_16x2(tokens, queries, grad_out, w_kv, doc_ids, span_order):
    dp_size = lax.axis_size("dp")
    rows_dev = queries.shape[1]
    swap = [(0, 1), (1, 0)]
    near = (Y, Z1, Y | Z1)
    flat = tokens[0]
    both = (True, False)
    own, tok_y, tok_z, far_d = slice_tokens(
        flat, [(0, both), (1, both), (2, both), (3, (True,))], "slice_first"
    )
    tok_y, tok_z, far_d = hop(tok_y, Y), hop(tok_z, Z1), hop(far_d, Y | Z1)
    keys, values = project(flat, w_kv)
    keys_in, values_in = lax.ppermute(keys, "seq", swap), lax.ppermute(values, "seq", swap)
    docs = doc_ids.reshape(-1, rows_dev)
    attention, query_grad, terms, done = attend(
        span_order, docs, queries[0], grad_out[0], [keys, keys_in, values, values_in], [tok_y, tok_z]
    )
    grad = round_grad(terms, lax.ppermute(terms, "seq", swap), [done])
    grads = [grad] + [hop(grad, bits) for bits in near]
    keep, send = weight_part([own, tok_y, tok_z, far_d], grads, dp_size, [0, 0, 0, 0])
    part = fold(keep, hop(send, CORE))
    far = hop(part, Z2)
    (near_d,) = slice_tokens(flat, [(3, (False,))], "slice_near_diagonal")
    near_d = hop(near_d, Y | Z1)
    keep, send = weight_part([own, tok_y, tok_z, near_d], grads, dp_size, [2, 2, 2, 0])
    own = finish(fold(keep, far), hop(send, CORE))
    z1, y, d, z2 = hop(own, Z1), hop(own, Y), hop(own, Y | Z1), hop(own, Z2)
    z21, z2y, z2d = hop(z2, Z1), hop(z2, Y), hop(z2, Y | Z1)
    first = hop(stack([own, z1, y, d]), CORE)
    last = hop(stack([z2, z21, z2y, z2d]), CORE)
    pieces = [
        (own, [0]),
        (z1, [Z1]),
        (y, [Y]),
        (d, [Y | Z1]),
        (z2, [Z2]),
        (z21, [Z2 | Z1]),
        (z2y, [Z2 | Y]),
        (z2d, [Z2 | Y | Z1]),
    ]
    held = [[bit | CORE for _, bits in part for bit in bits] for part in (pieces[:4], pieces[4:])]
    weight_grad = assemble(pieces + [(first, held[0])], dp_size)
    weight_grad = assemble([(last, held[1])], dp_size, weight_grad)
    return (attention[None], query_grad[None], weight_grad)


def per_device(tokens, queries, grad_out, w_kv, doc_ids, span_order):
    dp_size = lax.axis_size("dp")
    rows_dev = queries.shape[1]
    flat = tokens[0]
    spread = lax.all_to_all(flat, "dp", split_axis=1, concat_axis=0, tiled=True)
    partial = jnp.dot(flat, w_kv, preferred_element_type=F32)
    own = lax.psum_scatter(partial, "seq", scatter_dimension=0, tiled=True).astype(BF16)
    kvs = [lax.all_gather(own, "seq", axis=0, tiled=True)]
    docs = doc_ids.reshape(-1, rows_dev)
    attention, query_grad, terms, done = attend(span_order, docs, queries[0], grad_out[0], kvs)
    grad_kv = lax.psum(terms.T, "seq").astype(BF16)
    all_grads = lax.all_gather(grad_kv, "dp", axis=0, tiled=True)
    piece = (_mm(spread, all_grads, TN) * (1.0 / dp_size)).astype(BF16)
    weight_grad = lax.all_gather(piece, "dp", axis=0, tiled=True)
    return (attention[None], query_grad[None], weight_grad)


def solution(mesh):
    small = mesh.shape["dp"] == 16 and mesh.shape["seq"] == 2
    return jax.shard_map(
        per_device_16x2 if small else per_device,
        mesh=mesh,
        in_specs=(
            P("dp", None, "seq"),
            P("dp", "seq", None),
            P("dp", "seq", None),
            P("seq", None),
            P("dp", None),
            P(),
        ),
        out_specs=(P("dp", "seq", None), P("dp", "seq", None), P("seq", None)),
        check_vma=False,
    )
```
